512 devices in a mesh: wide: 64 (over x, z, core), narrow: 8 (over y).
Axes of the slice: x: 4, y: 8, z: 8, core: 2. Of those that a mesh axis runs over, the one named last changes fastest.
Arguments:
- right_side: float32 [3, 1024, 128, 128], P(None, 'wide', 'narrow'), may hold values from -8 to 8
- occupancy: int32 [1024, 128, 128], P('wide', 'narrow'), may hold values from 0 to 1, as said below
- region: int32 [1024, 128, 128], P('wide', 'narrow'), may hold values from 0 to 3
- coarse_inverse: float32 [6144, 6144], P(('wide', 'narrow')), as said below
Outputs:
- solution_field: float32 [3, 1024, 128, 128], P(None, 'wide', 'narrow')
- residual: float32 [3, 1024, 128, 128], P(None, 'wide', 'narrow')
The draws below stay inside these ranges and needn't reach their ends.
Inputs may be any that keep to these rules, and one draw needn't show every extreme that they name: `occupancy`: each subdomain has its own bone fraction between 0.15 and 0.9. `coarse_inverse`: symmetric positive definite.
All inputs are finite; a program needn't handle non-finite values.
Results may differ from the reference program's by a relative error of at most 0.00021.
Values sent between devices are 32-bit elements; how exact they have to be, the bound alone decides.
No kernel may reach another device: no remote copies, remote signals or barrier semaphores. Data moves between devices by JAX's collectives and lax.ppermute only.
A program may use at most 64 MiB of HBM per device.

```python
import jax
import jax.numpy as jnp
from jax import lax

CX = 16
CY = 16
CZ = 128
NREG = 4
ITERS = 2
NX = 1024
NY = 128
NZ = 128
NCOARSE = 6144
N_WIDE = 64
N_NARROW = 8


def draw_occupancy(key, part):
    first, second = jax.random.split(key)
    wide_count = NX // CX
    narrow_count = NY // CY
    percent = jax.random.randint(first, (wide_count, narrow_count), 15, 91)
    level = jnp.repeat(jnp.repeat(percent, CX, axis=0), CY, axis=1)[:, :, None]
    bits = jax.random.randint(second, (NX, NY, NZ), 0, 100)
    return (bits < level).astype(jnp.int32)


def draw_coarse_inverse(key, part):
    first, second = jax.random.split(jax.random.fold_in(key, 7), 2)
    count = NCOARSE
    factor = jax.random.normal(first, (count, count), jnp.float32)
    gram = jnp.dot(factor, factor.T) / count
    gram = 0.5 * (gram + gram.T)
    diag = jax.random.uniform(second, (count,), jnp.float32, 0.5, 1.5)
    whole = gram + jnp.diag(diag)
    scale = 0.05 * jnp.sqrt(jnp.float32(NREG) / jnp.float32(CX * CY * CZ))
    return (whole * scale).astype(jnp.float32)


def with_ends(values, rng, low, top_value):
    dims = values.shape
    spot = [jax.random.randint(jax.random.fold_in(rng, axis), (), 0, dims[axis]) for axis in range(len(dims))]
    values = values.at[tuple(spot)].set(low)
    longest = dims.index(max(dims))
    spot[longest] = (spot[longest] + 1) % dims[longest]
    return values.at[tuple(spot)].set(top_value)


def level_of(stream_key, extent, shards, smallest, largest):
    factor_of = 1.0
    for dim, parts in shards:
        steps = jax.random.uniform(jax.random.fold_in(jax.random.fold_in(stream_key, 6), dim), (parts,), jnp.float32, smallest / len(shards), largest / len(shards))
        factor_of = factor_of * jnp.repeat(jnp.exp(steps), extent[dim] // parts).reshape((-1,) + (1,) * (len(extent) - 1 - dim))
    return factor_of


def centred(rng, shape, width, most, pieces=(), dtype=jnp.bfloat16):
    values = jax.random.normal(rng, shape, jnp.float32) * width
    if len(pieces) > 0:
        values = level_of(rng, shape, pieces, -0.22, 0.18) * values
    return jnp.clip(values, min=-most, max=most).astype(dtype)


def setup_inputs(seed: int = 0) -> dict:
    key_of = jax.random.split(jax.random.key(seed), 5)
    return {
        "right_side": centred(key_of[0], (3, NX, NY, NZ), 1.0, 8.0, ((1, 64), (2, 8)), jnp.float32),
        "occupancy": draw_occupancy(jax.random.fold_in(key_of[4], 71), 0),
        "region": with_ends(jax.random.randint(key_of[2], (NX, NY, NZ), 0, NREG), jax.random.fold_in(key_of[2], 1), 0, NREG - 1).astype(jnp.int32),
        "coarse_inverse": draw_coarse_inverse(jax.random.fold_in(key_of[4], 71), 0),
    }


bone_stiff = 1.0
soft_stiff = 0.1


def neighbours(padded):
    return [padded[..., 2:, 1:-1, 1:-1], padded[..., :-2, 1:-1, 1:-1],
            padded[..., 1:-1, 2:, 1:-1], padded[..., 1:-1, :-2, 1:-1],
            padded[..., 1:-1, 1:-1, 2:], padded[..., 1:-1, 1:-1, :-2]]


def reference(right_side, occupancy, region, coarse_inverse):
    stiff = soft_stiff + (bone_stiff - soft_stiff) * occupancy.astype(jnp.float32)
    faces = [0.5 * (stiff + other) for other in neighbours(jnp.pad(stiff, 1))]
    diagonal = sum(faces) + 0.5 * stiff
    wide_count = N_WIDE
    narrow_count = N_NARROW

    def operate(field):
        padded = jnp.pad(field, ((0, 0), (1, 1), (1, 1), (1, 1)))
        result = 0.25 * stiff * (field + jnp.sum(field, axis=0, keepdims=True))
        for face, other in zip(faces, neighbours(padded)):
            result = result + face * (field - other)
        return result

    selects = [(region == g).astype(jnp.float32).reshape(wide_count, CX, narrow_count, CY, CZ) for g in range(NREG)]

    def precondition(resid):
        blocks = resid.reshape(3, wide_count, CX, narrow_count, CY, CZ)
        coarse = jnp.stack([jnp.einsum('cwxnyz,wxnyz->wnc', blocks, s, precision=lax.Precision.HIGHEST) for s in selects], axis=2).reshape(-1)
        answer = jnp.dot(coarse_inverse, coarse, precision=lax.Precision.HIGHEST).reshape(wide_count, narrow_count, NREG, 3)
        spread = jnp.zeros_like(blocks)
        for g in range(NREG):
            spread = spread + jnp.einsum('wxnyz,wnc->cwxnyz', selects[g], answer[:, :, g, :], precision=lax.Precision.HIGHEST)
        return resid / diagonal + spread.reshape(resid.shape)

    solution = jnp.zeros_like(right_side)
    resid = right_side
    precond = precondition(resid)
    direction = precond
    rz_now = jnp.sum(resid * precond)
    for step in range(ITERS):
        image = operate(direction)
        alpha = rz_now / jnp.sum(direction * image)
        solution = solution + alpha * direction
        resid = resid - alpha * image
        precond = precondition(resid)
        rz_next = jnp.sum(resid * precond)
        direction = precond + (rz_next / rz_now) * direction
        rz_now = rz_next
    return solution, resid
```

```python
import jax
import jax.numpy as jnp
from jax import lax
from jax.experimental import pallas as pl
from jax.experimental.pallas import tpu as pltpu
from jax.sharding import Mesh
from jax.sharding import PartitionSpec as P

WIDE = ("x", "z", "c")
ROWS = ("x", "z")
COLS = ("c", "y")
NROWS = 32
NCOLS = 16
F32 = jnp.float32
NREG = 4
SLAB = 96
VMEM = pl.BlockSpec(memory_space=pltpu.VMEM)


def shape(*dims):
    return jax.ShapeDtypeStruct(dims, F32)


def call(kernel, outs, ins, scratch=()):
    return pl.pallas_call(
        kernel,
        out_shape=outs,
        in_specs=[VMEM] * len(ins),
        out_specs=jax.tree.map(lambda _: VMEM, outs),
        scratch_shapes=list(scratch),
        compiler_params=pltpu.CompilerParams(vmem_limit_bytes=24 * 1024 * 1024),
    )(*ins)


def stiffness(occ):
    return 0.1 + 0.9 * occ.astype(F32)


def total(v):
    return jnp.sum(jnp.sum(v, axis=0, keepdims=True), axis=1, keepdims=True)


def add_regions(accs, label, field):
    out = list(accs)
    for g in range(NREG):
        mask = label == g + 1
        for c in range(3):
            out[3 * g + c] = out[3 * g + c] + jnp.where(mask, field[c], 0.0)
    return out


def fold(accs, coarse_ref, acc_ref, u_ref, pad_ref, out_ref, sums=()):
    for i in range(3 * NREG):
        acc_ref[i] = accs[i]
    rc = jnp.sum(jnp.sum(acc_ref[...], axis=1), axis=1, keepdims=True)
    u_ref[...] = jnp.sum(coarse_ref[...] * rc, axis=0, keepdims=True)
    pad_ref[...] = jnp.zeros_like(pad_ref)
    for w in range(2 * NROWS):
        pad_ref[w + 1 : w + 2, 0:SLAB] = u_ref[0:1, SLAB * w : SLAB * (w + 1)]
    if sums:
        lane = lax.broadcasted_iota(jnp.int32, (1, 128), 1)
        row = jnp.zeros((1, 128), F32)
        for i, s in enumerate(sums):
            row = jnp.where(lane == SLAB + i, s, row)
        tail = jnp.broadcast_to(row, (4, 128))
    for n in range(NROWS):
        window = pad_ref[2 * n : 2 * n + 4, :]
        if sums:
            window = window + tail
        out_ref[n] = window


FOLD_SCRATCH = (
    pltpu.VMEM((12, 16, 128), F32),
    pltpu.VMEM((1, 6144), F32),
    pltpu.VMEM((72, 128), F32),
)


def first_kernel(r_ref, occ_ref, reg_ref, coarse_ref, out_ref, lo_ref, hi_ref, acc_ref, u_ref, pad_ref):
    def step(x, accs):
        label = reg_ref[x] + 1
        return tuple(add_regions(accs, label, [r_ref[c, x] for c in range(3)]))

    zero = jnp.zeros((16, 128), F32)
    accs = lax.fori_loop(0, 16, step, (zero,) * 12)
    fold(accs, coarse_ref, acc_ref, u_ref, pad_ref, out_ref)
    for ref, at in ((lo_ref, 0), (hi_ref, 12)):
        ref[0] = stiffness(occ_ref[:, at : at + 4, :])
        ref[1] = reg_ref[:, at : at + 4, :].astype(F32) + 1.0
        for c in range(3):
            ref[2 + c] = r_ref[c, :, at : at + 4, :]


def hand_out(part, out_ref):
    for c in range(2):
        rows = part[c : c + 3]
        for y in range(8):
            out_ref[8 * c + y, 0:3, :] = pltpu.roll(rows, (12 - 12 * y) % 128, axis=1)
            out_ref[8 * c + y, 3:4, :] = part[0:1]


def around_kernel(recv_ref, r_ref, occ_ref, reg_ref, lo_ref, hi_ref, out_ref, up_ref, down_ref):
    hand_out(jnp.sum(recv_ref[...], axis=0), out_ref)
    for ref, at in ((up_ref, 13), (down_ref, 0)):
        rows = slice(at, at + 3)
        ref[0, :, 0:16, :] = stiffness(occ_ref[rows])
        ref[1, :, 0:16, :] = reg_ref[rows].astype(F32) + 1.0
        for c in range(3):
            ref[2 + c, :, 0:16, :] = r_ref[c, rows]
        for i in range(5):
            ref[i, :, 16:20, :] = hi_ref[i, rows]
            ref[i, :, 20:24, :] = lo_ref[i, rows]


def pass_kernel(recv_ref, out_ref):
    hand_out(jnp.sum(recv_ref[...], axis=0), out_ref)


def iotas():
    lane = lax.broadcasted_iota(jnp.int32, (24, 128), 1)
    return lane == 0, lane == 127


def coefficients(before, here, after):
    first, last = iotas()
    y_up = pltpu.roll(here, 23, axis=0)
    y_down = pltpu.roll(here, 1, axis=0)
    z_up = jnp.where(last, 0.0, pltpu.roll(here, 127, axis=1))
    z_down = jnp.where(first, 0.0, pltpu.roll(here, 1, axis=1))
    half = 0.5 * here
    faces = [half + 0.5 * other for other in (after, before, y_up, y_down, z_up, z_down)]
    diagonal = faces[0] + faces[1] + faces[2] + faces[3] + faces[4] + faces[5] + half
    faces[4] = jnp.where(last, 0.0, faces[4])
    faces[5] = jnp.where(first, 0.0, faces[5])
    return faces, diagonal


def operate(faces, diagonal, here, befores, fields, afters):
    quarter = 0.25 * here
    main = diagonal - quarter
    shared = quarter * (fields[0] + fields[1] + fields[2])
    out = []
    for c in range(3):
        u = fields[c]
        out.append(
            main * u
            + shared
            - faces[0] * afters[c]
            - faces[1] * befores[c]
            - faces[2] * pltpu.roll(u, 23, axis=0)
            - faces[3] * pltpu.roll(u, 1, axis=0)
            - faces[4] * pltpu.roll(u, 127, axis=1)
            - faces[5] * pltpu.roll(u, 1, axis=1)
        )
    return out


def spread_maps(q, map_ref):
    row = lax.broadcasted_iota(jnp.int32, (24, 128), 0)
    for s in range(3):
        for i in range(12):
            below, own, above = (q[s : s + 1, 12 * d + i : 12 * d + i + 1] for d in range(3))
            map_ref[s, i] = jnp.where(row < 16, own, jnp.where(row < 20, above, below))


def spread(label, map_ref, s, c):
    out = jnp.zeros((24, 128), F32)
    for g in range(NREG):
        out = jnp.where(label == g + 1, map_ref[s, 3 * g + c], out)
    return out


def second_kernel(
    recv_ref, r_ref, occ_ref, reg_ref, lo_ref, hi_ref, below_ref, above_ref, coarse_ref,
    out_ref, k_ref, label_ref, inv_ref, z_ref, w_ref,
    ext_ref, map_ref, acc_ref, u_ref, pad_ref,
):
    q = jnp.sum(recv_ref[...], axis=0)
    spread_maps(q, map_ref)
    k_ref[0:3] = below_ref[0]
    k_ref[19:22] = above_ref[0]
    label_ref[0:3] = below_ref[1]
    label_ref[19:22] = above_ref[1]
    k_ref[3:19, 0:16] = stiffness(occ_ref[...])
    label_ref[3:19, 0:16] = reg_ref[...].astype(F32) + 1.0
    for ref, i in ((k_ref, 0), (label_ref, 1)):
        ref[3:19, 16:20] = hi_ref[i]
        ref[3:19, 20:24] = lo_ref[i]
    for c in range(3):
        ext_ref[c, 0:3] = below_ref[2 + c]
        ext_ref[c, 19:22] = above_ref[2 + c]
        ext_ref[c, 3:19, 0:16] = r_ref[c]
        ext_ref[c, 3:19, 16:20] = hi_ref[2 + c]
        ext_ref[c, 3:19, 20:24] = lo_ref[2 + c]

    def first_step(s):
        def body(x, carry):
            here = k_ref[x]
            _, diagonal = coefficients(k_ref[x - 1], here, k_ref[x + 1])
            inv = jnp.where(here > 0.0, 1.0 / jnp.where(here > 0.0, diagonal, 1.0), 0.0)
            inv_ref[x] = inv
            label = label_ref[x]
            for c in range(3):
                z_ref[c, x] = ext_ref[c, x] * inv + spread(label, map_ref, s, c)
            return carry

        return body

    lax.fori_loop(1, 3, first_step(0), 0)
    lax.fori_loop(3, 19, first_step(1), 0)
    lax.fori_loop(19, 21, first_step(2), 0)

    def image(x):
        here = k_ref[x]
        faces, diagonal = coefficients(k_ref[x - 1], here, k_ref[x + 1])
        fields = [z_ref[c, x] for c in range(3)]
        w = operate(
            faces, diagonal, here, [z_ref[c, x - 1] for c in range(3)], fields, [z_ref[c, x + 1] for c in range(3)]
        )
        for c in range(3):
            w_ref[c, x] = w[c]
        return fields, w

    image(2)
    image(19)

    def second_step(x, carry):
        fields, w = image(x)
        own = [v[0:16] for v in w]
        rz, zw = carry[12], carry[13]
        for c in range(3):
            z = fields[c][0:16]
            rz = rz + ext_ref[c, x, 0:16] * z
            zw = zw + z * own[c]
        return (*add_regions(carry[:12], label_ref[x, 0:16], own), rz, zw)

    zero = jnp.zeros((16, 128), F32)
    carry = lax.fori_loop(3, 19, second_step, (zero,) * 14)
    fold(carry[:12], coarse_ref, acc_ref, u_ref, pad_ref, out_ref, (total(carry[12]), total(carry[13])))


def third_kernel(
    recv_ref, r_ref, k_ref, label_ref, inv_ref, z_ref, w_ref, out_ref, scal_ref, znew_ref, image_ref, map_ref
):
    q = jnp.sum(recv_ref[...], axis=0)
    spread_maps(q, map_ref)
    rz, zw = q[3:4, SLAB : SLAB + 1], q[3:4, SLAB + 1 : SLAB + 2]
    alpha = rz / zw

    def first_step(s):
        def body(x, carry):
            inv, label = inv_ref[x], label_ref[x]
            for c in range(3):
                y = w_ref[c, x] * inv + spread(label, map_ref, s, c)
                znew_ref[c, x - 2] = z_ref[c, x] - alpha * y
            return carry

        return body

    first_step(0)(2, 0)
    lax.fori_loop(3, 19, first_step(1), 0)
    first_step(2)(19, 0)

    def second_step(x, carry):
        here = k_ref[x + 2]
        faces, diagonal = coefficients(k_ref[x + 1], here, k_ref[x + 3])
        fields = [znew_ref[c, x] for c in range(3)]
        image = operate(
            faces, diagonal, here, [znew_ref[c, x - 1] for c in range(3)], fields, [znew_ref[c, x + 1] for c in range(3)]
        )
        new, zaz, cross = carry
        for c in range(3):
            z, az, w = fields[c][0:16], image[c][0:16], w_ref[c, x + 2, 0:16]
            image_ref[c, x - 1] = az
            new = new + (r_ref[c, x - 1] - alpha * w) * z
            zaz = zaz + z * az
            cross = cross + z * w
        return new, zaz, cross

    zero = jnp.zeros((16, 128), F32)
    sums = lax.fori_loop(1, 17, second_step, (zero,) * 3)
    lane = lax.broadcasted_iota(jnp.int32, (1, 128), 1)
    row = jnp.zeros((1, 128), F32)
    for i, s in enumerate(sums):
        row = jnp.where(lane == i, total(s), row)
    scal_ref[...] = q[3:4]
    for n in range(NCOLS):
        out_ref[n] = row


def sum_kernel(recv_ref, out_ref):
    row = jnp.sum(recv_ref[...], axis=0)
    for n in range(NROWS):
        out_ref[n] = row


def last_kernel(recv_ref, scal_ref, r_ref, z_ref, w_ref, znew_ref, image_ref, x_ref, res_ref):
    sums = jnp.sum(recv_ref[...], axis=0)
    new, zaz, cross = (sums[:, i : i + 1] for i in range(3))
    scal = scal_ref[...]
    rz, zw = scal[:, SLAB : SLAB + 1], scal[:, SLAB + 1 : SLAB + 2]
    alpha = rz / zw
    ratio = new / rz
    product = zaz + ratio * (2.0 * cross + ratio * zw)
    second = new / product

    def step(x, carry):
        for c in range(3):
            z, w = z_ref[c, x + 3, 0:16], w_ref[c, x + 3, 0:16]
            x_ref[c, x] = alpha * z + second * (znew_ref[c, x + 1, 0:16] + ratio * z)
            res_ref[c, x] = (r_ref[c, x] - alpha * w) - second * (image_ref[c, x] + ratio * w)
        return carry

    lax.fori_loop(0, 16, step, 0)


def exchange(array, axes):
    return lax.all_to_all(array, axes, 0, 0, tiled=True)


def shifted(array, axis, step):
    count = lax.axis_size(axis)
    pairs = [(i, i + step) for i in range(count) if 0 <= i + step < count]
    return lax.ppermute(array, axis, pairs)


def local(right, occ, reg, coarse):
    send, lo, hi = call(
        first_kernel,
        (shape(NROWS, 4, 128), shape(5, 16, 4, 128), shape(5, 16, 4, 128)),
        (right, occ, reg, coarse),
        FOLD_SCRATCH,
    )
    before = shifted(hi, "y", 1)
    after = shifted(lo, "y", -1)
    got = exchange(send, ROWS)
    send, up, down = call(
        around_kernel,
        (shape(NCOLS, 4, 128), shape(5, 3, 24, 128), shape(5, 3, 24, 128)),
        (got, right, occ, reg, before, after),
    )
    below = shifted(up, WIDE, 1)
    above = shifted(down, WIDE, -1)
    got = exchange(send, COLS)
    plane = (24, 128)
    send, k, label, inv, z, w = call(
        second_kernel,
        (
            shape(NROWS, 4, 128),
            shape(22, *plane),
            shape(22, *plane),
            shape(22, *plane),
            shape(3, 22, *plane),
            shape(3, 22, *plane),
        ),
        (got, right, occ, reg, before, after, below, above, coarse),
        (pltpu.VMEM((3, 22, *plane), F32), pltpu.VMEM((3, 12, *plane), F32), *FOLD_SCRATCH),
    )
    got = exchange(send, ROWS)
    send = call(pass_kernel, shape(NCOLS, 4, 128), (got,))
    got = exchange(send, COLS)
    send, scal, znew, image = call(
        third_kernel,
        (shape(NCOLS, 1, 128), shape(1, 128), shape(3, 18, *plane), shape(3, 16, 16, 128)),
        (got, right, k, label, inv, z, w),
        (pltpu.VMEM((3, 12, *plane), F32),),
    )
    got = exchange(send, COLS)
    send = call(sum_kernel, shape(NROWS, 1, 128), (got,))
    got = exchange(send, ROWS)
    return call(
        last_kernel,
        (shape(3, 16, 16, 128), shape(3, 16, 16, 128)),
        (got, scal, right, z, w, znew, image),
    )


def solution(mesh):
    finer = Mesh(mesh.devices.reshape(4, 8, 2, 8), ("x", "z", "c", "y"))
    field = P(None, WIDE, "y", None)
    labels = P(WIDE, "y", None)
    return jax.shard_map(
        local,
        mesh=finer,
        in_specs=(field, labels, labels, P((*WIDE, "y"), None)),
        out_specs=(field, field),
        check_vma=False,
    )
```

```python
import jax
import jax.numpy as jnp
import numpy as np
from jax import lax
from jax.experimental import pallas as pl
from jax.experimental.pallas import tpu as pltpu
from jax.sharding import Mesh
from jax.sharding import PartitionSpec as P

WIDE = ("x", "z", "c")
ROWS = ("x", "z")
COLS = ("c", "y")
NROWS = 32
NCOLS = 16
F32 = jnp.float32
NREG = 4
SLAB = 96
VMEM = pl.BlockSpec(memory_space=pltpu.VMEM)


def shape(*dims):
    return jax.ShapeDtypeStruct(dims, F32)


def call(kernel, outs, ins, scratch=(), space=VMEM, cost=0, limit=24):
    return pl.pallas_call(
        kernel,
        out_shape=outs,
        in_specs=[space] * len(ins),
        out_specs=jax.tree.map(lambda _: VMEM, outs),
        scratch_shapes=list(scratch),
        cost_estimate=pl.CostEstimate(flops=cost, bytes_accessed=cost, transcendentals=0) if cost else None,
        compiler_params=pltpu.CompilerParams(vmem_limit_bytes=int(limit * 1024 * 1024)),
    )(*ins)


def total(v):
    return jnp.sum(jnp.sum(v, axis=0, keepdims=True), axis=1, keepdims=True)


def add_regions(accs, label, field):
    out = list(accs)
    for g in range(NREG):
        mask = label == g + 1
        for c in range(3):
            out[3 * g + c] = out[3 * g + c] + jnp.where(mask, field[c], 0.0)
    return out


def in_lanes(acc_ref, at):
    sums = jnp.sum(jnp.sum(acc_ref[...], axis=1), axis=1, keepdims=True)
    row = lax.broadcasted_iota(jnp.int32, (12, 128), 0)
    lane = lax.broadcasted_iota(jnp.int32, (12, 128), 1)
    return jnp.sum(jnp.where(lane == row + at, sums, 0.0), axis=0, keepdims=True)


def fold(accs, coarse_ref, acc_ref, u_ref, pad_ref, out_ref, sums=()):
    for i in range(3 * NREG):
        acc_ref[i] = accs[i]
    rc = jnp.sum(jnp.sum(acc_ref[...], axis=1), axis=1, keepdims=True)
    u_ref[...] = jnp.sum(coarse_ref[...] * rc, axis=0, keepdims=True)
    pad_ref[...] = jnp.zeros_like(pad_ref)
    for w in range(2 * NROWS):
        pad_ref[w + 1 : w + 2, 0:SLAB] = u_ref[0:1, SLAB * w : SLAB * (w + 1)]
    if sums:
        lane = lax.broadcasted_iota(jnp.int32, (1, 128), 1)
        row = jnp.zeros((1, 128), F32)
        for i, s in enumerate(sums):
            row = jnp.where(lane == SLAB + i, s, row)
        tail = jnp.broadcast_to(row, (4, 128))
    for n in range(NROWS):
        window = pad_ref[2 * n : 2 * n + 4, :]
        if sums:
            window = window + tail
        out_ref[n] = window


FOLD_SCRATCH = (
    pltpu.VMEM((12, 16, 128), F32),
    pltpu.VMEM((1, 6144), F32),
    pltpu.VMEM((72, 128), F32),
)


def first_kernel(
    r_hbm, occ_hbm, reg_hbm, coarse_hbm,
    out_ref, lo_ref, hi_ref, r_ref, k_ref, label_ref, coarse_ref,
    occ_ref, reg_ref, acc_ref, u_ref, pad_ref, sems,
):
    pairs = ((r_hbm, r_ref), (reg_hbm, reg_ref), (occ_hbm, occ_ref), (coarse_hbm, coarse_ref))
    copies = [pltpu.make_async_copy(a, b, sems.at[i]) for i, (a, b) in enumerate(pairs)]
    for copy in copies:
        copy.start()
    for copy in copies[:3]:
        copy.wait()
    k_ref[...] = 0.1 + 0.9 * occ_ref[...].astype(F32)
    label_ref[...] = reg_ref[...].astype(F32) + 1.0
    for ref, deep, flat in ((lo_ref, 0, 0), (hi_ref, 12, 14)):
        ref[0] = k_ref[:, deep : deep + 4, :]
        ref[1, :, 0:2] = label_ref[:, flat : flat + 2, :]
        ref[1, :, 2:4] = r_ref[0, :, flat : flat + 2, :]
        ref[2, :, 0:2] = r_ref[1, :, flat : flat + 2, :]
        ref[2, :, 2:4] = r_ref[2, :, flat : flat + 2, :]

    def step(x, accs):
        return tuple(add_regions(accs, label_ref[x], [r_ref[c, x] for c in range(3)]))

    zero = jnp.zeros((16, 128), F32)
    accs = lax.fori_loop(0, 16, step, (zero,) * 12, unroll=2)
    copies[3].wait()
    fold(accs, coarse_ref, acc_ref, u_ref, pad_ref, out_ref)


def hand_out(part, out_ref):
    for c in range(2):
        rows = part[c : c + 3]
        for y in range(8):
            out_ref[8 * c + y, 0:3, :] = pltpu.roll(rows, (12 - 12 * y) % 128, axis=1)
            out_ref[8 * c + y, 3:4, :] = part[0:1]


def tail_rows(lo_ref, hi_ref, i, planes):
    if i == 0:
        return jnp.concatenate([hi_ref[0, planes], lo_ref[0, planes]], axis=1)
    block, at = 1 + (i - 1) // 2, 2 * ((i - 1) % 2)
    above, below = hi_ref[block, planes, at : at + 2], lo_ref[block, planes, at : at + 2]
    none = jnp.zeros((above.shape[0], 4, 128), F32)
    return jnp.concatenate([above, none, below], axis=1)


PACK = 72 + 4 * 40


def pack_kernel(k_ref, label_ref, r_ref, lo_ref, hi_ref, up_ref, down_ref):
    fields = [label_ref] + [r_ref.at[c] for c in range(3)]
    for ref, deep, near, next_ in ((up_ref, 13, 15, 14), (down_ref, 0, 0, 1)):
        tails = tail_rows(lo_ref, hi_ref, 0, pl.ds(deep, 3))
        for i in range(3):
            ref[24 * i : 24 * i + 16] = k_ref[deep + i]
            ref[24 * i + 16 : 24 * i + 24] = tails[i]
        for i, field in enumerate(fields):
            at = 72 + 40 * i
            ref[at : at + 16] = field[near]
            ref[at + 16 : at + 24] = tail_rows(lo_ref, hi_ref, 1 + i, pl.ds(near, 1))[0]
            ref[at + 24 : at + 40] = field[next_]


def extend_kernel(
    r_ref, k_own_ref, label_own_ref, lo_ref, hi_ref, below_ref, above_ref, k_ref, label_ref, inv_ref, f_ref
):
    whole = pl.ds(0, 16)
    k_ref[3:19, 0:16] = k_own_ref[...]
    label_ref[3:19, 0:16] = label_own_ref[...]
    k_ref[3:19, 16:24] = tail_rows(lo_ref, hi_ref, 0, whole)
    label_ref[3:19, 16:24] = tail_rows(lo_ref, hi_ref, 1, whole)
    none = jnp.zeros((8, 128), F32)
    for i in range(3):
        k_ref[i] = below_ref[24 * i : 24 * i + 24]
        k_ref[19 + i] = above_ref[24 * i : 24 * i + 24]
    targets = [label_ref] + [f_ref.at[c] for c in range(3)]
    for i, ref in enumerate(targets):
        at = 72 + 40 * i
        for pack, near, next_ in ((below_ref, 2, 1), (above_ref, 19, 20)):
            ref[near] = pack[at : at + 24]
            ref[next_, 0:16] = pack[at + 24 : at + 40]
            ref[next_, 16:24] = none
    for c in range(3):
        f_ref[c, 3:19, 0:16] = r_ref[c]
        f_ref[c, 3:19, 16:24] = tail_rows(lo_ref, hi_ref, 2 + c, whole)

    def step(x, carry):
        here = k_ref[x]
        _, diagonal = coefficients(k_ref[x - 1], here, k_ref[x + 1])
        inside = here > 0.0
        inv = jnp.where(inside, 1.0 / jnp.where(inside, diagonal, 1.0), 0.0)
        inv_ref[x] = inv
        for c in range(3):
            f_ref[c, x] = f_ref[c, x] * inv
        return carry

    lax.fori_loop(1, 21, step, 0, unroll=2)


def around_kernel(recv_ref, out_ref):
    hand_out(jnp.sum(recv_ref[...], axis=0), out_ref)


def pass_kernel(recv_ref, own_ref, pair_ref, out_ref):
    part = jnp.sum(recv_ref[...], axis=0)
    rows = jnp.concatenate([part, own_ref[...], pair_ref[...]], axis=0)
    for n in range(NCOLS):
        out_ref[n] = rows


def iotas():
    lane = lax.broadcasted_iota(jnp.int32, (24, 128), 1)
    return lane == 0, lane == 127


def coefficients(before, here, after):
    first, last = iotas()
    y_up = pltpu.roll(here, 23, axis=0)
    y_down = pltpu.roll(here, 1, axis=0)
    z_up = jnp.where(last, 0.0, pltpu.roll(here, 127, axis=1))
    z_down = jnp.where(first, 0.0, pltpu.roll(here, 1, axis=1))
    half = 0.5 * here
    faces = [half + 0.5 * other for other in (after, before, y_up, y_down, z_up, z_down)]
    diagonal = faces[0] + faces[1] + faces[2] + faces[3] + faces[4] + faces[5] + half
    faces[4] = jnp.where(last, 0.0, faces[4])
    faces[5] = jnp.where(first, 0.0, faces[5])
    return faces, diagonal


def operate(faces, diagonal, here, befores, fields, afters):
    quarter = 0.25 * here
    main = diagonal - quarter
    shared = quarter * (fields[0] + fields[1] + fields[2])
    out = []
    for c in range(3):
        u = fields[c]
        out.append(
            main * u
            + shared
            - faces[0] * afters[c]
            - faces[1] * befores[c]
            - faces[2] * pltpu.roll(u, 23, axis=0)
            - faces[3] * pltpu.roll(u, 1, axis=0)
            - faces[4] * pltpu.roll(u, 127, axis=1)
            - faces[5] * pltpu.roll(u, 1, axis=1)
        )
    return out


def spread_maps(q, map_ref):
    row = lax.broadcasted_iota(jnp.int32, (24, 128), 0)
    for s in range(3):
        for i in range(12):
            below, own, above = (q[s : s + 1, 12 * d + i : 12 * d + i + 1] for d in range(3))
            map_ref[s, i] = jnp.where(row < 16, own, jnp.where(row < 20, above, below))


def spread(label, map_ref, s, c):
    out = jnp.zeros((24, 128), F32)
    for g in range(NREG):
        out = jnp.where(label == g + 1, map_ref[s, 3 * g + c], out)
    return out


def second_kernel(
    recv_ref, r_ref, k_ref, label_ref, f_ref, coarse_ref,
    out_ref, z_ref, w_ref, own_ref,
    map_ref, acc_ref, u_ref, pad_ref,
):
    q = jnp.sum(recv_ref[...], axis=0)
    spread_maps(q, map_ref)

    def first_step(s):
        def body(x, carry):
            label = label_ref[x]
            for c in range(3):
                z_ref[c, x] = f_ref[c, x] + spread(label, map_ref, s, c)
            return carry

        return body

    lax.fori_loop(1, 3, first_step(0), 0)
    lax.fori_loop(3, 19, first_step(1), 0, unroll=2)
    lax.fori_loop(19, 21, first_step(2), 0)

    def image(x):
        here = k_ref[x]
        faces, diagonal = coefficients(k_ref[x - 1], here, k_ref[x + 1])
        fields = [z_ref[c, x] for c in range(3)]
        w = operate(
            faces, diagonal, here, [z_ref[c, x - 1] for c in range(3)], fields, [z_ref[c, x + 1] for c in range(3)]
        )
        for c in range(3):
            w_ref[c, x] = w[c]
        return fields, w

    image(2)
    image(19)

    def second_step(x, carry):
        fields, w = image(x)
        own = [v[0:16] for v in w]
        rz, zw = carry[12], carry[13]
        for c in range(3):
            z = fields[c][0:16]
            rz = rz + r_ref[c, x - 3] * z
            zw = zw + z * own[c]
        return (*add_regions(carry[:12], label_ref[x, 0:16], own), rz, zw)

    zero = jnp.zeros((16, 128), F32)
    carry = lax.fori_loop(3, 19, second_step, (zero,) * 14)
    fold(carry[:12], coarse_ref, acc_ref, u_ref, pad_ref, out_ref, (total(carry[12]), total(carry[13])))
    own_ref[...] = in_lanes(acc_ref, 12)


def selection():
    out = np.zeros((88, 3 * 128), np.float32)
    for n in range(5):
        for d in range(4):
            for h in range(4):
                g = (h + d) % 4
                for c in range(3):
                    lane = 128 * (n // 2) + 48 * (n % 2) + 12 * d + 3 * h + c
                    out[16 * n + 4 * g + h, lane] -= 1.0
                    if n == 0:
                        out[4 * h + g, lane] -= 1.0
                        if d == 0:
                            out[80 + g, lane] += 1.0
                            out[84 + g, lane] += 1.0
    for g in range(4):
        out[80 + g, 96 + 3 * g] = 1.0
    return out


def tiles(v):
    return v[0:8] + v[8:16]


def pair_kernel(k_ref, label_ref, select_ref, out_ref, acc_ref):
    row = lax.broadcasted_iota(jnp.int32, (24, 128), 0)
    lane = lax.broadcasted_iota(jnp.int32, (24, 128), 1)

    def plane(x, accs, inner):
        here, label = k_ref[x], label_ref[x]
        faces, diagonal = coefficients(k_ref[x - 1], here, k_ref[x + 1])
        y_label = jnp.where(row == 15, 0.0, pltpu.roll(label, 23, axis=0))[0:16]
        z_label = jnp.where(lane == 127, 0.0, pltpu.roll(label, 127, axis=1))[0:16]
        own = label[0:16]
        quarter, coupling = 0.25 * here[0:16], (diagonal - 0.5 * here)[0:16]
        masks = [own == g + 1 for g in range(NREG)]
        out = list(accs)
        for h in range(NREG):
            v = jnp.where(y_label == h + 1, faces[2][0:16], 0.0) + jnp.where(z_label == h + 1, faces[4][0:16], 0.0)
            if inner:
                v = v + jnp.where(label_ref[x + 1, 0:16] == h + 1, faces[0][0:16], 0.0)
            for g in range(NREG):
                out[4 * g + h] = out[4 * g + h] + tiles(jnp.where(masks[g], v, 0.0))
        for g in range(NREG):
            out[16 + g] = out[16 + g] + tiles(jnp.where(masks[g], quarter, 0.0))
            out[20 + g] = out[20 + g] + tiles(jnp.where(masks[g], coupling, 0.0))
        return tuple(out)

    zero = jnp.zeros((8, 128), F32)
    accs = lax.fori_loop(3, 18, lambda x, a: plane(x, a, True), (zero,) * 24)
    accs = plane(18, accs, False)
    for i in range(16):
        acc_ref[i] = accs[i]
    for i in range(8):
        acc_ref[80 + i] = accs[16 + i]
    own = pl.ds(3, 16)
    sides = (
        (k_ref[3, 0:16], label_ref[3, 0:16], k_ref[2, 0:16], label_ref[2, 0:16]),
        (k_ref[18, 0:16], label_ref[18, 0:16], k_ref[19, 0:16], label_ref[19, 0:16]),
        (k_ref[own, 0, :], label_ref[own, 0, :], k_ref[own, 23, :], label_ref[own, 23, :]),
        (k_ref[own, 15, :], label_ref[own, 15, :], k_ref[own, 16, :], label_ref[own, 16, :]),
    )
    for n, (k, label, other, other_label) in enumerate(sides):
        face = 0.5 * k + 0.5 * other
        for g in range(NREG):
            part = jnp.where(label == g + 1, face, 0.0)
            for h in range(NREG):
                acc_ref[16 * n + 16 + 4 * g + h] = tiles(jnp.where(other_label == h + 1, part, 0.0))
    sums = jnp.sum(jnp.sum(acc_ref[...], axis=1), axis=1, keepdims=True)
    for i in range(3):
        out_ref[i : i + 1] = jnp.sum(select_ref[:, 128 * i : 128 * i + 128] * sums, axis=0, keepdims=True)


def moment_kernel(k_ref, label_ref, inv_ref, w_ref, own_ref, out_ref, g_ref, acc_ref):
    def first_step(x, carry):
        inv = inv_ref[x]
        for c in range(3):
            g_ref[c, x - 2] = w_ref[c, x] * inv
        return carry

    lax.fori_loop(2, 20, first_step, 0, unroll=2)

    def step(x, carry):
        here = k_ref[x + 2]
        faces, diagonal = coefficients(k_ref[x + 1], here, k_ref[x + 3])
        fields = [g_ref[c, x] for c in range(3)]
        image = operate(
            faces, diagonal, here, [g_ref[c, x - 1] for c in range(3)], fields, [g_ref[c, x + 1] for c in range(3)]
        )
        own = [v[0:16] for v in image]
        wg, gg = carry[12], carry[13]
        for c in range(3):
            g = fields[c][0:16]
            wg = wg + w_ref[c, x + 2, 0:16] * g
            gg = gg + own[c] * g
        return (*add_regions(carry[:12], label_ref[x + 2, 0:16], own), wg, gg)

    zero = jnp.zeros((16, 128), F32)
    carry = lax.fori_loop(1, 17, step, (zero,) * 14)
    for i in range(12):
        acc_ref[i] = carry[i]
    lane = lax.broadcasted_iota(jnp.int32, (1, 128), 1)
    row = in_lanes(acc_ref, 0) + own_ref[...]
    out_ref[...] = jnp.where(lane == 24, total(carry[12]), jnp.where(lane == 25, total(carry[13]), row))


def group_kernel(recv_ref, out_ref):
    q = jnp.sum(recv_ref[:, 0:4, :], axis=0)
    own = recv_ref[:, 4, :]
    lane = lax.broadcasted_iota(jnp.int32, (16, 128), 1)
    shifted_rows = []
    for s in range(4):
        shifted_rows.append(
            jnp.concatenate([pltpu.roll(q[s : s + 1], (128 - 12 * y) % 128, axis=1) for y in range(8)], axis=0)
        )
    mine, below, above = (
        jnp.concatenate([shifted_rows[s], shifted_rows[s + 1]], axis=0) for s in (1, 0, 2)
    )

    def right(v, by):
        return pltpu.roll(v, by % 128, axis=1)

    def first(v):
        return jnp.where(lane < 12, v, 0.0)

    def four(v):
        v = first(v)
        v = v + right(v, 12)
        return v + right(v, 24)

    alone = first(mine)
    twice = alone + right(alone, 12)
    turned = alone
    for d in range(1, 4):
        turned = turned + right(first(right(twice, -3 * d)), 12 * d)
    turned = turned + right(turned, 48)
    three = mine + right(mine, -1) + right(mine, -2)
    products = (
        recv_ref[:, 5, :] * (turned * (four(mine) + right(four(below), 48)) + right(first(three * three), 96))
        + recv_ref[:, 6, :] * turned * (four(above) + right(four(right(mine, 12)), 48))
        + recv_ref[:, 7, :] * turned * four(right(mine, -12))
        + 2.0 * jnp.where(lane < 12, own * alone, 0.0)
        + jnp.where(lane == 25, own, 0.0)
    )
    pairing = jnp.where((lane >= 12) & (lane < 24), own * twice, jnp.where(lane == 24, own, 0.0))
    at = lax.broadcasted_iota(jnp.int32, (1, 128), 1)
    row = jnp.where(at == 0, total(pairing), jnp.where(at == 1, total(products), 0.0))
    for n in range(NROWS):
        out_ref[n] = row


def third_kernel(recv_ref, k_ref, label_ref, inv_ref, z_ref, w_ref, scal_ref, znew_ref, image_ref, map_ref):
    q = jnp.sum(recv_ref[:, 0:4, :], axis=0)
    near = jnp.where(lax.axis_index("c") == 0, q[0:3], q[1:4])
    spread_maps(pltpu.roll(near, lax.rem(140 - 12 * lax.axis_index("y"), 128), axis=1), map_ref)
    scal_ref[...] = q[0:1]
    rz, zw = q[0:1, SLAB : SLAB + 1], q[0:1, SLAB + 1 : SLAB + 2]
    alpha = rz / zw

    def first_step(s):
        def body(x, carry):
            inv, label = inv_ref[x], label_ref[x]
            for c in range(3):
                y = w_ref[c, x] * inv + spread(label, map_ref, s, c)
                znew_ref[c, x - 2] = z_ref[c, x] - alpha * y
            return carry

        return body

    first_step(0)(2, 0)
    lax.fori_loop(3, 19, first_step(1), 0, unroll=2)
    first_step(2)(19, 0)

    def second_step(x, carry):
        here = k_ref[x + 2]
        faces, diagonal = coefficients(k_ref[x + 1], here, k_ref[x + 3])
        fields = [znew_ref[c, x] for c in range(3)]
        image = operate(
            faces, diagonal, here, [znew_ref[c, x - 1] for c in range(3)], fields, [znew_ref[c, x + 1] for c in range(3)]
        )
        for c in range(3):
            image_ref[c, x - 1] = image[c][0:16]
        return carry

    lax.fori_loop(1, 17, second_step, 0)


def last_kernel(recv_ref, scal_ref, r_ref, z_ref, w_ref, znew_ref, image_ref, x_ref, res_ref):
    sums = jnp.sum(recv_ref[...], axis=0)
    wy, yay = sums[:, 0:1], sums[:, 1:2]
    scal = scal_ref[...]
    rz, zw = scal[:, SLAB : SLAB + 1], scal[:, SLAB + 1 : SLAB + 2]
    alpha = rz / zw
    new = rz + alpha * (alpha * wy - 2.0 * zw)
    zaz = zw + alpha * (alpha * yay - 2.0 * wy)
    cross = zw - alpha * wy
    ratio = new / rz
    second = new / (zaz + ratio * (2.0 * cross + ratio * zw))
    first = alpha + second * ratio

    def step(x, carry):
        for c in range(3):
            x_ref[c, x] = first * z_ref[c, x + 3, 0:16] + second * znew_ref[c, x + 1, 0:16]
            res_ref[c, x] = r_ref[c, x] - first * w_ref[c, x + 3, 0:16] - second * image_ref[c, x]
        return carry

    lax.fori_loop(0, 16, step, 0, unroll=2)


def exchange(array, axes):
    return lax.all_to_all(array, axes, 0, 0, tiled=True)


def shifted(array, axis, step):
    count = lax.axis_size(axis)
    pairs = [(i, i + step) for i in range(count) if 0 <= i + step < count]
    return lax.ppermute(array, axis, pairs)


def local(right, occ, reg, coarse):
    field, plane = (16, 16, 128), (24, 128)
    send, lo, hi, r, k_own, label_own, coarse = call(
        first_kernel,
        (
            shape(NROWS, 4, 128),
            shape(3, 16, 4, 128),
            shape(3, 16, 4, 128),
            shape(3, *field),
            shape(*field),
            shape(*field),
            shape(12, 6144),
        ),
        (right, occ, reg, coarse),
        (
            pltpu.VMEM(field, jnp.int32),
            pltpu.VMEM(field, jnp.int32),
            *FOLD_SCRATCH,
            pltpu.SemaphoreType.DMA((4,)),
        ),
        space=pl.BlockSpec(memory_space=pltpu.HBM),
        limit=53.5,
    )
    before = shifted(hi, "y", 1)
    after = shifted(lo, "y", -1)
    got = exchange(send, ROWS)
    up, down = call(
        pack_kernel, (shape(PACK, 128), shape(PACK, 128)), (k_own, label_own, r, before, after), cost=1000000
    )
    below = shifted(up, WIDE, 1)
    above = shifted(down, WIDE, -1)
    send = call(around_kernel, shape(NCOLS, 4, 128), (got,))
    got = exchange(send, COLS)
    k, label, inv, f = call(
        extend_kernel,
        (shape(22, *plane), shape(22, *plane), shape(22, *plane), shape(3, 22, *plane)),
        (r, k_own, label_own, before, after, below, above),
        cost=3000000,
    )
    pair = call(
        pair_kernel, shape(3, 128), (k, label, jnp.asarray(selection())), (pltpu.VMEM((88, 8, 128), F32),), cost=3000000
    )
    send, z, w, own = call(
        second_kernel,
        (shape(NROWS, 4, 128), shape(3, 22, *plane), shape(3, 22, *plane), shape(1, 128)),
        (got, r, k, label, f, coarse),
        (pltpu.VMEM((3, 12, *plane), F32), *FOLD_SCRATCH),
    )
    got = exchange(send, ROWS)
    own = call(
        moment_kernel,
        shape(1, 128),
        (k, label, inv, w, own),
        (pltpu.VMEM((3, 18, *plane), F32), pltpu.VMEM((12, 16, 128), F32)),
        cost=3000000,
    )
    send = call(pass_kernel, shape(NCOLS, 8, 128), (got, own, pair))
    got = exchange(send, COLS)
    send = call(group_kernel, shape(NROWS, 1, 128), (got,))
    scal, znew, image = call(
        third_kernel,
        (shape(1, 128), shape(3, 18, *plane), shape(3, *field)),
        (got, k, label, inv, z, w),
        (pltpu.VMEM((3, 12, *plane), F32),),
        cost=3000000,
    )
    got = exchange(send, ROWS)
    return call(
        last_kernel,
        (shape(3, *field), shape(3, *field)),
        (got, scal, r, z, w, znew, image),
    )


def solution(mesh):
    finer = Mesh(mesh.devices.reshape(4, 8, 2, 8), ("x", "z", "c", "y"))
    field = P(None, WIDE, "y", None)
    labels = P(WIDE, "y", None)
    return jax.shard_map(
        local,
        mesh=finer,
        in_specs=(field, labels, labels, P((*WIDE, "y"), None)),
        out_specs=(field, field),
        check_vma=False,
    )
```

```python
import jax
import jax.numpy as jnp
import numpy as np
from jax import lax
from jax.experimental import pallas as pl
from jax.experimental.pallas import tpu as pltpu
from jax.sharding import Mesh
from jax.sharding import PartitionSpec as P

WIDE = ("x", "z", "c")
ROWS = ("x", "z")
COLS = ("c", "y")
NROWS = 32
NCOLS = 16
F32 = jnp.float32
NREG = 4
SLAB = 96
VMEM = pl.BlockSpec(memory_space=pltpu.VMEM)


def shape(*dims):
    return jax.ShapeDtypeStruct(dims, F32)


def call(kernel, outs, ins, scratch=(), space=VMEM, cost=0, limit=24, alias=None):
    return pl.pallas_call(
        kernel,
        out_shape=outs,
        in_specs=[space] * len(ins),
        out_specs=jax.tree.map(lambda _: VMEM, outs),
        scratch_shapes=list(scratch),
        input_output_aliases=alias or {},
        cost_estimate=pl.CostEstimate(flops=cost, bytes_accessed=cost, transcendentals=0) if cost else None,
        compiler_params=pltpu.CompilerParams(vmem_limit_bytes=int(limit * 1024 * 1024)),
    )(*ins)


def total(v):
    return jnp.sum(jnp.sum(v, axis=0, keepdims=True), axis=1, keepdims=True)


def add_regions(accs, label, field):
    out = list(accs)
    for g in range(NREG):
        mask = label == g + 1
        for c in range(3):
            out[3 * g + c] = out[3 * g + c] + jnp.where(mask, field[c], 0.0)
    return out


def in_lanes(acc_ref, at):
    sums = jnp.sum(jnp.sum(acc_ref[...], axis=1), axis=1, keepdims=True)
    row = lax.broadcasted_iota(jnp.int32, (12, 128), 0)
    lane = lax.broadcasted_iota(jnp.int32, (12, 128), 1)
    return jnp.sum(jnp.where(lane == row + at, sums, 0.0), axis=0, keepdims=True)


def fold(accs, coarse_ref, acc_ref, u_ref, pad_ref, out_ref, sums=()):
    for i in range(3 * NREG):
        acc_ref[i] = accs[i]
    rc = jnp.sum(jnp.sum(acc_ref[...], axis=1), axis=1, keepdims=True)
    u_ref[...] = jnp.sum(coarse_ref[...] * rc, axis=0, keepdims=True)
    pad_ref[...] = jnp.zeros_like(pad_ref)
    for w in range(2 * NROWS):
        pad_ref[w + 1 : w + 2, 0:SLAB] = u_ref[0:1, SLAB * w : SLAB * (w + 1)]
    if sums:
        lane = lax.broadcasted_iota(jnp.int32, (1, 128), 1)
        row = jnp.zeros((1, 128), F32)
        for i, s in enumerate(sums):
            row = jnp.where(lane == SLAB + i, s, row)
        tail = jnp.broadcast_to(row, (4, 128))
    for n in range(NROWS):
        window = pad_ref[2 * n : 2 * n + 4, :]
        if sums:
            window = window + tail
        out_ref[n] = window


FOLD_SCRATCH = (
    pltpu.VMEM((12, 16, 128), F32),
    pltpu.VMEM((1, 6144), F32),
    pltpu.VMEM((72, 128), F32),
)


def first_kernel(
    r_hbm, occ_hbm, reg_hbm, coarse_hbm,
    out_ref, lo_ref, hi_ref, r_ref, k_ref, label_ref, coarse_ref,
    occ_ref, reg_ref, acc_ref, u_ref, pad_ref, sems,
):
    pairs = ((r_hbm, r_ref), (reg_hbm, reg_ref), (occ_hbm, occ_ref), (coarse_hbm, coarse_ref))
    copies = [pltpu.make_async_copy(a, b, sems.at[i]) for i, (a, b) in enumerate(pairs)]
    for copy in copies:
        copy.start()
    for copy in copies[:3]:
        copy.wait()
    k_ref[...] = 0.1 + 0.9 * occ_ref[...].astype(F32)
    label_ref[...] = reg_ref[...].astype(F32) + 1.0
    for ref, deep, flat in ((lo_ref, 0, 0), (hi_ref, 12, 14)):
        ref[0] = k_ref[:, deep : deep + 4, :]
        ref[1, :, 0:2] = label_ref[:, flat : flat + 2, :]
        ref[1, :, 2:4] = r_ref[0, :, flat : flat + 2, :]
        ref[2, :, 0:2] = r_ref[1, :, flat : flat + 2, :]
        ref[2, :, 2:4] = r_ref[2, :, flat : flat + 2, :]

    def step(x, accs):
        return tuple(add_regions(accs, label_ref[x], [r_ref[c, x] for c in range(3)]))

    zero = jnp.zeros((16, 128), F32)
    accs = lax.fori_loop(0, 16, step, (zero,) * 12, unroll=2)
    copies[3].wait()
    fold(accs, coarse_ref, acc_ref, u_ref, pad_ref, out_ref)


def hand_out(part, out_ref):
    for c in range(2):
        rows = part[c : c + 3]
        for y in range(8):
            out_ref[8 * c + y, 0:3, :] = pltpu.roll(rows, (12 - 12 * y) % 128, axis=1)
            out_ref[8 * c + y, 3:4, :] = part[0:1]


def tail_rows(lo_ref, hi_ref, i, planes):
    if i == 0:
        return jnp.concatenate([hi_ref[0, planes], lo_ref[0, planes]], axis=1)
    block, at = 1 + (i - 1) // 2, 2 * ((i - 1) % 2)
    above, below = hi_ref[block, planes, at : at + 2], lo_ref[block, planes, at : at + 2]
    none = jnp.zeros((above.shape[0], 4, 128), F32)
    return jnp.concatenate([above, none, below], axis=1)


PACK = 72 + 4 * 40


def pack_kernel(k_ref, label_ref, r_ref, lo_ref, hi_ref, up_ref, down_ref):
    fields = [label_ref] + [r_ref.at[c] for c in range(3)]
    for ref, deep, near, next_ in ((up_ref, 13, 15, 14), (down_ref, 0, 0, 1)):
        tails = tail_rows(lo_ref, hi_ref, 0, pl.ds(deep, 3))
        for i in range(3):
            ref[24 * i : 24 * i + 16] = k_ref[deep + i]
            ref[24 * i + 16 : 24 * i + 24] = tails[i]
        for i, field in enumerate(fields):
            at = 72 + 40 * i
            ref[at : at + 16] = field[near]
            ref[at + 16 : at + 24] = tail_rows(lo_ref, hi_ref, 1 + i, pl.ds(near, 1))[0]
            ref[at + 24 : at + 40] = field[next_]


def extend_kernel(
    r_ref, k_own_ref, label_own_ref, lo_ref, hi_ref, below_ref, above_ref, k_ref, label_ref, inv_ref, f_ref
):
    whole = pl.ds(0, 16)
    k_ref[3:19, 0:16] = k_own_ref[...]
    label_ref[3:19, 0:16] = label_own_ref[...]
    k_ref[3:19, 16:24] = tail_rows(lo_ref, hi_ref, 0, whole)
    label_ref[3:19, 16:24] = tail_rows(lo_ref, hi_ref, 1, whole)
    none = jnp.zeros((8, 128), F32)
    for i in range(3):
        k_ref[i] = below_ref[24 * i : 24 * i + 24]
        k_ref[19 + i] = above_ref[24 * i : 24 * i + 24]
    targets = [label_ref] + [f_ref.at[c] for c in range(3)]
    for i, ref in enumerate(targets):
        at = 72 + 40 * i
        for pack, near, next_ in ((below_ref, 2, 1), (above_ref, 19, 20)):
            ref[near] = pack[at : at + 24]
            ref[next_, 0:16] = pack[at + 24 : at + 40]
            ref[next_, 16:24] = none
    for c in range(3):
        f_ref[c, 3:19, 0:16] = r_ref[c]
        f_ref[c, 3:19, 16:24] = tail_rows(lo_ref, hi_ref, 2 + c, whole)

    def step(x, carry):
        here = k_ref[x]
        _, diagonal = coefficients(k_ref[x - 1], here, k_ref[x + 1])
        inside = here > 0.0
        inv = jnp.where(inside, 1.0 / jnp.where(inside, diagonal, 1.0), 0.0)
        inv_ref[x] = inv
        for c in range(3):
            f_ref[c, x] = f_ref[c, x] * inv
        return carry

    lax.fori_loop(1, 21, step, 0, unroll=2)


def around_kernel(recv_ref, out_ref):
    hand_out(jnp.sum(recv_ref[...], axis=0), out_ref)


def pass_kernel(recv_ref, own_ref, pair_ref, out_ref):
    part = jnp.sum(recv_ref[...], axis=0)
    rows = jnp.concatenate([part, own_ref[...], pair_ref[...]], axis=0)
    for n in range(NCOLS):
        out_ref[n] = rows


def iotas():
    lane = lax.broadcasted_iota(jnp.int32, (24, 128), 1)
    return lane == 0, lane == 127


def coefficients(before, here, after):
    first, last = iotas()
    y_up = pltpu.roll(here, 23, axis=0)
    y_down = pltpu.roll(here, 1, axis=0)
    z_up = jnp.where(last, 0.0, pltpu.roll(here, 127, axis=1))
    z_down = jnp.where(first, 0.0, pltpu.roll(here, 1, axis=1))
    half = 0.5 * here
    faces = [half + 0.5 * other for other in (after, before, y_up, y_down, z_up, z_down)]
    diagonal = faces[0] + faces[1] + faces[2] + faces[3] + faces[4] + faces[5] + half
    faces[4] = jnp.where(last, 0.0, faces[4])
    faces[5] = jnp.where(first, 0.0, faces[5])
    return faces, diagonal


def operate(faces, diagonal, here, befores, fields, afters):
    quarter = 0.25 * here
    main = diagonal - quarter
    shared = quarter * (fields[0] + fields[1] + fields[2])
    out = []
    for c in range(3):
        u = fields[c]
        out.append(
            main * u
            + shared
            - faces[0] * afters[c]
            - faces[1] * befores[c]
            - faces[2] * pltpu.roll(u, 23, axis=0)
            - faces[3] * pltpu.roll(u, 1, axis=0)
            - faces[4] * pltpu.roll(u, 127, axis=1)
            - faces[5] * pltpu.roll(u, 1, axis=1)
        )
    return out


def spread_maps(q, map_ref):
    row = lax.broadcasted_iota(jnp.int32, (24, 128), 0)
    for s in range(3):
        for i in range(12):
            below, own, above = (q[s : s + 1, 12 * d + i : 12 * d + i + 1] for d in range(3))
            map_ref[s, i] = jnp.where(row < 16, own, jnp.where(row < 20, above, below))


def spread(label, map_ref, s, c):
    out = jnp.zeros((24, 128), F32)
    for g in range(NREG):
        out = jnp.where(label == g + 1, map_ref[s, 3 * g + c], out)
    return out


def second_kernel(
    recv_ref, r_ref, k_ref, label_ref, f_ref, coarse_ref,
    out_ref, z_ref, w_ref, own_ref,
    map_ref, acc_ref, u_ref, pad_ref,
):
    q = jnp.sum(recv_ref[...], axis=0)
    spread_maps(q, map_ref)

    def first_step(s):
        def body(x, carry):
            label = label_ref[x]
            for c in range(3):
                z_ref[c, x] = f_ref[c, x] + spread(label, map_ref, s, c)
            return carry

        return body

    lax.fori_loop(1, 3, first_step(0), 0)
    lax.fori_loop(3, 19, first_step(1), 0, unroll=2)
    lax.fori_loop(19, 21, first_step(2), 0)

    def image(x):
        here = k_ref[x]
        faces, diagonal = coefficients(k_ref[x - 1], here, k_ref[x + 1])
        fields = [z_ref[c, x] for c in range(3)]
        w = operate(
            faces, diagonal, here, [z_ref[c, x - 1] for c in range(3)], fields, [z_ref[c, x + 1] for c in range(3)]
        )
        for c in range(3):
            w_ref[c, x - 2] = w[c]
        return fields, w

    image(2)
    image(19)

    def second_step(x, carry):
        fields, w = image(x)
        own = [v[0:16] for v in w]
        rz, zw = carry[12], carry[13]
        for c in range(3):
            z = fields[c][0:16]
            rz = rz + r_ref[c, x - 3] * z
            zw = zw + z * own[c]
        return (*add_regions(carry[:12], label_ref[x, 0:16], own), rz, zw)

    zero = jnp.zeros((16, 128), F32)
    carry = lax.fori_loop(3, 19, second_step, (zero,) * 14)
    fold(carry[:12], coarse_ref, acc_ref, u_ref, pad_ref, out_ref, (total(carry[12]), total(carry[13])))
    own_ref[...] = in_lanes(acc_ref, 12)


def selection():
    out = np.zeros((88, 3 * 128), np.float32)
    for n in range(5):
        for d in range(4):
            for h in range(4):
                g = (h + d) % 4
                for c in range(3):
                    lane = 128 * (n // 2) + 48 * (n % 2) + 12 * d + 3 * h + c
                    out[16 * n + 4 * g + h, lane] -= 1.0
                    if n == 0:
                        out[4 * h + g, lane] -= 1.0
                        if d == 0:
                            out[80 + g, lane] += 1.0
                            out[84 + g, lane] += 1.0
    for g in range(4):
        out[80 + g, 96 + 3 * g] = 1.0
    return out


def tiles(v):
    return v[0:8] + v[8:16]


def pair_kernel(k_ref, label_ref, select_ref, out_ref, acc_ref):
    row = lax.broadcasted_iota(jnp.int32, (24, 128), 0)
    lane = lax.broadcasted_iota(jnp.int32, (24, 128), 1)

    def plane(x, accs, inner):
        here, label = k_ref[x], label_ref[x]
        faces, diagonal = coefficients(k_ref[x - 1], here, k_ref[x + 1])
        y_label = jnp.where(row == 15, 0.0, pltpu.roll(label, 23, axis=0))[0:16]
        z_label = jnp.where(lane == 127, 0.0, pltpu.roll(label, 127, axis=1))[0:16]
        own = label[0:16]
        quarter, coupling = 0.25 * here[0:16], (diagonal - 0.5 * here)[0:16]
        masks = [own == g + 1 for g in range(NREG)]
        out = list(accs)
        for h in range(NREG):
            v = jnp.where(y_label == h + 1, faces[2][0:16], 0.0) + jnp.where(z_label == h + 1, faces[4][0:16], 0.0)
            if inner:
                v = v + jnp.where(label_ref[x + 1, 0:16] == h + 1, faces[0][0:16], 0.0)
            for g in range(NREG):
                out[4 * g + h] = out[4 * g + h] + tiles(jnp.where(masks[g], v, 0.0))
        for g in range(NREG):
            out[16 + g] = out[16 + g] + tiles(jnp.where(masks[g], quarter, 0.0))
            out[20 + g] = out[20 + g] + tiles(jnp.where(masks[g], coupling, 0.0))
        return tuple(out)

    zero = jnp.zeros((8, 128), F32)
    accs = lax.fori_loop(3, 18, lambda x, a: plane(x, a, True), (zero,) * 24)
    accs = plane(18, accs, False)
    for i in range(16):
        acc_ref[i] = accs[i]
    for i in range(8):
        acc_ref[80 + i] = accs[16 + i]
    own = pl.ds(3, 16)
    sides = (
        (k_ref[3, 0:16], label_ref[3, 0:16], k_ref[2, 0:16], label_ref[2, 0:16]),
        (k_ref[18, 0:16], label_ref[18, 0:16], k_ref[19, 0:16], label_ref[19, 0:16]),
        (k_ref[own, 0, :], label_ref[own, 0, :], k_ref[own, 23, :], label_ref[own, 23, :]),
        (k_ref[own, 15, :], label_ref[own, 15, :], k_ref[own, 16, :], label_ref[own, 16, :]),
    )
    for n, (k, label, other, other_label) in enumerate(sides):
        face = 0.5 * k + 0.5 * other
        for g in range(NREG):
            part = jnp.where(label == g + 1, face, 0.0)
            for h in range(NREG):
                acc_ref[16 * n + 16 + 4 * g + h] = tiles(jnp.where(other_label == h + 1, part, 0.0))
    sums = jnp.sum(jnp.sum(acc_ref[...], axis=1), axis=1, keepdims=True)
    for i in range(3):
        out_ref[i : i + 1] = jnp.sum(select_ref[:, 128 * i : 128 * i + 128] * sums, axis=0, keepdims=True)


def moment_kernel(k_ref, label_ref, inv_ref, w_ref, own_ref, out_ref, g_ref, acc_ref):
    def first_step(x, carry):
        inv = inv_ref[x]
        for c in range(3):
            g_ref[c, x - 2] = w_ref[c, x - 2] * inv
        return carry

    lax.fori_loop(2, 20, first_step, 0, unroll=2)

    def step(x, carry):
        here = k_ref[x + 2]
        faces, diagonal = coefficients(k_ref[x + 1], here, k_ref[x + 3])
        fields = [g_ref[c, x] for c in range(3)]
        image = operate(
            faces, diagonal, here, [g_ref[c, x - 1] for c in range(3)], fields, [g_ref[c, x + 1] for c in range(3)]
        )
        own = [v[0:16] for v in image]
        wg, gg = carry[12], carry[13]
        for c in range(3):
            g = fields[c][0:16]
            wg = wg + w_ref[c, x, 0:16] * g
            gg = gg + own[c] * g
        return (*add_regions(carry[:12], label_ref[x + 2, 0:16], own), wg, gg)

    zero = jnp.zeros((16, 128), F32)
    carry = lax.fori_loop(1, 17, step, (zero,) * 14)
    for i in range(12):
        acc_ref[i] = carry[i]
    lane = lax.broadcasted_iota(jnp.int32, (1, 128), 1)
    row = in_lanes(acc_ref, 0) + own_ref[...]
    out_ref[...] = jnp.where(lane == 24, total(carry[12]), jnp.where(lane == 25, total(carry[13]), row))


def group_kernel(recv_ref, out_ref):
    q = jnp.sum(recv_ref[:, 0:4, :], axis=0)
    own = recv_ref[:, 4, :]
    lane = lax.broadcasted_iota(jnp.int32, (16, 128), 1)
    shifted_rows = []
    for s in range(4):
        shifted_rows.append(
            jnp.concatenate([pltpu.roll(q[s : s + 1], (128 - 12 * y) % 128, axis=1) for y in range(8)], axis=0)
        )
    mine, below, above = (
        jnp.concatenate([shifted_rows[s], shifted_rows[s + 1]], axis=0) for s in (1, 0, 2)
    )

    def right(v, by):
        return pltpu.roll(v, by % 128, axis=1)

    def first(v):
        return jnp.where(lane < 12, v, 0.0)

    def four(v):
        v = first(v)
        v = v + right(v, 12)
        return v + right(v, 24)

    alone = first(mine)
    twice = alone + right(alone, 12)
    turned = alone
    for d in range(1, 4):
        turned = turned + right(first(right(twice, -3 * d)), 12 * d)
    turned = turned + right(turned, 48)
    three = mine + right(mine, -1) + right(mine, -2)
    products = (
        recv_ref[:, 5, :] * (turned * (four(mine) + right(four(below), 48)) + right(first(three * three), 96))
        + recv_ref[:, 6, :] * turned * (four(above) + right(four(right(mine, 12)), 48))
        + recv_ref[:, 7, :] * turned * four(right(mine, -12))
        + 2.0 * jnp.where(lane < 12, own * alone, 0.0)
        + jnp.where(lane == 25, own, 0.0)
    )
    pairing = jnp.where((lane >= 12) & (lane < 24), own * twice, jnp.where(lane == 24, own, 0.0))
    at = lax.broadcasted_iota(jnp.int32, (1, 128), 1)
    row = jnp.where(at == 0, total(pairing), jnp.where(at == 1, total(products), 0.0))
    for n in range(NROWS):
        out_ref[n] = row


def third_kernel(recv_ref, k_ref, label_ref, inv_ref, z_ref, w_ref, scal_ref, own_ref, image_ref, znew_ref, map_ref):
    q = jnp.sum(recv_ref[:, 0:4, :], axis=0)
    near = jnp.where(lax.axis_index("c") == 0, q[0:3], q[1:4])
    spread_maps(pltpu.roll(near, lax.rem(140 - 12 * lax.axis_index("y"), 128), axis=1), map_ref)
    scal_ref[...] = q[0:1]
    rz, zw = q[0:1, SLAB : SLAB + 1], q[0:1, SLAB + 1 : SLAB + 2]
    alpha = rz / zw

    def first_step(s):
        def body(x, carry):
            inv, label = inv_ref[x], label_ref[x]
            for c in range(3):
                y = w_ref[c, x - 2] * inv + spread(label, map_ref, s, c)
                znew_ref[c, x - 2] = z_ref[c, x] - alpha * y
            return carry

        return body

    first_step(0)(2, 0)
    lax.fori_loop(3, 19, first_step(1), 0, unroll=2)
    first_step(2)(19, 0)

    def second_step(x, carry):
        here = k_ref[x + 2]
        faces, diagonal = coefficients(k_ref[x + 1], here, k_ref[x + 3])
        fields = [znew_ref[c, x] for c in range(3)]
        image = operate(
            faces, diagonal, here, [znew_ref[c, x - 1] for c in range(3)], fields, [znew_ref[c, x + 1] for c in range(3)]
        )
        for c in range(3):
            own_ref[c, x - 1] = fields[c][0:16]
            image_ref[c, x - 1] = image[c][0:16]
        return carry

    lax.fori_loop(1, 17, second_step, 0)


def last_kernel(recv_ref, scal_ref, r_ref, z_ref, w_ref, znew_ref, image_ref, x_ref, res_ref):
    sums = jnp.sum(recv_ref[...], axis=0)
    wy, yay = sums[:, 0:1], sums[:, 1:2]
    scal = scal_ref[...]
    rz, zw = scal[:, SLAB : SLAB + 1], scal[:, SLAB + 1 : SLAB + 2]
    alpha = rz / zw
    new = rz + alpha * (alpha * wy - 2.0 * zw)
    zaz = zw + alpha * (alpha * yay - 2.0 * wy)
    cross = zw - alpha * wy
    ratio = new / rz
    second = new / (zaz + ratio * (2.0 * cross + ratio * zw))
    first = alpha + second * ratio

    def step(x, carry):
        for c in range(3):
            x_ref[c, x] = first * z_ref[c, x + 3, 0:16] + second * znew_ref[c, x]
            res_ref[c, x] = r_ref[c, x] - first * w_ref[c, x + 1, 0:16] - second * image_ref[c, x]
        return carry

    lax.fori_loop(0, 16, step, 0, unroll=2)


def exchange(array, axes):
    return lax.all_to_all(array, axes, 0, 0, tiled=True)


def shifted(array, axis, step):
    count = lax.axis_size(axis)
    pairs = [(i, i + step) for i in range(count) if 0 <= i + step < count]
    return lax.ppermute(array, axis, pairs)


def local(right, occ, reg, coarse):
    field, plane = (16, 16, 128), (24, 128)
    send, lo, hi, r, k_own, label_own, coarse = call(
        first_kernel,
        (
            shape(NROWS, 4, 128),
            shape(3, 16, 4, 128),
            shape(3, 16, 4, 128),
            shape(3, *field),
            shape(*field),
            shape(*field),
            shape(12, 6144),
        ),
        tuple(pltpu.with_memory_space_constraint(a, pltpu.HBM) for a in (right, occ, reg, coarse)),
        (
            pltpu.VMEM(field, jnp.int32),
            pltpu.VMEM(field, jnp.int32),
            *FOLD_SCRATCH,
            pltpu.SemaphoreType.DMA((4,)),
        ),
        space=pl.BlockSpec(memory_space=pltpu.HBM),
        limit=24,
    )
    before = shifted(hi, "y", 1)
    after = shifted(lo, "y", -1)
    got = exchange(send, ROWS)
    up, down = call(
        pack_kernel, (shape(PACK, 128), shape(PACK, 128)), (k_own, label_own, r, before, after), cost=1000000
    )
    below = shifted(up, WIDE, 1)
    above = shifted(down, WIDE, -1)
    send = call(around_kernel, shape(NCOLS, 4, 128), (got,))
    got = exchange(send, COLS)
    k, label, inv, f = call(
        extend_kernel,
        (shape(22, *plane), shape(22, *plane), shape(22, *plane), shape(3, 22, *plane)),
        (r, k_own, label_own, before, after, below, above),
        cost=3000000,
    )
    pair = call(
        pair_kernel, shape(3, 128), (k, label, jnp.asarray(selection())), (pltpu.VMEM((88, 8, 128), F32),), cost=3000000
    )
    send, z, w, own = call(
        second_kernel,
        (shape(NROWS, 4, 128), shape(3, 22, *plane), shape(3, 18, *plane), shape(1, 128)),
        (got, r, k, label, f, coarse),
        (pltpu.VMEM((3, 12, *plane), F32), *FOLD_SCRATCH),
        alias={4: 1},
    )
    got = exchange(send, ROWS)
    own = call(
        moment_kernel,
        shape(1, 128),
        (k, label, inv, w, own),
        (pltpu.VMEM((3, 18, *plane), F32), pltpu.VMEM((12, 16, 128), F32)),
        cost=3000000,
    )
    send = call(pass_kernel, shape(NCOLS, 8, 128), (got, own, pair))
    got = exchange(send, COLS)
    send = call(group_kernel, shape(NROWS, 1, 128), (got,))
    scal, znew, image = call(
        third_kernel,
        (shape(1, 128), shape(3, *field), shape(3, *field)),
        (got, k, label, inv, z, w),
        (pltpu.VMEM((3, 18, *plane), F32), pltpu.VMEM((3, 12, *plane), F32)),
        cost=3000000,
    )
    got = exchange(send, ROWS)
    return call(
        last_kernel,
        (shape(3, *field), shape(3, *field)),
        (got, scal, right, z, w, znew, image),
    )


def solution(mesh):
    finer = Mesh(mesh.devices.reshape(4, 8, 2, 8), ("x", "z", "c", "y"))
    field = P(None, WIDE, "y", None)
    labels = P(WIDE, "y", None)
    return jax.shard_map(
        local,
        mesh=finer,
        in_specs=(field, labels, labels, P((*WIDE, "y"), None)),
        out_specs=(field, field),
        check_vma=False,
    )
```

```python
import jax
import jax.numpy as jnp
import numpy as np
from jax import lax
from jax.experimental import pallas as pl
from jax.experimental.pallas import tpu as pltpu
from jax.sharding import Mesh
from jax.sharding import PartitionSpec as P

WIDE = ("x", "z", "c")
ROWS = ("x", "z")
COLS = ("c", "y")
NROWS = 32
NCOLS = 16
F32 = jnp.float32
NREG = 4
SLAB = 96
VMEM = pl.BlockSpec(memory_space=pltpu.VMEM)


def shape(*dims):
    return jax.ShapeDtypeStruct(dims, F32)


def call(kernel, outs, ins, scratch=(), space=VMEM, cost=0, limit=24, alias=None):
    return pl.pallas_call(
        kernel,
        out_shape=outs,
        in_specs=[space] * len(ins),
        out_specs=jax.tree.map(lambda _: VMEM, outs),
        scratch_shapes=list(scratch),
        input_output_aliases=alias or {},
        cost_estimate=pl.CostEstimate(flops=cost, bytes_accessed=cost, transcendentals=0) if cost else None,
        compiler_params=pltpu.CompilerParams(vmem_limit_bytes=int(limit * 1024 * 1024)),
    )(*ins)


def total(v):
    return jnp.sum(jnp.sum(v, axis=0, keepdims=True), axis=1, keepdims=True)


def add_regions(accs, label, field):
    out = list(accs)
    for g in range(NREG):
        mask = label == g + 1
        for c in range(3):
            out[3 * g + c] = out[3 * g + c] + jnp.where(mask, field[c], 0.0)
    return out


def in_lanes(acc_ref, at):
    sums = jnp.sum(jnp.sum(acc_ref[...], axis=1), axis=1, keepdims=True)
    row = lax.broadcasted_iota(jnp.int32, (12, 128), 0)
    lane = lax.broadcasted_iota(jnp.int32, (12, 128), 1)
    return jnp.sum(jnp.where(lane == row + at, sums, 0.0), axis=0, keepdims=True)


def fold(accs, coarse_ref, acc_ref, u_ref, pad_ref, out_ref, sums=()):
    for i in range(3 * NREG):
        acc_ref[i] = accs[i]
    rc = jnp.sum(jnp.sum(acc_ref[...], axis=1), axis=1, keepdims=True)
    u_ref[...] = jnp.sum(coarse_ref[...] * rc, axis=0, keepdims=True)
    pad_ref[...] = jnp.zeros_like(pad_ref)
    for w in range(2 * NROWS):
        pad_ref[w + 1 : w + 2, 0:SLAB] = u_ref[0:1, SLAB * w : SLAB * (w + 1)]
    if sums:
        lane = lax.broadcasted_iota(jnp.int32, (1, 128), 1)
        row = jnp.zeros((1, 128), F32)
        for i, s in enumerate(sums):
            row = jnp.where(lane == SLAB + i, s, row)
        tail = jnp.broadcast_to(row, (4, 128))
    for n in range(NROWS):
        window = pad_ref[2 * n : 2 * n + 4, :]
        if sums:
            window = window + tail
        out_ref[n] = window


FOLD_SCRATCH = (
    pltpu.VMEM((12, 16, 128), F32),
    pltpu.VMEM((1, 6144), F32),
    pltpu.VMEM((72, 128), F32),
)


def even_column():
    return lax.rem(lax.axis_index("y"), 2) == 0


def first_kernel(
    r_hbm, occ_hbm, reg_hbm, coarse_hbm,
    out_ref, a_ref, b_ref, r_ref, k_ref, label_ref, coarse_ref,
    occ_ref, reg_ref, acc_ref, u_ref, pad_ref, sems,
):
    pairs = ((r_hbm, r_ref), (reg_hbm, reg_ref), (occ_hbm, occ_ref), (coarse_hbm, coarse_ref))
    copies = [pltpu.make_async_copy(a, b, sems.at[i]) for i, (a, b) in enumerate(pairs)]
    for copy in copies:
        copy.start()
    for copy in copies[:3]:
        copy.wait()
    k_ref[...] = 0.1 + 0.9 * occ_ref[...].astype(F32)
    label_ref[...] = reg_ref[...].astype(F32) + 1.0
    even = even_column()
    for ref, last in ((a_ref, even), (b_ref, jnp.logical_not(even))):
        ref[0] = jnp.where(last, k_ref[:, 12:16, :], k_ref[:, 0:4, :])
        for i, field in enumerate([label_ref] + [r_ref.at[c] for c in range(3)]):
            at = 2 * (i % 2)
            ref[1 + i // 2, :, at : at + 2] = jnp.where(last, field[:, 14:16, :], field[:, 0:2, :])

    def step(x, accs):
        return tuple(add_regions(accs, label_ref[x], [r_ref[c, x] for c in range(3)]))

    zero = jnp.zeros((16, 128), F32)
    accs = lax.fori_loop(0, 16, step, (zero,) * 12, unroll=2)
    copies[3].wait()
    fold(accs, coarse_ref, acc_ref, u_ref, pad_ref, out_ref)


def hand_out(part, out_ref):
    for c in range(2):
        rows = part[c : c + 3]
        for y in range(8):
            out_ref[8 * c + y, 0:3, :] = pltpu.roll(rows, (12 - 12 * y) % 128, axis=1)
            out_ref[8 * c + y, 3:4, :] = part[0:1]


def tail_rows(a_ref, b_ref, i, planes):
    even = even_column()
    if i == 0:
        one, two = a_ref[0, planes], b_ref[0, planes]
        return jnp.concatenate([jnp.where(even, one, two), jnp.where(even, two, one)], axis=1)
    block, at = 1 + (i - 1) // 2, 2 * ((i - 1) % 2)
    one, two = a_ref[block, planes, at : at + 2], b_ref[block, planes, at : at + 2]
    none = jnp.zeros((one.shape[0], 4, 128), F32)
    return jnp.concatenate([jnp.where(even, one, two), none, jnp.where(even, two, one)], axis=1)


PACK = 72 + 4 * 40


def pack_kernel(k_ref, label_ref, r_ref, a_ref, b_ref, first_ref, second_ref):
    fields = [label_ref] + [r_ref.at[c] for c in range(3)]
    core = lax.axis_index("c")
    for ref, up in ((first_ref, core == 0), (second_ref, core == 1)):
        deep, near, next_ = jnp.where(up, 13, 0), jnp.where(up, 15, 0), jnp.where(up, 14, 1)
        tails = tail_rows(a_ref, b_ref, 0, pl.ds(deep, 3))
        for i in range(3):
            ref[24 * i : 24 * i + 16] = k_ref[deep + i]
            ref[24 * i + 16 : 24 * i + 24] = tails[i]
        for i, field in enumerate(fields):
            at = 72 + 40 * i
            ref[at : at + 16] = field[near]
            ref[at + 16 : at + 24] = tail_rows(a_ref, b_ref, 1 + i, pl.ds(near, 1))[0]
            ref[at + 24 : at + 40] = field[next_]


def extend_kernel(
    r_ref, k_own_ref, label_own_ref, a_ref, b_ref, first_ref, second_ref, k_ref, label_ref, inv_ref, f_ref
):
    whole = pl.ds(0, 16)
    core = lax.axis_index("c")

    def sides(rows):
        one, two = first_ref[rows], second_ref[rows]
        return jnp.where(core == 0, two, one), jnp.where(core == 0, one, two)

    k_ref[3:19, 0:16] = k_own_ref[...]
    label_ref[3:19, 0:16] = label_own_ref[...]
    k_ref[3:19, 16:24] = tail_rows(a_ref, b_ref, 0, whole)
    label_ref[3:19, 16:24] = tail_rows(a_ref, b_ref, 1, whole)
    none = jnp.zeros((8, 128), F32)
    for i in range(3):
        below, above = sides(slice(24 * i, 24 * i + 24))
        k_ref[i] = below
        k_ref[19 + i] = above
    targets = [label_ref] + [f_ref.at[c] for c in range(3)]
    for i, ref in enumerate(targets):
        at = 72 + 40 * i
        ref[2], ref[19] = sides(slice(at, at + 24))
        ref[1, 0:16], ref[20, 0:16] = sides(slice(at + 24, at + 40))
        ref[1, 16:24] = ref[20, 16:24] = none
    for c in range(3):
        f_ref[c, 3:19, 0:16] = r_ref[c]
        f_ref[c, 3:19, 16:24] = tail_rows(a_ref, b_ref, 2 + c, whole)

    def step(x, carry):
        here = k_ref[x]
        _, diagonal = coefficients(k_ref[x - 1], here, k_ref[x + 1])
        inside = here > 0.0
        inv = jnp.where(inside, 1.0 / jnp.where(inside, diagonal, 1.0), 0.0)
        inv_ref[x] = inv
        for c in range(3):
            f_ref[c, x] = f_ref[c, x] * inv
        return carry

    lax.fori_loop(1, 21, step, 0, unroll=2)


def around_kernel(recv_ref, out_ref):
    hand_out(jnp.sum(recv_ref[...], axis=0), out_ref)


def pass_kernel(recv_ref, own_ref, pair_ref, out_ref):
    part = jnp.sum(recv_ref[...], axis=0)
    rows = jnp.concatenate([part, own_ref[...], pair_ref[...]], axis=0)
    for n in range(NCOLS):
        out_ref[n] = rows


def iotas():
    lane = lax.broadcasted_iota(jnp.int32, (24, 128), 1)
    return lane == 0, lane == 127


def coefficients(before, here, after):
    first, last = iotas()
    y_up = pltpu.roll(here, 23, axis=0)
    y_down = pltpu.roll(here, 1, axis=0)
    z_up = jnp.where(last, 0.0, pltpu.roll(here, 127, axis=1))
    z_down = jnp.where(first, 0.0, pltpu.roll(here, 1, axis=1))
    half = 0.5 * here
    faces = [half + 0.5 * other for other in (after, before, y_up, y_down, z_up, z_down)]
    diagonal = faces[0] + faces[1] + faces[2] + faces[3] + faces[4] + faces[5] + half
    faces[4] = jnp.where(last, 0.0, faces[4])
    faces[5] = jnp.where(first, 0.0, faces[5])
    return faces, diagonal


def operate(faces, diagonal, here, befores, fields, afters):
    quarter = 0.25 * here
    main = diagonal - quarter
    shared = quarter * (fields[0] + fields[1] + fields[2])
    out = []
    for c in range(3):
        u = fields[c]
        out.append(
            main * u
            + shared
            - faces[0] * afters[c]
            - faces[1] * befores[c]
            - faces[2] * pltpu.roll(u, 23, axis=0)
            - faces[3] * pltpu.roll(u, 1, axis=0)
            - faces[4] * pltpu.roll(u, 127, axis=1)
            - faces[5] * pltpu.roll(u, 1, axis=1)
        )
    return out


def spread_maps(q, map_ref):
    row = lax.broadcasted_iota(jnp.int32, (24, 128), 0)
    for s in range(3):
        for i in range(12):
            below, own, above = (q[s : s + 1, 12 * d + i : 12 * d + i + 1] for d in range(3))
            map_ref[s, i] = jnp.where(row < 16, own, jnp.where(row < 20, above, below))


def spread(label, map_ref, s, c):
    out = jnp.zeros((24, 128), F32)
    for g in range(NREG):
        out = jnp.where(label == g + 1, map_ref[s, 3 * g + c], out)
    return out


def second_kernel(
    recv_ref, r_ref, k_ref, label_ref, f_ref, coarse_ref,
    out_ref, z_ref, w_ref, own_ref,
    map_ref, acc_ref, u_ref, pad_ref,
):
    q = jnp.sum(recv_ref[...], axis=0)
    spread_maps(q, map_ref)

    def first_step(s):
        def body(x, carry):
            label = label_ref[x]
            for c in range(3):
                z_ref[c, x] = f_ref[c, x] + spread(label, map_ref, s, c)
            return carry

        return body

    lax.fori_loop(1, 3, first_step(0), 0)
    lax.fori_loop(3, 19, first_step(1), 0, unroll=2)
    lax.fori_loop(19, 21, first_step(2), 0)

    def image(x):
        here = k_ref[x]
        faces, diagonal = coefficients(k_ref[x - 1], here, k_ref[x + 1])
        fields = [z_ref[c, x] for c in range(3)]
        w = operate(
            faces, diagonal, here, [z_ref[c, x - 1] for c in range(3)], fields, [z_ref[c, x + 1] for c in range(3)]
        )
        for c in range(3):
            w_ref[c, x - 2] = w[c]
        return fields, w

    image(2)
    image(19)

    def second_step(x, carry):
        fields, w = image(x)
        own = [v[0:16] for v in w]
        rz, zw = carry[12], carry[13]
        for c in range(3):
            z = fields[c][0:16]
            rz = rz + r_ref[c, x - 3] * z
            zw = zw + z * own[c]
        return (*add_regions(carry[:12], label_ref[x, 0:16], own), rz, zw)

    zero = jnp.zeros((16, 128), F32)
    carry = lax.fori_loop(3, 19, second_step, (zero,) * 14)
    fold(carry[:12], coarse_ref, acc_ref, u_ref, pad_ref, out_ref, (total(carry[12]), total(carry[13])))
    own_ref[...] = in_lanes(acc_ref, 12)


def selection():
    out = np.zeros((88, 3 * 128), np.float32)
    for n in range(5):
        for d in range(4):
            for h in range(4):
                g = (h + d) % 4
                for c in range(3):
                    lane = 128 * (n // 2) + 48 * (n % 2) + 12 * d + 3 * h + c
                    out[16 * n + 4 * g + h, lane] -= 1.0
                    if n == 0:
                        out[4 * h + g, lane] -= 1.0
                        if d == 0:
                            out[80 + g, lane] += 1.0
                            out[84 + g, lane] += 1.0
    for g in range(4):
        out[80 + g, 96 + 3 * g] = 1.0
    return out


def tiles(v):
    return v[0:8] + v[8:16]


def pair_kernel(k_ref, label_ref, select_ref, out_ref, acc_ref):
    row = lax.broadcasted_iota(jnp.int32, (24, 128), 0)
    lane = lax.broadcasted_iota(jnp.int32, (24, 128), 1)

    def plane(x, accs, inner):
        here, label = k_ref[x], label_ref[x]
        faces, diagonal = coefficients(k_ref[x - 1], here, k_ref[x + 1])
        y_label = jnp.where(row == 15, 0.0, pltpu.roll(label, 23, axis=0))[0:16]
        z_label = jnp.where(lane == 127, 0.0, pltpu.roll(label, 127, axis=1))[0:16]
        own = label[0:16]
        quarter, coupling = 0.25 * here[0:16], (diagonal - 0.5 * here)[0:16]
        masks = [own == g + 1 for g in range(NREG)]
        out = list(accs)
        for h in range(NREG):
            v = jnp.where(y_label == h + 1, faces[2][0:16], 0.0) + jnp.where(z_label == h + 1, faces[4][0:16], 0.0)
            if inner:
                v = v + jnp.where(label_ref[x + 1, 0:16] == h + 1, faces[0][0:16], 0.0)
            for g in range(NREG):
                out[4 * g + h] = out[4 * g + h] + tiles(jnp.where(masks[g], v, 0.0))
        for g in range(NREG):
            out[16 + g] = out[16 + g] + tiles(jnp.where(masks[g], quarter, 0.0))
            out[20 + g] = out[20 + g] + tiles(jnp.where(masks[g], coupling, 0.0))
        return tuple(out)

    zero = jnp.zeros((8, 128), F32)
    accs = lax.fori_loop(3, 18, lambda x, a: plane(x, a, True), (zero,) * 24)
    accs = plane(18, accs, False)
    for i in range(16):
        acc_ref[i] = accs[i]
    for i in range(8):
        acc_ref[80 + i] = accs[16 + i]
    own = pl.ds(3, 16)
    sides = (
        (k_ref[3, 0:16], label_ref[3, 0:16], k_ref[2, 0:16], label_ref[2, 0:16]),
        (k_ref[18, 0:16], label_ref[18, 0:16], k_ref[19, 0:16], label_ref[19, 0:16]),
        (k_ref[own, 0, :], label_ref[own, 0, :], k_ref[own, 23, :], label_ref[own, 23, :]),
        (k_ref[own, 15, :], label_ref[own, 15, :], k_ref[own, 16, :], label_ref[own, 16, :]),
    )
    for n, (k, label, other, other_label) in enumerate(sides):
        face = 0.5 * k + 0.5 * other
        for g in range(NREG):
            part = jnp.where(label == g + 1, face, 0.0)
            for h in range(NREG):
                acc_ref[16 * n + 16 + 4 * g + h] = tiles(jnp.where(other_label == h + 1, part, 0.0))
    sums = jnp.sum(jnp.sum(acc_ref[...], axis=1), axis=1, keepdims=True)
    for i in range(3):
        out_ref[i : i + 1] = jnp.sum(select_ref[:, 128 * i : 128 * i + 128] * sums, axis=0, keepdims=True)


def moment_kernel(k_ref, label_ref, inv_ref, w_ref, own_ref, out_ref, g_ref, acc_ref):
    def first_step(x, carry):
        inv = inv_ref[x]
        for c in range(3):
            g_ref[c, x - 2] = w_ref[c, x - 2] * inv
        return carry

    lax.fori_loop(2, 20, first_step, 0, unroll=2)

    def step(x, carry):
        here = k_ref[x + 2]
        faces, diagonal = coefficients(k_ref[x + 1], here, k_ref[x + 3])
        fields = [g_ref[c, x] for c in range(3)]
        image = operate(
            faces, diagonal, here, [g_ref[c, x - 1] for c in range(3)], fields, [g_ref[c, x + 1] for c in range(3)]
        )
        own = [v[0:16] for v in image]
        wg, gg = carry[12], carry[13]
        for c in range(3):
            g = fields[c][0:16]
            wg = wg + w_ref[c, x, 0:16] * g
            gg = gg + own[c] * g
        return (*add_regions(carry[:12], label_ref[x + 2, 0:16], own), wg, gg)

    zero = jnp.zeros((16, 128), F32)
    carry = lax.fori_loop(1, 17, step, (zero,) * 14)
    for i in range(12):
        acc_ref[i] = carry[i]
    lane = lax.broadcasted_iota(jnp.int32, (1, 128), 1)
    row = in_lanes(acc_ref, 0) + own_ref[...]
    out_ref[...] = jnp.where(lane == 24, total(carry[12]), jnp.where(lane == 25, total(carry[13]), row))


def group_kernel(recv_ref, out_ref):
    q = jnp.sum(recv_ref[:, 0:4, :], axis=0)
    own = recv_ref[:, 4, :]
    lane = lax.broadcasted_iota(jnp.int32, (16, 128), 1)
    shifted_rows = []
    for s in range(4):
        shifted_rows.append(
            jnp.concatenate([pltpu.roll(q[s : s + 1], (128 - 12 * y) % 128, axis=1) for y in range(8)], axis=0)
        )
    mine, below, above = (
        jnp.concatenate([shifted_rows[s], shifted_rows[s + 1]], axis=0) for s in (1, 0, 2)
    )

    def right(v, by):
        return pltpu.roll(v, by % 128, axis=1)

    def first(v):
        return jnp.where(lane < 12, v, 0.0)

    def four(v):
        v = first(v)
        v = v + right(v, 12)
        return v + right(v, 24)

    alone = first(mine)
    twice = alone + right(alone, 12)
    turned = alone
    for d in range(1, 4):
        turned = turned + right(first(right(twice, -3 * d)), 12 * d)
    turned = turned + right(turned, 48)
    three = mine + right(mine, -1) + right(mine, -2)
    products = (
        recv_ref[:, 5, :] * (turned * (four(mine) + right(four(below), 48)) + right(first(three * three), 96))
        + recv_ref[:, 6, :] * turned * (four(above) + right(four(right(mine, 12)), 48))
        + recv_ref[:, 7, :] * turned * four(right(mine, -12))
        + 2.0 * jnp.where(lane < 12, own * alone, 0.0)
        + jnp.where(lane == 25, own, 0.0)
    )
    pairing = jnp.where((lane >= 12) & (lane < 24), own * twice, jnp.where(lane == 24, own, 0.0))
    at = lax.broadcasted_iota(jnp.int32, (1, 128), 1)
    row = jnp.where(at == 0, total(pairing), jnp.where(at == 1, total(products), 0.0))
    for n in range(NROWS):
        out_ref[n] = row


def third_kernel(recv_ref, k_ref, label_ref, inv_ref, z_ref, w_ref, scal_ref, own_ref, image_ref, znew_ref, map_ref):
    q = jnp.sum(recv_ref[:, 0:4, :], axis=0)
    near = jnp.where(lax.axis_index("c") == 0, q[0:3], q[1:4])
    spread_maps(pltpu.roll(near, lax.rem(140 - 12 * lax.axis_index("y"), 128), axis=1), map_ref)
    scal_ref[...] = q[0:1]
    rz, zw = q[0:1, SLAB : SLAB + 1], q[0:1, SLAB + 1 : SLAB + 2]
    alpha = rz / zw

    def first_step(s):
        def body(x, carry):
            inv, label = inv_ref[x], label_ref[x]
            for c in range(3):
                y = w_ref[c, x - 2] * inv + spread(label, map_ref, s, c)
                znew_ref[c, x - 2] = z_ref[c, x] - alpha * y
            return carry

        return body

    first_step(0)(2, 0)
    lax.fori_loop(3, 19, first_step(1), 0, unroll=2)
    first_step(2)(19, 0)

    def second_step(x, carry):
        here = k_ref[x + 2]
        faces, diagonal = coefficients(k_ref[x + 1], here, k_ref[x + 3])
        fields = [znew_ref[c, x] for c in range(3)]
        image = operate(
            faces, diagonal, here, [znew_ref[c, x - 1] for c in range(3)], fields, [znew_ref[c, x + 1] for c in range(3)]
        )
        for c in range(3):
            own_ref[c, x - 1] = fields[c][0:16]
            image_ref[c, x - 1] = image[c][0:16]
        return carry

    lax.fori_loop(1, 17, second_step, 0)


def last_kernel(recv_ref, scal_ref, r_ref, z_ref, w_ref, znew_ref, image_ref, x_ref, res_ref):
    sums = jnp.sum(recv_ref[...], axis=0)
    wy, yay = sums[:, 0:1], sums[:, 1:2]
    scal = scal_ref[...]
    rz, zw = scal[:, SLAB : SLAB + 1], scal[:, SLAB + 1 : SLAB + 2]
    alpha = rz / zw
    new = rz + alpha * (alpha * wy - 2.0 * zw)
    zaz = zw + alpha * (alpha * yay - 2.0 * wy)
    cross = zw - alpha * wy
    ratio = new / rz
    second = new / (zaz + ratio * (2.0 * cross + ratio * zw))
    first = alpha + second * ratio

    def step(x, carry):
        for c in range(3):
            x_ref[c, x] = first * z_ref[c, x + 3, 0:16] + second * znew_ref[c, x]
            res_ref[c, x] = r_ref[c, x] - first * w_ref[c, x + 1, 0:16] - second * image_ref[c, x]
        return carry

    lax.fori_loop(0, 16, step, 0, unroll=2)


def exchange(array, axes):
    return lax.all_to_all(array, axes, 0, 0, tiled=True)


def swapped(array, axis, first):
    count = lax.axis_size(axis)
    pairs = [(i, i + 1) for i in range(first, count - 1, 2)]
    return lax.ppermute(array, axis, pairs + [(b, a) for a, b in pairs])


def local(right, occ, reg, coarse):
    field, plane = (16, 16, 128), (24, 128)
    send, one, two, r, k_own, label_own, coarse = call(
        first_kernel,
        (
            shape(NROWS, 4, 128),
            shape(3, 16, 4, 128),
            shape(3, 16, 4, 128),
            shape(3, *field),
            shape(*field),
            shape(*field),
            shape(12, 6144),
        ),
        tuple(pltpu.with_memory_space_constraint(a, pltpu.HBM) for a in (right, occ, reg, coarse)),
        (
            pltpu.VMEM(field, jnp.int32),
            pltpu.VMEM(field, jnp.int32),
            *FOLD_SCRATCH,
            pltpu.SemaphoreType.DMA((4,)),
        ),
        space=pl.BlockSpec(memory_space=pltpu.HBM),
        limit=24,
    )
    one = swapped(one, "y", 0)
    two = swapped(two, "y", 1)
    got = exchange(send, ROWS)
    first, second = call(
        pack_kernel, (shape(PACK, 128), shape(PACK, 128)), (k_own, label_own, r, one, two), cost=1000000
    )
    first = swapped(first, WIDE, 0)
    second = swapped(second, WIDE, 1)
    send = call(around_kernel, shape(NCOLS, 4, 128), (got,))
    got = exchange(send, COLS)
    k, label, inv, f = call(
        extend_kernel,
        (shape(22, *plane), shape(22, *plane), shape(22, *plane), shape(3, 22, *plane)),
        (r, k_own, label_own, one, two, first, second),
        cost=3000000,
    )
    pair = call(
        pair_kernel, shape(3, 128), (k, label, jnp.asarray(selection())), (pltpu.VMEM((88, 8, 128), F32),), cost=3000000
    )
    send, z, w, own = call(
        second_kernel,
        (shape(NROWS, 4, 128), shape(3, 22, *plane), shape(3, 18, *plane), shape(1, 128)),
        (got, r, k, label, f, coarse),
        (pltpu.VMEM((3, 12, *plane), F32), *FOLD_SCRATCH),
        alias={4: 1},
    )
    got = exchange(send, ROWS)
    own = call(
        moment_kernel,
        shape(1, 128),
        (k, label, inv, w, own),
        (pltpu.VMEM((3, 18, *plane), F32), pltpu.VMEM((12, 16, 128), F32)),
        cost=3000000,
    )
    send = call(pass_kernel, shape(NCOLS, 8, 128), (got, own, pair))
    got = exchange(send, COLS)
    send = call(group_kernel, shape(NROWS, 1, 128), (got,))
    scal, znew, image = call(
        third_kernel,
        (shape(1, 128), shape(3, *field), shape(3, *field)),
        (got, k, label, inv, z, w),
        (pltpu.VMEM((3, 18, *plane), F32), pltpu.VMEM((3, 12, *plane), F32)),
        cost=3000000,
    )
    got = exchange(send, ROWS)
    return call(
        last_kernel,
        (shape(3, *field), shape(3, *field)),
        (got, scal, right, z, w, znew, image),
    )


def solution(mesh):
    finer = Mesh(mesh.devices.reshape(4, 8, 2, 8), ("x", "z", "c", "y"))
    field = P(None, WIDE, "y", None)
    labels = P(WIDE, "y", None)
    return jax.shard_map(
        local,
        mesh=finer,
        in_specs=(field, labels, labels, P((*WIDE, "y"), None)),
        out_specs=(field, field),
        check_vma=False,
    )
```

```python
import jax
import jax.numpy as jnp
import numpy as np
from jax import lax
from jax.experimental import pallas as pl
from jax.experimental.pallas import tpu as pltpu
from jax.sharding import Mesh
from jax.sharding import PartitionSpec as P

WIDE = ("x", "z", "c")
ROWS = ("x", "z")
COLS = ("c", "y")
NROWS = 32
NCOLS = 16
F32 = jnp.float32
NREG = 4
SLAB = 96
VMEM = pl.BlockSpec(memory_space=pltpu.VMEM)


def shape(*dims):
    return jax.ShapeDtypeStruct(dims, F32)


def call(kernel, outs, ins, scratch=(), space=VMEM, cost=0, limit=24, alias=None):
    return pl.pallas_call(
        kernel,
        out_shape=outs,
        in_specs=[space] * len(ins),
        out_specs=jax.tree.map(lambda _: VMEM, outs),
        scratch_shapes=list(scratch),
        input_output_aliases=alias or {},
        cost_estimate=pl.CostEstimate(flops=cost, bytes_accessed=cost, transcendentals=0) if cost else None,
        compiler_params=pltpu.CompilerParams(vmem_limit_bytes=int(limit * 1024 * 1024)),
    )(*ins)


def total(v):
    return jnp.sum(jnp.sum(v, axis=0, keepdims=True), axis=1, keepdims=True)


def add_regions(accs, label, field):
    out = list(accs)
    for g in range(NREG):
        mask = label == g + 1
        for c in range(3):
            out[3 * g + c] = out[3 * g + c] + jnp.where(mask, field[c], 0.0)
    return out


def totals(acc_ref):
    return jnp.sum(jnp.sum(acc_ref[...], axis=1), axis=1, keepdims=True)


def in_lanes(column, at):
    row = lax.broadcasted_iota(jnp.int32, (12, 128), 0)
    lane = lax.broadcasted_iota(jnp.int32, (12, 128), 1)
    return jnp.sum(jnp.where(lane == row + at, column, 0.0), axis=0, keepdims=True)


def in_rows(lanes, at):
    row = lax.broadcasted_iota(jnp.int32, (12, 128), 0)
    lane = lax.broadcasted_iota(jnp.int32, (12, 128), 1)
    return jnp.sum(jnp.where(lane == row + at, lanes, 0.0), axis=1, keepdims=True)


def fold(rc, coarse_ref, u_ref, pad_ref, out_ref, sums=()):
    u_ref[...] = jnp.sum(coarse_ref[...] * rc, axis=0, keepdims=True)
    pad_ref[...] = jnp.zeros_like(pad_ref)
    for w in range(2 * NROWS):
        pad_ref[w + 1 : w + 2, 0:SLAB] = u_ref[0:1, SLAB * w : SLAB * (w + 1)]
    if sums:
        lane = lax.broadcasted_iota(jnp.int32, (1, 128), 1)
        row = jnp.zeros((1, 128), F32)
        for i, s in enumerate(sums):
            row = jnp.where(lane == SLAB + i, s, row)
        tail = jnp.broadcast_to(row, (4, 128))
    for n in range(NROWS):
        window = pad_ref[2 * n : 2 * n + 4, :]
        if sums:
            window = window + tail
        out_ref[n] = window


FOLD_SCRATCH = (
    pltpu.VMEM((1, 6144), F32),
    pltpu.VMEM((72, 128), F32),
)


def even_column():
    return lax.rem(lax.axis_index("y"), 2) == 0


def first_kernel(
    r_hbm, reg_hbm, coarse_hbm,
    out_ref, r_ref, label_ref, coarse_ref, rc_ref,
    reg_ref, acc_ref, u_ref, pad_ref, sems,
):
    pairs = ((r_hbm, r_ref), (reg_hbm, reg_ref), (coarse_hbm, coarse_ref))
    copies = [pltpu.make_async_copy(a, b, sems.at[i]) for i, (a, b) in enumerate(pairs)]
    for copy in copies:
        copy.start()
    for copy in copies[:2]:
        copy.wait()

    def step(x, accs):
        label = reg_ref[x].astype(F32) + 1.0
        label_ref[x] = label
        return tuple(add_regions(accs, label, [r_ref[c, x] for c in range(3)]))

    zero = jnp.zeros((16, 128), F32)
    accs = lax.fori_loop(0, 16, step, (zero,) * 12, unroll=16)
    for i in range(12):
        acc_ref[i] = accs[i]
    rc = totals(acc_ref)
    rc_ref[...] = jnp.broadcast_to(rc, (12, 128))
    copies[2].wait()
    fold(rc, coarse_ref, u_ref, pad_ref, out_ref)


def edge_kernel(occ_ref, label_ref, r_ref, k_ref, a_ref, b_ref):
    k_ref[...] = 0.1 + 0.9 * occ_ref[...].astype(F32)
    even = even_column()
    for ref, last in ((a_ref, even), (b_ref, jnp.logical_not(even))):
        ref[0] = jnp.where(last, k_ref[:, 12:16, :], k_ref[:, 0:4, :])
        for i, field in enumerate([label_ref] + [r_ref.at[c] for c in range(3)]):
            at = 2 * (i % 2)
            ref[1 + i // 2, :, at : at + 2] = jnp.where(last, field[:, 14:16, :], field[:, 0:2, :])


def tail_rows(a_ref, b_ref, i, planes):
    even = even_column()
    if i == 0:
        one, two = a_ref[0, planes], b_ref[0, planes]
        return jnp.concatenate([jnp.where(even, one, two), jnp.where(even, two, one)], axis=1)
    block, at = 1 + (i - 1) // 2, 2 * ((i - 1) % 2)
    one, two = a_ref[block, planes, at : at + 2], b_ref[block, planes, at : at + 2]
    none = jnp.zeros((one.shape[0], 4, 128), F32)
    return jnp.concatenate([jnp.where(even, one, two), none, jnp.where(even, two, one)], axis=1)


PACK = 72 + 4 * 40


def pack_kernel(k_ref, label_ref, r_ref, a_ref, b_ref, first_ref, second_ref):
    fields = [label_ref] + [r_ref.at[c] for c in range(3)]
    core = lax.axis_index("c")
    for ref, up in ((first_ref, core == 0), (second_ref, core == 1)):
        deep, near, next_ = jnp.where(up, 13, 0), jnp.where(up, 15, 0), jnp.where(up, 14, 1)
        tails = tail_rows(a_ref, b_ref, 0, pl.ds(deep, 3))
        for i in range(3):
            ref[24 * i : 24 * i + 16] = k_ref[deep + i]
            ref[24 * i + 16 : 24 * i + 24] = tails[i]
        for i, field in enumerate(fields):
            at = 72 + 40 * i
            ref[at : at + 16] = field[near]
            ref[at + 16 : at + 24] = tail_rows(a_ref, b_ref, 1 + i, pl.ds(near, 1))[0]
            ref[at + 24 : at + 40] = field[next_]


def extend_kernel(
    r_ref, k_own_ref, label_own_ref, a_ref, b_ref, first_ref, second_ref, k_ref, label_ref, inv_ref, f_ref
):
    whole = pl.ds(0, 16)
    core = lax.axis_index("c")

    def sides(rows):
        one, two = first_ref[rows], second_ref[rows]
        return jnp.where(core == 0, two, one), jnp.where(core == 0, one, two)

    k_ref[3:19, 0:16] = k_own_ref[...]
    label_ref[3:19, 0:16] = label_own_ref[...]
    k_ref[3:19, 16:24] = tail_rows(a_ref, b_ref, 0, whole)
    label_ref[3:19, 16:24] = tail_rows(a_ref, b_ref, 1, whole)
    none = jnp.zeros((8, 128), F32)
    for i in range(3):
        below, above = sides(slice(24 * i, 24 * i + 24))
        k_ref[i] = below
        k_ref[19 + i] = above
    targets = [label_ref] + [f_ref.at[c] for c in range(3)]
    for i, ref in enumerate(targets):
        at = 72 + 40 * i
        ref[2], ref[19] = sides(slice(at, at + 24))
        ref[1, 0:16], ref[20, 0:16] = sides(slice(at + 24, at + 40))
        ref[1, 16:24] = ref[20, 16:24] = none
    for c in range(3):
        f_ref[c, 3:19, 0:16] = r_ref[c]
        f_ref[c, 3:19, 16:24] = tail_rows(a_ref, b_ref, 2 + c, whole)

    def step(x, carry):
        here = k_ref[x]
        _, diagonal = coefficients(k_ref[x - 1], here, k_ref[x + 1])
        inside = here > 0.0
        inv = jnp.where(inside, 1.0 / jnp.where(inside, diagonal, 1.0), 0.0)
        inv_ref[x] = inv
        for c in range(3):
            f_ref[c, x] = f_ref[c, x] * inv
        return carry

    lax.fori_loop(1, 21, step, 0, unroll=20)


def around_kernel(recv_ref, out_ref):
    part = jnp.sum(recv_ref[...], axis=0)
    for n in range(NCOLS):
        out_ref[n] = part


def pass_kernel(recv_ref, own_ref, pair_ref, out_ref):
    part = jnp.sum(recv_ref[...], axis=0)
    rows = jnp.concatenate([part, own_ref[...], pair_ref[...]], axis=0)
    for n in range(NCOLS):
        out_ref[n] = rows


def around(q):
    near = jnp.where(lax.axis_index("c") == 0, q[0:3], q[1:4])
    return pltpu.roll(near, lax.rem(140 - 12 * lax.axis_index("y"), 128), axis=1)


def iotas():
    lane = lax.broadcasted_iota(jnp.int32, (24, 128), 1)
    return lane == 0, lane == 127


def coefficients(before, here, after):
    first, last = iotas()
    y_up = pltpu.roll(here, 23, axis=0)
    y_down = pltpu.roll(here, 1, axis=0)
    z_up = jnp.where(last, 0.0, pltpu.roll(here, 127, axis=1))
    z_down = jnp.where(first, 0.0, pltpu.roll(here, 1, axis=1))
    half = 0.5 * here
    faces = [half + 0.5 * other for other in (after, before, y_up, y_down, z_up, z_down)]
    diagonal = faces[0] + faces[1] + faces[2] + faces[3] + faces[4] + faces[5] + half
    faces[4] = jnp.where(last, 0.0, faces[4])
    faces[5] = jnp.where(first, 0.0, faces[5])
    return faces, diagonal


def operate(faces, diagonal, here, befores, fields, afters):
    quarter = 0.25 * here
    main = diagonal - quarter
    shared = quarter * (fields[0] + fields[1] + fields[2])
    out = []
    for c in range(3):
        u = fields[c]
        out.append(
            main * u
            + shared
            - faces[0] * afters[c]
            - faces[1] * befores[c]
            - faces[2] * pltpu.roll(u, 23, axis=0)
            - faces[3] * pltpu.roll(u, 1, axis=0)
            - faces[4] * pltpu.roll(u, 127, axis=1)
            - faces[5] * pltpu.roll(u, 1, axis=1)
        )
    return out


def spread_maps(q, map_ref):
    row = lax.broadcasted_iota(jnp.int32, (24, 128), 0)
    for s in range(3):
        for i in range(12):
            below, own, above = (q[s : s + 1, 12 * d + i : 12 * d + i + 1] for d in range(3))
            map_ref[s, i] = jnp.where(row < 16, own, jnp.where(row < 20, above, below))


def spread(label, map_ref, s, c):
    out = jnp.zeros((24, 128), F32)
    for g in range(NREG):
        out = jnp.where(label == g + 1, map_ref[s, 3 * g + c], out)
    return out


def image_of(k_ref, x, field_ref, at):
    here = k_ref[x]
    faces, diagonal = coefficients(k_ref[x - 1], here, k_ref[x + 1])
    planes = [[field_ref[c, i] for c in range(3)] for i in (at - 1, at, at + 1)]
    return planes[1], operate(faces, diagonal, here, *planes)


def start_kernel(k_ref, label_ref, f_ref, r_ref, out_ref, acc_ref):
    def step(x, carry):
        fields, image = image_of(k_ref, x, f_ref, x)
        own = [v[0:16] for v in image]
        rf, faf = carry[12], carry[13]
        for c in range(3):
            f = fields[c][0:16]
            rf = rf + r_ref[c, x - 3] * f
            faf = faf + f * own[c]
        return (*add_regions(carry[:12], label_ref[x, 0:16], own), rf, faf)

    zero = jnp.zeros((16, 128), F32)
    carry = lax.fori_loop(3, 19, step, (zero,) * 14, unroll=16)
    for i in range(14):
        acc_ref[i] = carry[i]
    out_ref[...] = jnp.broadcast_to(totals(acc_ref), (14, 128))


def second_kernel(recv_ref, rc_ref, start_ref, rows_ref, coarse_ref, out_ref, own_ref, near_ref, u_ref, pad_ref):
    near = around(jnp.sum(recv_ref[...], axis=0))
    near_ref[...] = near
    product = rows_ref[0] * near[0:1] + rows_ref[1] * near[1:2] + rows_ref[2] * near[2:3]
    e = start_ref[0:12, 0:1]
    aggregates = e + jnp.sum(product, axis=1, keepdims=True)
    q = in_rows(near[1:2], 12)
    rz = start_ref[12:13, 0:1] + jnp.sum(rc_ref[:, 0:1] * q, axis=0, keepdims=True)
    zw = start_ref[13:14, 0:1] + jnp.sum(q * (e + aggregates), axis=0, keepdims=True)
    fold(aggregates, coarse_ref, u_ref, pad_ref, out_ref, (rz, zw))
    own_ref[...] = in_lanes(aggregates, 12)


def selection():
    out = np.zeros((88, 3 * 128), np.float32)
    for n in range(5):
        for d in range(4):
            for h in range(4):
                g = (h + d) % 4
                for c in range(3):
                    lane = 128 * (n // 2) + 48 * (n % 2) + 12 * d + 3 * h + c
                    out[16 * n + 4 * g + h, lane] -= 1.0
                    if n == 0:
                        out[4 * h + g, lane] -= 1.0
                        if d == 0:
                            out[80 + g, lane] += 1.0
                            out[84 + g, lane] += 1.0
    for g in range(4):
        out[80 + g, 96 + 3 * g] = 1.0
    return out


def tiles(v):
    return v[0:8] + v[8:16]


def pair_kernel(k_ref, label_ref, select_ref, out_ref, rows_ref, acc_ref, sum_ref):
    row = lax.broadcasted_iota(jnp.int32, (24, 128), 0)
    lane = lax.broadcasted_iota(jnp.int32, (24, 128), 1)

    def plane(x, accs, inner):
        here, label = k_ref[x], label_ref[x]
        faces, diagonal = coefficients(k_ref[x - 1], here, k_ref[x + 1])
        y_label = jnp.where(row == 15, 0.0, pltpu.roll(label, 23, axis=0))[0:16]
        z_label = jnp.where(lane == 127, 0.0, pltpu.roll(label, 127, axis=1))[0:16]
        own = label[0:16]
        quarter, coupling = 0.25 * here[0:16], (diagonal - 0.5 * here)[0:16]
        masks = [own == g + 1 for g in range(NREG)]
        out = list(accs)
        for h in range(NREG):
            v = jnp.where(y_label == h + 1, faces[2][0:16], 0.0) + jnp.where(z_label == h + 1, faces[4][0:16], 0.0)
            if inner:
                v = v + jnp.where(label_ref[x + 1, 0:16] == h + 1, faces[0][0:16], 0.0)
            for g in range(NREG):
                out[4 * g + h] = out[4 * g + h] + tiles(jnp.where(masks[g], v, 0.0))
        for g in range(NREG):
            out[16 + g] = out[16 + g] + tiles(jnp.where(masks[g], quarter, 0.0))
            out[20 + g] = out[20 + g] + tiles(jnp.where(masks[g], coupling, 0.0))
        return tuple(out)

    zero = jnp.zeros((8, 128), F32)
    accs = lax.fori_loop(3, 18, lambda x, a: plane(x, a, True), (zero,) * 24, unroll=15)
    accs = plane(18, accs, False)
    for i in range(16):
        acc_ref[i] = accs[i]
    for i in range(8):
        acc_ref[80 + i] = accs[16 + i]
    own = pl.ds(3, 16)
    sides = (
        (k_ref[3, 0:16], label_ref[3, 0:16], k_ref[2, 0:16], label_ref[2, 0:16]),
        (k_ref[18, 0:16], label_ref[18, 0:16], k_ref[19, 0:16], label_ref[19, 0:16]),
        (k_ref[own, 0, :], label_ref[own, 0, :], k_ref[own, 23, :], label_ref[own, 23, :]),
        (k_ref[own, 15, :], label_ref[own, 15, :], k_ref[own, 16, :], label_ref[own, 16, :]),
    )
    for n, (k, label, other, other_label) in enumerate(sides):
        face = 0.5 * k + 0.5 * other
        for g in range(NREG):
            part = jnp.where(label == g + 1, face, 0.0)
            for h in range(NREG):
                acc_ref[16 * n + 16 + 4 * g + h] = tiles(jnp.where(other_label == h + 1, part, 0.0))
    sums = jnp.sum(jnp.sum(acc_ref[...], axis=1), axis=1, keepdims=True)
    for i in range(3):
        out_ref[i : i + 1] = jnp.sum(select_ref[:, 128 * i : 128 * i + 128] * sums, axis=0, keepdims=True)
    sum_ref[...] = jnp.broadcast_to(sums, (88, 128))
    row = lax.broadcasted_iota(jnp.int32, (12, 128), 0)
    lane = lax.broadcasted_iota(jnp.int32, (12, 128), 1)
    first = 3 * ((row >= 3).astype(jnp.int32) + (row >= 6).astype(jnp.int32) + (row >= 9).astype(jnp.int32))
    component = row - first

    def column(indices):
        return jnp.concatenate([jnp.broadcast_to(sum_ref[i : i + 1], (3, 128)) for i in indices], axis=0)

    def block(n, at):
        out = jnp.zeros((12, 128), F32)
        for h in range(NREG):
            value = column([16 * n + 4 * g + h for g in range(NREG)])
            if n == 0:
                value = value + column([4 * h + g for g in range(NREG)])
            out = out - jnp.where(lane == at + 3 * h + component, value, 0.0)
        return out

    quarter, coupling = column(range(80, 84)), column(range(84, 88))
    rows_ref[0] = block(1, 12)
    rows_ref[1] = (
        block(0, 12)
        + block(3, 0)
        + block(4, 24)
        + jnp.where(lane == 12 + row, quarter + coupling, 0.0)
        + jnp.where((lane >= 12 + first) & (lane < 15 + first), quarter, 0.0)
    )
    rows_ref[2] = block(2, 12)


def moment_kernel(
    near_ref, k_ref, label_ref, inv_ref, f_ref, own_ref, z_ref, w_ref, out_ref, g_ref, acc_ref, map_ref
):
    spread_maps(near_ref[...], map_ref)

    def first_step(s):
        def body(x, carry):
            label = label_ref[x]
            for c in range(3):
                z_ref[c, x] = f_ref[c, x] + spread(label, map_ref, s, c)
            return carry

        return body

    lax.fori_loop(1, 3, first_step(0), 0)
    lax.fori_loop(3, 19, first_step(1), 0, unroll=16)
    lax.fori_loop(19, 21, first_step(2), 0)

    def second_step(x, carry):
        _, w = image_of(k_ref, x, z_ref, x)
        inv = inv_ref[x]
        for c in range(3):
            w_ref[c, x - 2] = w[c]
            g_ref[c, x - 2] = w[c] * inv
        return carry

    lax.fori_loop(2, 20, second_step, 0, unroll=18)

    def step(x, carry):
        fields, image = image_of(k_ref, x + 2, g_ref, x)
        own = [v[0:16] for v in image]
        wg, gg = carry[12], carry[13]
        for c in range(3):
            g = fields[c][0:16]
            wg = wg + w_ref[c, x, 0:16] * g
            gg = gg + own[c] * g
        return (*add_regions(carry[:12], label_ref[x + 2, 0:16], own), wg, gg)

    zero = jnp.zeros((16, 128), F32)
    carry = lax.fori_loop(1, 17, step, (zero,) * 14, unroll=16)
    for i in range(12):
        acc_ref[i] = carry[i]
    lane = lax.broadcasted_iota(jnp.int32, (1, 128), 1)
    row = in_lanes(totals(acc_ref), 0) + own_ref[...]
    out_ref[...] = jnp.where(lane == 24, total(carry[12]), jnp.where(lane == 25, total(carry[13]), row))


def group_kernel(recv_ref, out_ref):
    q = jnp.sum(recv_ref[:, 0:4, :], axis=0)
    own = recv_ref[:, 4, :]
    lane = lax.broadcasted_iota(jnp.int32, (16, 128), 1)
    shifted_rows = []
    for s in range(4):
        shifted_rows.append(
            jnp.concatenate([pltpu.roll(q[s : s + 1], (128 - 12 * y) % 128, axis=1) for y in range(8)], axis=0)
        )
    mine, below, above = (
        jnp.concatenate([shifted_rows[s], shifted_rows[s + 1]], axis=0) for s in (1, 0, 2)
    )

    def right(v, by):
        return pltpu.roll(v, by % 128, axis=1)

    def first(v):
        return jnp.where(lane < 12, v, 0.0)

    def four(v):
        v = first(v)
        v = v + right(v, 12)
        return v + right(v, 24)

    alone = first(mine)
    twice = alone + right(alone, 12)
    turned = alone
    for d in range(1, 4):
        turned = turned + right(first(right(twice, -3 * d)), 12 * d)
    turned = turned + right(turned, 48)
    three = mine + right(mine, -1) + right(mine, -2)
    products = (
        recv_ref[:, 5, :] * (turned * (four(mine) + right(four(below), 48)) + right(first(three * three), 96))
        + recv_ref[:, 6, :] * turned * (four(above) + right(four(right(mine, 12)), 48))
        + recv_ref[:, 7, :] * turned * four(right(mine, -12))
        + 2.0 * jnp.where(lane < 12, own * alone, 0.0)
        + jnp.where(lane == 25, own, 0.0)
    )
    pairing = jnp.where((lane >= 12) & (lane < 24), own * twice, jnp.where(lane == 24, own, 0.0))
    at = lax.broadcasted_iota(jnp.int32, (1, 128), 1)
    row = jnp.where(at == 0, total(pairing), jnp.where(at == 1, total(products), 0.0))
    for n in range(NROWS):
        out_ref[n] = row


def third_kernel(recv_ref, k_ref, label_ref, inv_ref, z_ref, w_ref, scal_ref, own_ref, image_ref, znew_ref, map_ref):
    q = jnp.sum(recv_ref[:, 0:4, :], axis=0)
    spread_maps(around(q), map_ref)
    scal_ref[...] = q[0:1]
    rz, zw = q[0:1, SLAB : SLAB + 1], q[0:1, SLAB + 1 : SLAB + 2]
    alpha = rz / zw

    def first_step(s):
        def body(x, carry):
            inv, label = inv_ref[x], label_ref[x]
            for c in range(3):
                y = w_ref[c, x - 2] * inv + spread(label, map_ref, s, c)
                znew_ref[c, x - 2] = z_ref[c, x] - alpha * y
            return carry

        return body

    first_step(0)(2, 0)
    lax.fori_loop(3, 19, first_step(1), 0, unroll=16)
    first_step(2)(19, 0)

    def second_step(x, carry):
        here = k_ref[x + 2]
        faces, diagonal = coefficients(k_ref[x + 1], here, k_ref[x + 3])
        fields = [znew_ref[c, x] for c in range(3)]
        image = operate(
            faces, diagonal, here, [znew_ref[c, x - 1] for c in range(3)], fields, [znew_ref[c, x + 1] for c in range(3)]
        )
        for c in range(3):
            own_ref[c, x - 1] = fields[c][0:16]
            image_ref[c, x - 1] = image[c][0:16]
        return carry

    lax.fori_loop(1, 17, second_step, 0, unroll=16)


def last_kernel(recv_ref, scal_ref, r_ref, z_ref, w_ref, znew_ref, image_ref, x_ref, res_ref):
    sums = jnp.sum(recv_ref[...], axis=0)
    wy, yay = sums[:, 0:1], sums[:, 1:2]
    scal = scal_ref[...]
    rz, zw = scal[:, SLAB : SLAB + 1], scal[:, SLAB + 1 : SLAB + 2]
    alpha = rz / zw
    new = rz + alpha * (alpha * wy - 2.0 * zw)
    zaz = zw + alpha * (alpha * yay - 2.0 * wy)
    cross = zw - alpha * wy
    ratio = new / rz
    second = new / (zaz + ratio * (2.0 * cross + ratio * zw))
    first = alpha + second * ratio

    def step(x, carry):
        for c in range(3):
            x_ref[c, x] = first * z_ref[c, x + 3, 0:16] + second * znew_ref[c, x]
            res_ref[c, x] = r_ref[c, x] - first * w_ref[c, x + 1, 0:16] - second * image_ref[c, x]
        return carry

    lax.fori_loop(0, 16, step, 0, unroll=2)


def exchange(array, axes):
    return lax.all_to_all(array, axes, 0, 0, tiled=True)


def swapped(array, axis, first):
    count = lax.axis_size(axis)
    pairs = [(i, i + 1) for i in range(first, count - 1, 2)]
    return lax.ppermute(array, axis, pairs + [(b, a) for a, b in pairs])


def local(right, occ, reg, coarse):
    field, plane = (16, 16, 128), (24, 128)
    send, r, label_own, coarse, rc = call(
        first_kernel,
        (shape(NROWS, 4, 128), shape(3, *field), shape(*field), shape(12, 6144), shape(12, 128)),
        tuple(pltpu.with_memory_space_constraint(a, pltpu.HBM) for a in (right, reg, coarse)),
        (
            pltpu.VMEM(field, jnp.int32),
            pltpu.VMEM((12, 16, 128), F32),
            *FOLD_SCRATCH,
            pltpu.SemaphoreType.DMA((3,)),
        ),
        space=pl.BlockSpec(memory_space=pltpu.HBM),
    )
    k_own, one, two = call(
        edge_kernel,
        (shape(*field), shape(3, 16, 4, 128), shape(3, 16, 4, 128)),
        (occ, label_own, r),
        cost=3000000,
    )
    one = swapped(one, "y", 0)
    two = swapped(two, "y", 1)
    got = exchange(send, ROWS)
    first, second = call(
        pack_kernel, (shape(PACK, 128), shape(PACK, 128)), (k_own, label_own, r, one, two), cost=1000000
    )
    first = swapped(first, WIDE, 0)
    second = swapped(second, WIDE, 1)
    send = call(around_kernel, shape(NCOLS, 4, 128), (got,))
    got = exchange(send, COLS)
    k, label, inv, f = call(
        extend_kernel,
        (shape(22, *plane), shape(22, *plane), shape(22, *plane), shape(3, 22, *plane)),
        (r, k_own, label_own, one, two, first, second),
        cost=3000000,
    )
    start = call(start_kernel, shape(14, 128), (k, label, f, r), (pltpu.VMEM((14, 16, 128), F32),), cost=3000000)
    pair, rows = call(
        pair_kernel,
        (shape(3, 128), shape(3, 12, 128)),
        (k, label, jnp.asarray(selection())),
        (pltpu.VMEM((88, 8, 128), F32), pltpu.VMEM((88, 128), F32)),
        cost=3000000,
    )
    send, own, near = call(
        second_kernel,
        (shape(NROWS, 4, 128), shape(1, 128), shape(3, 128)),
        (got, rc, start, rows, coarse),
        FOLD_SCRATCH,
    )
    got = exchange(send, ROWS)
    z, w, own = call(
        moment_kernel,
        (shape(3, 22, *plane), shape(3, 18, *plane), shape(1, 128)),
        (near, k, label, inv, f, own),
        (pltpu.VMEM((3, 18, *plane), F32), pltpu.VMEM((12, 16, 128), F32), pltpu.VMEM((3, 12, *plane), F32)),
        cost=3000000,
        alias={4: 0},
    )
    send = call(pass_kernel, shape(NCOLS, 8, 128), (got, own, pair))
    got = exchange(send, COLS)
    send = call(group_kernel, shape(NROWS, 1, 128), (got,))
    scal, znew, image = call(
        third_kernel,
        (shape(1, 128), shape(3, *field), shape(3, *field)),
        (got, k, label, inv, z, w),
        (pltpu.VMEM((3, 18, *plane), F32), pltpu.VMEM((3, 12, *plane), F32)),
        cost=3000000,
    )
    got = exchange(send, ROWS)
    return call(
        last_kernel,
        (shape(3, *field), shape(3, *field)),
        (got, scal, right, z, w, znew, image),
    )


def solution(mesh):
    finer = Mesh(mesh.devices.reshape(4, 8, 2, 8), ("x", "z", "c", "y"))
    field = P(None, WIDE, "y", None)
    labels = P(WIDE, "y", None)
    return jax.shard_map(
        local,
        mesh=finer,
        in_specs=(field, labels, labels, P((*WIDE, "y"), None)),
        out_specs=(field, field),
        check_vma=False,
    )
```

```python
import jax
import jax.numpy as jnp
import numpy as np
from jax import lax
from jax.experimental import pallas as pl
from jax.experimental.pallas import tpu as pltpu
from jax.sharding import Mesh
from jax.sharding import PartitionSpec as P

WIDE = ("x", "z", "c")
ROWS = ("x", "z")
COLS = ("c", "y")
NROWS = 32
NCOLS = 16
F32 = jnp.float32
NREG = 4
SLAB = 96
VMEM = pl.BlockSpec(memory_space=pltpu.VMEM)
HBM = pl.BlockSpec(memory_space=pltpu.HBM)
PARTS = 4


def shape(*dims):
    return jax.ShapeDtypeStruct(dims, F32)


def call(kernel, outs, ins, scratch=(), space=VMEM, target=VMEM, cost=0, limit=24, alias=None):
    return pl.pallas_call(
        kernel,
        out_shape=outs,
        in_specs=[space] * len(ins),
        out_specs=jax.tree.map(lambda _: target, outs),
        scratch_shapes=list(scratch),
        input_output_aliases=alias or {},
        cost_estimate=pl.CostEstimate(flops=cost, bytes_accessed=cost, transcendentals=0) if cost else None,
        compiler_params=pltpu.CompilerParams(vmem_limit_bytes=int(limit * 1024 * 1024)),
    )(*ins)


def total(v):
    return jnp.sum(jnp.sum(v, axis=0, keepdims=True), axis=1, keepdims=True)


def add_regions(accs, label, field):
    out = list(accs)
    for g in range(NREG):
        mask = label == g + 1
        for c in range(3):
            out[3 * g + c] = out[3 * g + c] + jnp.where(mask, field[c], 0.0)
    return out


def totals(acc_ref):
    return jnp.sum(jnp.sum(acc_ref[...], axis=1), axis=1, keepdims=True)


def in_lanes(column, at):
    row = lax.broadcasted_iota(jnp.int32, (12, 128), 0)
    lane = lax.broadcasted_iota(jnp.int32, (12, 128), 1)
    return jnp.sum(jnp.where(lane == row + at, column, 0.0), axis=0, keepdims=True)


def in_rows(lanes, at):
    row = lax.broadcasted_iota(jnp.int32, (12, 128), 0)
    lane = lax.broadcasted_iota(jnp.int32, (12, 128), 1)
    return jnp.sum(jnp.where(lane == row + at, lanes, 0.0), axis=1, keepdims=True)


def fold(rc, coarse_ref, u_ref, pad_ref, out_ref, sums=()):
    u_ref[...] = jnp.sum(coarse_ref[...] * rc, axis=0, keepdims=True)
    pad_ref[...] = jnp.zeros_like(pad_ref)
    for w in range(2 * NROWS):
        pad_ref[w + 1 : w + 2, 0:SLAB] = u_ref[0:1, SLAB * w : SLAB * (w + 1)]
    if sums:
        lane = lax.broadcasted_iota(jnp.int32, (1, 128), 1)
        row = jnp.zeros((1, 128), F32)
        for i, s in enumerate(sums):
            row = jnp.where(lane == SLAB + i, s, row)
        tail = jnp.broadcast_to(row, (4, 128))
    for n in range(NROWS):
        window = pad_ref[2 * n : 2 * n + 4, :]
        if sums:
            window = window + tail
        out_ref[n] = window


FOLD_SCRATCH = (
    pltpu.VMEM((1, 6144), F32),
    pltpu.VMEM((72, 128), F32),
)


def even_column():
    return lax.rem(lax.axis_index("y"), 2) == 0


def first_kernel(
    r_hbm, reg_hbm, coarse_hbm,
    out_ref, r_ref, label_ref, coarse_ref, rc_ref,
    reg_ref, acc_ref, u_ref, pad_ref, sems,
):
    pairs = ((r_hbm, r_ref), (reg_hbm, reg_ref), (coarse_hbm, coarse_ref))
    copies = [pltpu.make_async_copy(a, b, sems.at[i]) for i, (a, b) in enumerate(pairs)]
    for copy in copies:
        copy.start()
    for copy in copies[:2]:
        copy.wait()

    def step(x, accs):
        label = reg_ref[x].astype(F32) + 1.0
        label_ref[x] = label
        return tuple(add_regions(accs, label, [r_ref[c, x] for c in range(3)]))

    zero = jnp.zeros((16, 128), F32)
    accs = lax.fori_loop(0, 16, step, (zero,) * 12, unroll=16)
    for i in range(12):
        acc_ref[i] = accs[i]
    rc = totals(acc_ref)
    rc_ref[...] = jnp.broadcast_to(rc, (12, 128))
    copies[2].wait()
    fold(rc, coarse_ref, u_ref, pad_ref, out_ref)


def edge_kernel(occ_ref, label_ref, r_ref, k_ref, a_ref, b_ref):
    k_ref[...] = 0.1 + 0.9 * occ_ref[...].astype(F32)
    even = even_column()
    for ref, last in ((a_ref, even), (b_ref, jnp.logical_not(even))):
        ref[0] = jnp.where(last, k_ref[:, 12:16, :], k_ref[:, 0:4, :])
        for i, field in enumerate([label_ref] + [r_ref.at[c] for c in range(3)]):
            at = 2 * (i % 2)
            ref[1 + i // 2, :, at : at + 2] = jnp.where(last, field[:, 14:16, :], field[:, 0:2, :])


def tail_rows(a_ref, b_ref, i, planes):
    even = even_column()
    if i == 0:
        one, two = a_ref[0, planes], b_ref[0, planes]
        return jnp.concatenate([jnp.where(even, one, two), jnp.where(even, two, one)], axis=1)
    block, at = 1 + (i - 1) // 2, 2 * ((i - 1) % 2)
    one, two = a_ref[block, planes, at : at + 2], b_ref[block, planes, at : at + 2]
    none = jnp.zeros((one.shape[0], 4, 128), F32)
    return jnp.concatenate([jnp.where(even, one, two), none, jnp.where(even, two, one)], axis=1)


PACK = 72 + 4 * 40


def pack_kernel(k_ref, label_ref, r_ref, a_ref, b_ref, first_ref, second_ref):
    fields = [label_ref] + [r_ref.at[c] for c in range(3)]
    core = lax.axis_index("c")
    for ref, up in ((first_ref, core == 0), (second_ref, core == 1)):
        deep, near, next_ = jnp.where(up, 13, 0), jnp.where(up, 15, 0), jnp.where(up, 14, 1)
        tails = tail_rows(a_ref, b_ref, 0, pl.ds(deep, 3))
        for i in range(3):
            ref[24 * i : 24 * i + 16] = k_ref[deep + i]
            ref[24 * i + 16 : 24 * i + 24] = tails[i]
        for i, field in enumerate(fields):
            at = 72 + 40 * i
            ref[at : at + 16] = field[near]
            ref[at + 16 : at + 24] = tail_rows(a_ref, b_ref, 1 + i, pl.ds(near, 1))[0]
            ref[at + 24 : at + 40] = field[next_]


def extend_kernel(
    r_ref, k_own_ref, label_own_ref, a_ref, b_ref, first_ref, second_ref, k_ref, label_ref, inv_ref, f_ref
):
    whole = pl.ds(0, 16)
    core = lax.axis_index("c")

    def sides(rows):
        one, two = first_ref[rows], second_ref[rows]
        return jnp.where(core == 0, two, one), jnp.where(core == 0, one, two)

    k_ref[3:19, 0:16] = k_own_ref[...]
    label_ref[3:19, 0:16] = label_own_ref[...]
    k_ref[3:19, 16:24] = tail_rows(a_ref, b_ref, 0, whole)
    label_ref[3:19, 16:24] = tail_rows(a_ref, b_ref, 1, whole)
    none = jnp.zeros((8, 128), F32)
    for i in range(3):
        below, above = sides(slice(24 * i, 24 * i + 24))
        k_ref[i] = below
        k_ref[19 + i] = above
    targets = [label_ref] + [f_ref.at[c] for c in range(3)]
    for i, ref in enumerate(targets):
        at = 72 + 40 * i
        ref[2], ref[19] = sides(slice(at, at + 24))
        ref[1, 0:16], ref[20, 0:16] = sides(slice(at + 24, at + 40))
        ref[1, 16:24] = ref[20, 16:24] = none
    for c in range(3):
        f_ref[c, 3:19, 0:16] = r_ref[c]
        f_ref[c, 3:19, 16:24] = tail_rows(a_ref, b_ref, 2 + c, whole)

    def step(x, carry):
        here = k_ref[x]
        _, diagonal = coefficients(k_ref[x - 1], here, k_ref[x + 1])
        inside = here > 0.0
        inv = jnp.where(inside, 1.0 / jnp.where(inside, diagonal, 1.0), 0.0)
        inv_ref[x] = inv
        for c in range(3):
            f_ref[c, x] = f_ref[c, x] * inv
        return carry

    lax.fori_loop(1, 21, step, 0, unroll=20)


def around_kernel(recv_ref, out_ref):
    part = jnp.sum(recv_ref[...], axis=0)
    for n in range(NCOLS):
        out_ref[n] = part


def pass_kernel(recv_ref, own_ref, pair_ref, out_ref):
    part = jnp.sum(recv_ref[...], axis=0)
    rows = jnp.concatenate([part, own_ref[...], pair_ref[...]], axis=0)
    for n in range(NCOLS):
        out_ref[n] = rows


def around(q):
    near = jnp.where(lax.axis_index("c") == 0, q[0:3], q[1:4])
    return pltpu.roll(near, lax.rem(140 - 12 * lax.axis_index("y"), 128), axis=1)


def iotas():
    lane = lax.broadcasted_iota(jnp.int32, (24, 128), 1)
    return lane == 0, lane == 127


def coefficients(before, here, after):
    first, last = iotas()
    y_up = pltpu.roll(here, 23, axis=0)
    y_down = pltpu.roll(here, 1, axis=0)
    z_up = jnp.where(last, 0.0, pltpu.roll(here, 127, axis=1))
    z_down = jnp.where(first, 0.0, pltpu.roll(here, 1, axis=1))
    half = 0.5 * here
    faces = [half + 0.5 * other for other in (after, before, y_up, y_down, z_up, z_down)]
    diagonal = faces[0] + faces[1] + faces[2] + faces[3] + faces[4] + faces[5] + half
    faces[4] = jnp.where(last, 0.0, faces[4])
    faces[5] = jnp.where(first, 0.0, faces[5])
    return faces, diagonal


def operate(faces, diagonal, here, befores, fields, afters):
    quarter = 0.25 * here
    main = diagonal - quarter
    shared = quarter * (fields[0] + fields[1] + fields[2])
    out = []
    for c in range(3):
        u = fields[c]
        out.append(
            main * u
            + shared
            - faces[0] * afters[c]
            - faces[1] * befores[c]
            - faces[2] * pltpu.roll(u, 23, axis=0)
            - faces[3] * pltpu.roll(u, 1, axis=0)
            - faces[4] * pltpu.roll(u, 127, axis=1)
            - faces[5] * pltpu.roll(u, 1, axis=1)
        )
    return out


def spread_maps(q, map_ref):
    row = lax.broadcasted_iota(jnp.int32, (24, 128), 0)
    for s in range(3):
        for i in range(12):
            below, own, above = (q[s : s + 1, 12 * d + i : 12 * d + i + 1] for d in range(3))
            map_ref[s, i] = jnp.where(row < 16, own, jnp.where(row < 20, above, below))


def spread(label, map_ref, s, c):
    out = jnp.zeros((24, 128), F32)
    for g in range(NREG):
        out = jnp.where(label == g + 1, map_ref[s, 3 * g + c], out)
    return out


def image_of(k_ref, x, field_ref, at):
    here = k_ref[x]
    faces, diagonal = coefficients(k_ref[x - 1], here, k_ref[x + 1])
    planes = [[field_ref[c, i] for c in range(3)] for i in (at - 1, at, at + 1)]
    return planes[1], operate(faces, diagonal, here, *planes)


def start_kernel(k_ref, label_ref, f_ref, r_ref, out_ref, acc_ref):
    def step(x, carry):
        fields, image = image_of(k_ref, x, f_ref, x)
        own = [v[0:16] for v in image]
        rf, faf = carry[12], carry[13]
        for c in range(3):
            f = fields[c][0:16]
            rf = rf + r_ref[c, x - 3] * f
            faf = faf + f * own[c]
        return (*add_regions(carry[:12], label_ref[x, 0:16], own), rf, faf)

    zero = jnp.zeros((16, 128), F32)
    carry = lax.fori_loop(3, 19, step, (zero,) * 14, unroll=16)
    for i in range(14):
        acc_ref[i] = carry[i]
    out_ref[...] = jnp.broadcast_to(totals(acc_ref), (14, 128))


def second_kernel(recv_ref, rc_ref, start_ref, rows_ref, coarse_ref, out_ref, own_ref, near_ref, u_ref, pad_ref):
    near = around(jnp.sum(recv_ref[...], axis=0))
    near_ref[...] = near
    product = rows_ref[0] * near[0:1] + rows_ref[1] * near[1:2] + rows_ref[2] * near[2:3]
    e = start_ref[0:12, 0:1]
    aggregates = e + jnp.sum(product, axis=1, keepdims=True)
    q = in_rows(near[1:2], 12)
    rz = start_ref[12:13, 0:1] + jnp.sum(rc_ref[:, 0:1] * q, axis=0, keepdims=True)
    zw = start_ref[13:14, 0:1] + jnp.sum(q * (e + aggregates), axis=0, keepdims=True)
    fold(aggregates, coarse_ref, u_ref, pad_ref, out_ref, (rz, zw))
    own_ref[...] = in_lanes(aggregates, 12)


def selection():
    out = np.zeros((88, 3 * 128), np.float32)
    for n in range(5):
        for d in range(4):
            for h in range(4):
                g = (h + d) % 4
                for c in range(3):
                    lane = 128 * (n // 2) + 48 * (n % 2) + 12 * d + 3 * h + c
                    out[16 * n + 4 * g + h, lane] -= 1.0
                    if n == 0:
                        out[4 * h + g, lane] -= 1.0
                        if d == 0:
                            out[80 + g, lane] += 1.0
                            out[84 + g, lane] += 1.0
    for g in range(4):
        out[80 + g, 96 + 3 * g] = 1.0
    return out


def tiles(v):
    return v[0:8] + v[8:16]


def pair_kernel(k_ref, label_ref, select_ref, out_ref, rows_ref, acc_ref, sum_ref):
    row = lax.broadcasted_iota(jnp.int32, (24, 128), 0)
    lane = lax.broadcasted_iota(jnp.int32, (24, 128), 1)

    def plane(x, accs, inner):
        here, label = k_ref[x], label_ref[x]
        faces, diagonal = coefficients(k_ref[x - 1], here, k_ref[x + 1])
        y_label = jnp.where(row == 15, 0.0, pltpu.roll(label, 23, axis=0))[0:16]
        z_label = jnp.where(lane == 127, 0.0, pltpu.roll(label, 127, axis=1))[0:16]
        own = label[0:16]
        quarter, coupling = 0.25 * here[0:16], (diagonal - 0.5 * here)[0:16]
        masks = [own == g + 1 for g in range(NREG)]
        out = list(accs)
        for h in range(NREG):
            v = jnp.where(y_label == h + 1, faces[2][0:16], 0.0) + jnp.where(z_label == h + 1, faces[4][0:16], 0.0)
            if inner:
                v = v + jnp.where(label_ref[x + 1, 0:16] == h + 1, faces[0][0:16], 0.0)
            for g in range(NREG):
                out[4 * g + h] = out[4 * g + h] + tiles(jnp.where(masks[g], v, 0.0))
        for g in range(NREG):
            out[16 + g] = out[16 + g] + tiles(jnp.where(masks[g], quarter, 0.0))
            out[20 + g] = out[20 + g] + tiles(jnp.where(masks[g], coupling, 0.0))
        return tuple(out)

    zero = jnp.zeros((8, 128), F32)
    accs = lax.fori_loop(3, 18, lambda x, a: plane(x, a, True), (zero,) * 24, unroll=15)
    accs = plane(18, accs, False)
    for i in range(16):
        acc_ref[i] = accs[i]
    for i in range(8):
        acc_ref[80 + i] = accs[16 + i]
    own = pl.ds(3, 16)
    sides = (
        (k_ref[3, 0:16], label_ref[3, 0:16], k_ref[2, 0:16], label_ref[2, 0:16]),
        (k_ref[18, 0:16], label_ref[18, 0:16], k_ref[19, 0:16], label_ref[19, 0:16]),
        (k_ref[own, 0, :], label_ref[own, 0, :], k_ref[own, 23, :], label_ref[own, 23, :]),
        (k_ref[own, 15, :], label_ref[own, 15, :], k_ref[own, 16, :], label_ref[own, 16, :]),
    )
    for n, (k, label, other, other_label) in enumerate(sides):
        face = 0.5 * k + 0.5 * other
        for g in range(NREG):
            part = jnp.where(label == g + 1, face, 0.0)
            for h in range(NREG):
                acc_ref[16 * n + 16 + 4 * g + h] = tiles(jnp.where(other_label == h + 1, part, 0.0))
    sums = jnp.sum(jnp.sum(acc_ref[...], axis=1), axis=1, keepdims=True)
    for i in range(3):
        out_ref[i : i + 1] = jnp.sum(select_ref[:, 128 * i : 128 * i + 128] * sums, axis=0, keepdims=True)
    sum_ref[...] = jnp.broadcast_to(sums, (88, 128))
    row = lax.broadcasted_iota(jnp.int32, (12, 128), 0)
    lane = lax.broadcasted_iota(jnp.int32, (12, 128), 1)
    first = 3 * ((row >= 3).astype(jnp.int32) + (row >= 6).astype(jnp.int32) + (row >= 9).astype(jnp.int32))
    component = row - first

    def column(indices):
        return jnp.concatenate([jnp.broadcast_to(sum_ref[i : i + 1], (3, 128)) for i in indices], axis=0)

    def block(n, at):
        out = jnp.zeros((12, 128), F32)
        for h in range(NREG):
            value = column([16 * n + 4 * g + h for g in range(NREG)])
            if n == 0:
                value = value + column([4 * h + g for g in range(NREG)])
            out = out - jnp.where(lane == at + 3 * h + component, value, 0.0)
        return out

    quarter, coupling = column(range(80, 84)), column(range(84, 88))
    rows_ref[0] = block(1, 12)
    rows_ref[1] = (
        block(0, 12)
        + block(3, 0)
        + block(4, 24)
        + jnp.where(lane == 12 + row, quarter + coupling, 0.0)
        + jnp.where((lane >= 12 + first) & (lane < 15 + first), quarter, 0.0)
    )
    rows_ref[2] = block(2, 12)


def moment_kernel(
    near_ref, k_ref, label_ref, inv_ref, f_ref, own_ref, z_ref, w_ref, out_ref, g_ref, acc_ref, map_ref
):
    spread_maps(near_ref[...], map_ref)

    def first_step(s):
        def body(x, carry):
            label = label_ref[x]
            for c in range(3):
                z_ref[c, x] = f_ref[c, x] + spread(label, map_ref, s, c)
            return carry

        return body

    lax.fori_loop(1, 3, first_step(0), 0)
    lax.fori_loop(3, 19, first_step(1), 0, unroll=16)
    lax.fori_loop(19, 21, first_step(2), 0)

    def second_step(x, carry):
        _, w = image_of(k_ref, x, z_ref, x)
        inv = inv_ref[x]
        for c in range(3):
            w_ref[c, x - 2] = w[c]
            g_ref[c, x - 2] = w[c] * inv
        return carry

    lax.fori_loop(2, 20, second_step, 0, unroll=18)

    def step(x, carry):
        fields, image = image_of(k_ref, x + 2, g_ref, x)
        own = [v[0:16] for v in image]
        wg, gg = carry[12], carry[13]
        for c in range(3):
            g = fields[c][0:16]
            wg = wg + w_ref[c, x, 0:16] * g
            gg = gg + own[c] * g
        return (*add_regions(carry[:12], label_ref[x + 2, 0:16], own), wg, gg)

    zero = jnp.zeros((16, 128), F32)
    carry = lax.fori_loop(1, 17, step, (zero,) * 14, unroll=16)
    for i in range(12):
        acc_ref[i] = carry[i]
    lane = lax.broadcasted_iota(jnp.int32, (1, 128), 1)
    row = in_lanes(totals(acc_ref), 0) + own_ref[...]
    out_ref[...] = jnp.where(lane == 24, total(carry[12]), jnp.where(lane == 25, total(carry[13]), row))


def group_kernel(recv_ref, out_ref):
    q = jnp.sum(recv_ref[:, 0:4, :], axis=0)
    own = recv_ref[:, 4, :]
    lane = lax.broadcasted_iota(jnp.int32, (16, 128), 1)
    shifted_rows = []
    for s in range(4):
        shifted_rows.append(
            jnp.concatenate([pltpu.roll(q[s : s + 1], (128 - 12 * y) % 128, axis=1) for y in range(8)], axis=0)
        )
    mine, below, above = (
        jnp.concatenate([shifted_rows[s], shifted_rows[s + 1]], axis=0) for s in (1, 0, 2)
    )

    def right(v, by):
        return pltpu.roll(v, by % 128, axis=1)

    def first(v):
        return jnp.where(lane < 12, v, 0.0)

    def four(v):
        v = first(v)
        v = v + right(v, 12)
        return v + right(v, 24)

    alone = first(mine)
    twice = alone + right(alone, 12)
    turned = alone
    for d in range(1, 4):
        turned = turned + right(first(right(twice, -3 * d)), 12 * d)
    turned = turned + right(turned, 48)
    three = mine + right(mine, -1) + right(mine, -2)
    products = (
        recv_ref[:, 5, :] * (turned * (four(mine) + right(four(below), 48)) + right(first(three * three), 96))
        + recv_ref[:, 6, :] * turned * (four(above) + right(four(right(mine, 12)), 48))
        + recv_ref[:, 7, :] * turned * four(right(mine, -12))
        + 2.0 * jnp.where(lane < 12, own * alone, 0.0)
        + jnp.where(lane == 25, own, 0.0)
    )
    pairing = jnp.where((lane >= 12) & (lane < 24), own * twice, jnp.where(lane == 24, own, 0.0))
    at = lax.broadcasted_iota(jnp.int32, (1, 128), 1)
    row = jnp.where(at == 0, total(pairing), jnp.where(at == 1, total(products), 0.0))
    for n in range(NROWS):
        out_ref[n] = row


def third_kernel(recv_ref, k_ref, label_ref, inv_ref, z_ref, w_ref, scal_ref, own_ref, image_ref, znew_ref, map_ref):
    q = jnp.sum(recv_ref[:, 0:4, :], axis=0)
    spread_maps(around(q), map_ref)
    scal_ref[...] = q[0:1]
    rz, zw = q[0:1, SLAB : SLAB + 1], q[0:1, SLAB + 1 : SLAB + 2]
    alpha = rz / zw

    def first_step(s):
        def body(x, carry):
            inv, label = inv_ref[x], label_ref[x]
            for c in range(3):
                y = w_ref[c, x - 2] * inv + spread(label, map_ref, s, c)
                znew_ref[c, x - 2] = z_ref[c, x] - alpha * y
            return carry

        return body

    first_step(0)(2, 0)
    lax.fori_loop(3, 19, first_step(1), 0, unroll=16)
    first_step(2)(19, 0)

    def second_step(x, carry):
        here = k_ref[x + 2]
        faces, diagonal = coefficients(k_ref[x + 1], here, k_ref[x + 3])
        fields = [znew_ref[c, x] for c in range(3)]
        image = operate(
            faces, diagonal, here, [znew_ref[c, x - 1] for c in range(3)], fields, [znew_ref[c, x + 1] for c in range(3)]
        )
        for c in range(3):
            own_ref[c, x - 1] = fields[c][0:16]
            image_ref[c, x - 1] = image[c][0:16]
        return carry

    lax.fori_loop(1, 17, second_step, 0, unroll=16)


def last_kernel(recv_ref, scal_ref, r_ref, z_ref, w_ref, znew_ref, image_ref, x_hbm, res_hbm, x_ref, res_ref, sems):
    sums = jnp.sum(recv_ref[...], axis=0)
    wy, yay = sums[:, 0:1], sums[:, 1:2]
    scal = scal_ref[...]
    rz, zw = scal[:, SLAB : SLAB + 1], scal[:, SLAB + 1 : SLAB + 2]
    alpha = rz / zw
    new = rz + alpha * (alpha * wy - 2.0 * zw)
    zaz = zw + alpha * (alpha * yay - 2.0 * wy)
    cross = zw - alpha * wy
    ratio = new / rz
    second = new / (zaz + ratio * (2.0 * cross + ratio * zw))
    first = alpha + second * ratio

    copies = []
    for part in range(PARTS):
        planes = range(part * 16 // PARTS, (part + 1) * 16 // PARTS)
        for x in planes:
            for c in range(3):
                x_ref[c, x] = first * z_ref[c, x + 3, 0:16] + second * znew_ref[c, x]
                res_ref[c, x] = r_ref[c, x] - first * w_ref[c, x + 1, 0:16] - second * image_ref[c, x]
        own = pl.ds(planes[0], len(planes))
        for i, (ref, out) in enumerate(((x_ref, x_hbm), (res_ref, res_hbm))):
            copies.append(pltpu.make_async_copy(ref.at[:, own], out.at[:, own], sems.at[2 * part + i]))
            copies[-1].start()
    for copy in copies:
        copy.wait()


def exchange(array, axes):
    return lax.all_to_all(array, axes, 0, 0, tiled=True)


def swapped(array, axis, first):
    count = lax.axis_size(axis)
    pairs = [(i, i + 1) for i in range(first, count - 1, 2)]
    return lax.ppermute(array, axis, pairs + [(b, a) for a, b in pairs])


def local(right, occ, reg, coarse):
    field, plane = (16, 16, 128), (24, 128)
    send, r, label_own, coarse, rc = call(
        first_kernel,
        (shape(NROWS, 4, 128), shape(3, *field), shape(*field), shape(12, 6144), shape(12, 128)),
        tuple(pltpu.with_memory_space_constraint(a, pltpu.HBM) for a in (right, reg, coarse)),
        (
            pltpu.VMEM(field, jnp.int32),
            pltpu.VMEM((12, 16, 128), F32),
            *FOLD_SCRATCH,
            pltpu.SemaphoreType.DMA((3,)),
        ),
        space=HBM,
    )
    k_own, one, two = call(
        edge_kernel,
        (shape(*field), shape(3, 16, 4, 128), shape(3, 16, 4, 128)),
        (occ, label_own, r),
        cost=3000000,
    )
    one = swapped(one, "y", 0)
    two = swapped(two, "y", 1)
    got = exchange(send, ROWS)
    first, second = call(
        pack_kernel, (shape(PACK, 128), shape(PACK, 128)), (k_own, label_own, r, one, two), cost=1000000
    )
    first = swapped(first, WIDE, 0)
    second = swapped(second, WIDE, 1)
    send = call(around_kernel, shape(NCOLS, 4, 128), (got,))
    got = exchange(send, COLS)
    k, label, inv, f = call(
        extend_kernel,
        (shape(22, *plane), shape(22, *plane), shape(22, *plane), shape(3, 22, *plane)),
        (r, k_own, label_own, one, two, first, second),
        cost=3000000,
    )
    start = call(start_kernel, shape(14, 128), (k, label, f, r), (pltpu.VMEM((14, 16, 128), F32),), cost=3000000)
    pair, rows = call(
        pair_kernel,
        (shape(3, 128), shape(3, 12, 128)),
        (k, label, jnp.asarray(selection())),
        (pltpu.VMEM((88, 8, 128), F32), pltpu.VMEM((88, 128), F32)),
        cost=3000000,
    )
    send, own, near = call(
        second_kernel,
        (shape(NROWS, 4, 128), shape(1, 128), shape(3, 128)),
        (got, rc, start, rows, coarse),
        FOLD_SCRATCH,
    )
    got = exchange(send, ROWS)
    z, w, own = call(
        moment_kernel,
        (shape(3, 22, *plane), shape(3, 18, *plane), shape(1, 128)),
        (near, k, label, inv, f, own),
        (pltpu.VMEM((3, 18, *plane), F32), pltpu.VMEM((12, 16, 128), F32), pltpu.VMEM((3, 12, *plane), F32)),
        cost=3000000,
        alias={4: 0},
    )
    send = call(pass_kernel, shape(NCOLS, 8, 128), (got, own, pair))
    got = exchange(send, COLS)
    send = call(group_kernel, shape(NROWS, 1, 128), (got,))
    scal, znew, image = call(
        third_kernel,
        (shape(1, 128), shape(3, *field), shape(3, *field)),
        (got, k, label, inv, z, w),
        (pltpu.VMEM((3, 18, *plane), F32), pltpu.VMEM((3, 12, *plane), F32)),
        cost=3000000,
    )
    got = exchange(send, ROWS)
    return call(
        last_kernel,
        (shape(3, *field), shape(3, *field)),
        (got, scal, right, z, w, znew, image),
        (pltpu.VMEM((3, *field), F32), pltpu.VMEM((3, *field), F32), pltpu.SemaphoreType.DMA((2 * PARTS,))),
        target=HBM,
    )


def solution(mesh):
    finer = Mesh(mesh.devices.reshape(4, 8, 2, 8), ("x", "z", "c", "y"))
    field = P(None, WIDE, "y", None)
    labels = P(WIDE, "y", None)
    return jax.shard_map(
        local,
        mesh=finer,
        in_specs=(field, labels, labels, P((*WIDE, "y"), None)),
        out_specs=(field, field),
        check_vma=False,
    )
```

```python
import jax
import jax.numpy as jnp
import numpy as np
from jax import lax
from jax.experimental import pallas as pl
from jax.experimental.pallas import tpu as pltpu
from jax.sharding import Mesh
from jax.sharding import PartitionSpec as P

WIDE = ("x", "z", "c")
ROWS = ("x", "z")
COLS = ("c", "y")
NROWS = 32
NCOLS = 16
F32 = jnp.float32
NREG = 4
SLAB = 96
VMEM = pl.BlockSpec(memory_space=pltpu.VMEM)
HBM = pl.BlockSpec(memory_space=pltpu.HBM)
PARTS = 4
CHUNK = 8


def shape(*dims):
    return jax.ShapeDtypeStruct(dims, F32)


def call(kernel, outs, ins, scratch=(), space=VMEM, target=VMEM, cost=0, limit=24, alias=None):
    return pl.pallas_call(
        kernel,
        out_shape=outs,
        in_specs=[space] * len(ins),
        out_specs=target if isinstance(target, tuple) else jax.tree.map(lambda _: target, outs),
        scratch_shapes=list(scratch),
        input_output_aliases=alias or {},
        cost_estimate=pl.CostEstimate(flops=cost, bytes_accessed=cost, transcendentals=0) if cost else None,
        compiler_params=pltpu.CompilerParams(vmem_limit_bytes=int(limit * 1024 * 1024)),
    )(*ins)


def total(v):
    return jnp.sum(jnp.sum(v, axis=0, keepdims=True), axis=1, keepdims=True)


def add_regions(accs, label, field):
    out = list(accs)
    for g in range(NREG):
        mask = label == g + 1
        for c in range(3):
            out[3 * g + c] = out[3 * g + c] + jnp.where(mask, field[c], 0.0)
    return out


def totals(acc_ref):
    return jnp.sum(jnp.sum(acc_ref[...], axis=1), axis=1, keepdims=True)


def in_lanes(column, at):
    row = lax.broadcasted_iota(jnp.int32, (12, 128), 0)
    lane = lax.broadcasted_iota(jnp.int32, (12, 128), 1)
    return jnp.sum(jnp.where(lane == row + at, column, 0.0), axis=0, keepdims=True)


def in_rows(lanes, at):
    row = lax.broadcasted_iota(jnp.int32, (12, 128), 0)
    lane = lax.broadcasted_iota(jnp.int32, (12, 128), 1)
    return jnp.sum(jnp.where(lane == row + at, lanes, 0.0), axis=1, keepdims=True)


def fold(rc, coarse_ref, u_ref, pad_ref, send_ref, sems, out_ref, sums=()):
    u_ref[...] = jnp.sum(coarse_ref[...] * rc, axis=0, keepdims=True)
    pad_ref[...] = jnp.zeros_like(pad_ref)
    for w in range(2 * NROWS):
        pad_ref[w + 1 : w + 2, 0:SLAB] = u_ref[0:1, SLAB * w : SLAB * (w + 1)]
    if sums:
        lane = lax.broadcasted_iota(jnp.int32, (1, 128), 1)
        row = jnp.zeros((1, 128), F32)
        for i, s in enumerate(sums):
            row = jnp.where(lane == SLAB + i, s, row)
        tail = jnp.broadcast_to(row, (4, 128))
    copies = []
    for n in range(NROWS):
        window = pad_ref[2 * n : 2 * n + 4, :]
        if sums:
            window = window + tail
        send_ref[n] = window
        if n % CHUNK == CHUNK - 1:
            part = pl.ds(n + 1 - CHUNK, CHUNK)
            copies.append(pltpu.make_async_copy(send_ref.at[part], out_ref.at[part], sems.at[n // CHUNK]))
            copies[-1].start()
    return copies


FOLD_SCRATCH = (
    pltpu.VMEM((1, 6144), F32),
    pltpu.VMEM((72, 128), F32),
    pltpu.VMEM((NROWS, 4, 128), F32),
    pltpu.SemaphoreType.DMA((NROWS // 8,)),
)


def even_column():
    return lax.rem(lax.axis_index("y"), 2) == 0


def first_kernel(
    r_hbm, reg_hbm, coarse_hbm, occ_hbm,
    out_hbm, r_ref, label_ref, coarse_ref, rc_ref, k_ref, a_ref, b_ref,
    reg_ref, occ_ref, acc_ref, sems, u_ref, pad_ref, send_ref, send_sems,
):
    pairs = ((r_hbm, r_ref), (reg_hbm, reg_ref), (coarse_hbm, coarse_ref), (occ_hbm, occ_ref))
    copies = [pltpu.make_async_copy(a, b, sems.at[i]) for i, (a, b) in enumerate(pairs)]
    for copy in copies:
        copy.start()
    for copy in copies[:2]:
        copy.wait()

    def step(x, accs):
        label = reg_ref[x].astype(F32) + 1.0
        label_ref[x] = label
        return tuple(add_regions(accs, label, [r_ref[c, x] for c in range(3)]))

    zero = jnp.zeros((16, 128), F32)
    accs = lax.fori_loop(0, 16, step, (zero,) * 12, unroll=16)
    for i in range(12):
        acc_ref[i] = accs[i]
    rc = totals(acc_ref)
    rc_ref[...] = jnp.broadcast_to(rc, (12, 128))
    copies[2].wait()
    sends = fold(rc, coarse_ref, u_ref, pad_ref, send_ref, send_sems, out_hbm)
    copies[3].wait()
    k_ref[...] = 0.1 + 0.9 * occ_ref[...].astype(F32)
    even = even_column()
    for ref, last in ((a_ref, even), (b_ref, jnp.logical_not(even))):
        ref[0] = jnp.where(last, k_ref[:, 12:16, :], k_ref[:, 0:4, :])
        for i, field in enumerate([label_ref] + [r_ref.at[c] for c in range(3)]):
            at = 2 * (i % 2)
            ref[1 + i // 2, :, at : at + 2] = jnp.where(last, field[:, 14:16, :], field[:, 0:2, :])
    for copy in sends:
        copy.wait()


def tail_rows(a_ref, b_ref, i, planes):
    even = even_column()
    if i == 0:
        one, two = a_ref[0, planes], b_ref[0, planes]
        return jnp.concatenate([jnp.where(even, one, two), jnp.where(even, two, one)], axis=1)
    block, at = 1 + (i - 1) // 2, 2 * ((i - 1) % 2)
    one, two = a_ref[block, planes, at : at + 2], b_ref[block, planes, at : at + 2]
    none = jnp.zeros((one.shape[0], 4, 128), F32)
    return jnp.concatenate([jnp.where(even, one, two), none, jnp.where(even, two, one)], axis=1)


PACK = 72 + 4 * 40


def pack_kernel(k_ref, label_ref, r_ref, a_ref, b_ref, first_ref, second_ref):
    fields = [label_ref] + [r_ref.at[c] for c in range(3)]
    core = lax.axis_index("c")
    for ref, up in ((first_ref, core == 0), (second_ref, core == 1)):
        deep, near, next_ = jnp.where(up, 13, 0), jnp.where(up, 15, 0), jnp.where(up, 14, 1)
        tails = tail_rows(a_ref, b_ref, 0, pl.ds(deep, 3))
        for i in range(3):
            ref[24 * i : 24 * i + 16] = k_ref[deep + i]
            ref[24 * i + 16 : 24 * i + 24] = tails[i]
        for i, field in enumerate(fields):
            at = 72 + 40 * i
            ref[at : at + 16] = field[near]
            ref[at + 16 : at + 24] = tail_rows(a_ref, b_ref, 1 + i, pl.ds(near, 1))[0]
            ref[at + 24 : at + 40] = field[next_]


def extend_kernel(
    r_ref, k_own_ref, label_own_ref, a_ref, b_ref, first_ref, second_ref, k_ref, label_ref, inv_ref, f_ref
):
    whole = pl.ds(0, 16)
    core = lax.axis_index("c")

    def sides(rows):
        one, two = first_ref[rows], second_ref[rows]
        return jnp.where(core == 0, two, one), jnp.where(core == 0, one, two)

    k_ref[3:19, 0:16] = k_own_ref[...]
    label_ref[3:19, 0:16] = label_own_ref[...]
    k_ref[3:19, 16:24] = tail_rows(a_ref, b_ref, 0, whole)
    label_ref[3:19, 16:24] = tail_rows(a_ref, b_ref, 1, whole)
    none = jnp.zeros((8, 128), F32)
    for i in range(3):
        below, above = sides(slice(24 * i, 24 * i + 24))
        k_ref[i] = below
        k_ref[19 + i] = above
    targets = [label_ref] + [f_ref.at[c] for c in range(3)]
    for i, ref in enumerate(targets):
        at = 72 + 40 * i
        ref[2], ref[19] = sides(slice(at, at + 24))
        ref[1, 0:16], ref[20, 0:16] = sides(slice(at + 24, at + 40))
        ref[1, 16:24] = ref[20, 16:24] = none
    for c in range(3):
        f_ref[c, 3:19, 0:16] = r_ref[c]
        f_ref[c, 3:19, 16:24] = tail_rows(a_ref, b_ref, 2 + c, whole)

    def step(x, carry):
        here = k_ref[x]
        _, diagonal = coefficients(k_ref[x - 1], here, k_ref[x + 1])
        inside = here > 0.0
        inv = jnp.where(inside, 1.0 / jnp.where(inside, diagonal, 1.0), 0.0)
        inv_ref[x] = inv
        for c in range(3):
            f_ref[c, x] = f_ref[c, x] * inv
        return carry

    lax.fori_loop(1, 21, step, 0, unroll=20)


def around_kernel(recv_ref, out_ref):
    part = jnp.sum(recv_ref[...], axis=0)
    for n in range(NCOLS):
        out_ref[n] = part


def pass_kernel(recv_ref, own_ref, pair_ref, out_ref):
    part = jnp.sum(recv_ref[...], axis=0)
    rows = jnp.concatenate([part, own_ref[...], pair_ref[...]], axis=0)
    for n in range(NCOLS):
        out_ref[n] = rows


def around(q):
    near = jnp.where(lax.axis_index("c") == 0, q[0:3], q[1:4])
    return pltpu.roll(near, lax.rem(140 - 12 * lax.axis_index("y"), 128), axis=1)


def iotas():
    lane = lax.broadcasted_iota(jnp.int32, (24, 128), 1)
    return lane == 0, lane == 127


def coefficients(before, here, after):
    first, last = iotas()
    y_up = pltpu.roll(here, 23, axis=0)
    y_down = pltpu.roll(here, 1, axis=0)
    z_up = jnp.where(last, 0.0, pltpu.roll(here, 127, axis=1))
    z_down = jnp.where(first, 0.0, pltpu.roll(here, 1, axis=1))
    half = 0.5 * here
    faces = [half + 0.5 * other for other in (after, before, y_up, y_down, z_up, z_down)]
    diagonal = faces[0] + faces[1] + faces[2] + faces[3] + faces[4] + faces[5] + half
    faces[4] = jnp.where(last, 0.0, faces[4])
    faces[5] = jnp.where(first, 0.0, faces[5])
    return faces, diagonal


def operate(faces, diagonal, here, befores, fields, afters):
    quarter = 0.25 * here
    main = diagonal - quarter
    shared = quarter * (fields[0] + fields[1] + fields[2])
    out = []
    for c in range(3):
        u = fields[c]
        out.append(
            main * u
            + shared
            - faces[0] * afters[c]
            - faces[1] * befores[c]
            - faces[2] * pltpu.roll(u, 23, axis=0)
            - faces[3] * pltpu.roll(u, 1, axis=0)
            - faces[4] * pltpu.roll(u, 127, axis=1)
            - faces[5] * pltpu.roll(u, 1, axis=1)
        )
    return out


def spread_maps(q, map_ref):
    row = lax.broadcasted_iota(jnp.int32, (24, 128), 0)
    for s in range(3):
        for i in range(12):
            below, own, above = (q[s : s + 1, 12 * d + i : 12 * d + i + 1] for d in range(3))
            map_ref[s, i] = jnp.where(row < 16, own, jnp.where(row < 20, above, below))


def spread(label, map_ref, s, c):
    out = jnp.zeros((24, 128), F32)
    for g in range(NREG):
        out = jnp.where(label == g + 1, map_ref[s, 3 * g + c], out)
    return out


def image_of(k_ref, x, field_ref, at):
    here = k_ref[x]
    faces, diagonal = coefficients(k_ref[x - 1], here, k_ref[x + 1])
    planes = [[field_ref[c, i] for c in range(3)] for i in (at - 1, at, at + 1)]
    return planes[1], operate(faces, diagonal, here, *planes)


def start_kernel(k_ref, label_ref, f_ref, r_ref, out_ref, acc_ref):
    def step(x, carry):
        fields, image = image_of(k_ref, x, f_ref, x)
        own = [v[0:16] for v in image]
        rf, faf = carry[12], carry[13]
        for c in range(3):
            f = fields[c][0:16]
            rf = rf + r_ref[c, x - 3] * f
            faf = faf + f * own[c]
        return (*add_regions(carry[:12], label_ref[x, 0:16], own), rf, faf)

    zero = jnp.zeros((16, 128), F32)
    carry = lax.fori_loop(3, 19, step, (zero,) * 14, unroll=16)
    for i in range(14):
        acc_ref[i] = carry[i]
    out_ref[...] = jnp.broadcast_to(totals(acc_ref), (14, 128))


def second_kernel(
    recv_ref, rc_ref, start_ref, rows_ref, coarse_ref,
    out_hbm, own_ref, near_ref, u_ref, pad_ref, send_ref, send_sems,
):
    near = around(jnp.sum(recv_ref[...], axis=0))
    near_ref[...] = near
    product = rows_ref[0] * near[0:1] + rows_ref[1] * near[1:2] + rows_ref[2] * near[2:3]
    e = start_ref[0:12, 0:1]
    aggregates = e + jnp.sum(product, axis=1, keepdims=True)
    q = in_rows(near[1:2], 12)
    rz = start_ref[12:13, 0:1] + jnp.sum(rc_ref[:, 0:1] * q, axis=0, keepdims=True)
    zw = start_ref[13:14, 0:1] + jnp.sum(q * (e + aggregates), axis=0, keepdims=True)
    sends = fold(aggregates, coarse_ref, u_ref, pad_ref, send_ref, send_sems, out_hbm, (rz, zw))
    own_ref[...] = in_lanes(aggregates, 12)
    for copy in sends:
        copy.wait()


def selection():
    out = np.zeros((88, 3 * 128), np.float32)
    for n in range(5):
        for d in range(4):
            for h in range(4):
                g = (h + d) % 4
                for c in range(3):
                    lane = 128 * (n // 2) + 48 * (n % 2) + 12 * d + 3 * h + c
                    out[16 * n + 4 * g + h, lane] -= 1.0
                    if n == 0:
                        out[4 * h + g, lane] -= 1.0
                        if d == 0:
                            out[80 + g, lane] += 1.0
                            out[84 + g, lane] += 1.0
    for g in range(4):
        out[80 + g, 96 + 3 * g] = 1.0
    return out


def tiles(v):
    return v[0:8] + v[8:16]


def pair_kernel(k_ref, label_ref, select_ref, out_ref, rows_ref, acc_ref, sum_ref):
    row = lax.broadcasted_iota(jnp.int32, (24, 128), 0)
    lane = lax.broadcasted_iota(jnp.int32, (24, 128), 1)

    def plane(x, accs, inner):
        here, label = k_ref[x], label_ref[x]
        faces, diagonal = coefficients(k_ref[x - 1], here, k_ref[x + 1])
        y_label = jnp.where(row == 15, 0.0, pltpu.roll(label, 23, axis=0))[0:16]
        z_label = jnp.where(lane == 127, 0.0, pltpu.roll(label, 127, axis=1))[0:16]
        own = label[0:16]
        quarter, coupling = 0.25 * here[0:16], (diagonal - 0.5 * here)[0:16]
        masks = [own == g + 1 for g in range(NREG)]
        out = list(accs)
        for h in range(NREG):
            v = jnp.where(y_label == h + 1, faces[2][0:16], 0.0) + jnp.where(z_label == h + 1, faces[4][0:16], 0.0)
            if inner:
                v = v + jnp.where(label_ref[x + 1, 0:16] == h + 1, faces[0][0:16], 0.0)
            for g in range(NREG):
                out[4 * g + h] = out[4 * g + h] + tiles(jnp.where(masks[g], v, 0.0))
        for g in range(NREG):
            out[16 + g] = out[16 + g] + tiles(jnp.where(masks[g], quarter, 0.0))
            out[20 + g] = out[20 + g] + tiles(jnp.where(masks[g], coupling, 0.0))
        return tuple(out)

    zero = jnp.zeros((8, 128), F32)
    accs = lax.fori_loop(3, 18, lambda x, a: plane(x, a, True), (zero,) * 24, unroll=15)
    accs = plane(18, accs, False)
    for i in range(16):
        acc_ref[i] = accs[i]
    for i in range(8):
        acc_ref[80 + i] = accs[16 + i]
    own = pl.ds(3, 16)
    sides = (
        (k_ref[3, 0:16], label_ref[3, 0:16], k_ref[2, 0:16], label_ref[2, 0:16]),
        (k_ref[18, 0:16], label_ref[18, 0:16], k_ref[19, 0:16], label_ref[19, 0:16]),
        (k_ref[own, 0, :], label_ref[own, 0, :], k_ref[own, 23, :], label_ref[own, 23, :]),
        (k_ref[own, 15, :], label_ref[own, 15, :], k_ref[own, 16, :], label_ref[own, 16, :]),
    )
    for n, (k, label, other, other_label) in enumerate(sides):
        face = 0.5 * k + 0.5 * other
        for g in range(NREG):
            part = jnp.where(label == g + 1, face, 0.0)
            for h in range(NREG):
                acc_ref[16 * n + 16 + 4 * g + h] = tiles(jnp.where(other_label == h + 1, part, 0.0))
    sums = jnp.sum(jnp.sum(acc_ref[...], axis=1), axis=1, keepdims=True)
    for i in range(3):
        out_ref[i : i + 1] = jnp.sum(select_ref[:, 128 * i : 128 * i + 128] * sums, axis=0, keepdims=True)
    sum_ref[...] = jnp.broadcast_to(sums, (88, 128))
    row = lax.broadcasted_iota(jnp.int32, (12, 128), 0)
    lane = lax.broadcasted_iota(jnp.int32, (12, 128), 1)
    first = 3 * ((row >= 3).astype(jnp.int32) + (row >= 6).astype(jnp.int32) + (row >= 9).astype(jnp.int32))
    component = row - first

    def column(indices):
        return jnp.concatenate([jnp.broadcast_to(sum_ref[i : i + 1], (3, 128)) for i in indices], axis=0)

    def block(n, at):
        out = jnp.zeros((12, 128), F32)
        for h in range(NREG):
            value = column([16 * n + 4 * g + h for g in range(NREG)])
            if n == 0:
                value = value + column([4 * h + g for g in range(NREG)])
            out = out - jnp.where(lane == at + 3 * h + component, value, 0.0)
        return out

    quarter, coupling = column(range(80, 84)), column(range(84, 88))
    rows_ref[0] = block(1, 12)
    rows_ref[1] = (
        block(0, 12)
        + block(3, 0)
        + block(4, 24)
        + jnp.where(lane == 12 + row, quarter + coupling, 0.0)
        + jnp.where((lane >= 12 + first) & (lane < 15 + first), quarter, 0.0)
    )
    rows_ref[2] = block(2, 12)


def moment_kernel(
    near_ref, k_ref, label_ref, inv_ref, f_ref, own_ref, z_ref, w_ref, out_ref, g_ref, acc_ref, map_ref
):
    spread_maps(near_ref[...], map_ref)

    def first_step(s):
        def body(x, carry):
            label = label_ref[x]
            for c in range(3):
                z_ref[c, x] = f_ref[c, x] + spread(label, map_ref, s, c)
            return carry

        return body

    lax.fori_loop(1, 3, first_step(0), 0)
    lax.fori_loop(3, 19, first_step(1), 0, unroll=16)
    lax.fori_loop(19, 21, first_step(2), 0)

    def second_step(x, carry):
        _, w = image_of(k_ref, x, z_ref, x)
        inv = inv_ref[x]
        for c in range(3):
            w_ref[c, x - 2] = w[c]
            g_ref[c, x - 2] = w[c] * inv
        return carry

    lax.fori_loop(2, 20, second_step, 0, unroll=18)

    def step(x, carry):
        fields, image = image_of(k_ref, x + 2, g_ref, x)
        own = [v[0:16] for v in image]
        wg, gg = carry[12], carry[13]
        for c in range(3):
            g = fields[c][0:16]
            wg = wg + w_ref[c, x, 0:16] * g
            gg = gg + own[c] * g
        return (*add_regions(carry[:12], label_ref[x + 2, 0:16], own), wg, gg)

    zero = jnp.zeros((16, 128), F32)
    carry = lax.fori_loop(1, 17, step, (zero,) * 14, unroll=16)
    for i in range(12):
        acc_ref[i] = carry[i]
    lane = lax.broadcasted_iota(jnp.int32, (1, 128), 1)
    row = in_lanes(totals(acc_ref), 0) + own_ref[...]
    out_ref[...] = jnp.where(lane == 24, total(carry[12]), jnp.where(lane == 25, total(carry[13]), row))


def group_kernel(recv_ref, out_ref):
    q = jnp.sum(recv_ref[:, 0:4, :], axis=0)
    own = recv_ref[:, 4, :]
    lane = lax.broadcasted_iota(jnp.int32, (16, 128), 1)
    shifted_rows = []
    for s in range(4):
        shifted_rows.append(
            jnp.concatenate([pltpu.roll(q[s : s + 1], (128 - 12 * y) % 128, axis=1) for y in range(8)], axis=0)
        )
    mine, below, above = (
        jnp.concatenate([shifted_rows[s], shifted_rows[s + 1]], axis=0) for s in (1, 0, 2)
    )

    def right(v, by):
        return pltpu.roll(v, by % 128, axis=1)

    def first(v):
        return jnp.where(lane < 12, v, 0.0)

    def four(v):
        v = first(v)
        v = v + right(v, 12)
        return v + right(v, 24)

    alone = first(mine)
    twice = alone + right(alone, 12)
    turned = alone
    for d in range(1, 4):
        turned = turned + right(first(right(twice, -3 * d)), 12 * d)
    turned = turned + right(turned, 48)
    three = mine + right(mine, -1) + right(mine, -2)
    products = (
        recv_ref[:, 5, :] * (turned * (four(mine) + right(four(below), 48)) + right(first(three * three), 96))
        + recv_ref[:, 6, :] * turned * (four(above) + right(four(right(mine, 12)), 48))
        + recv_ref[:, 7, :] * turned * four(right(mine, -12))
        + 2.0 * jnp.where(lane < 12, own * alone, 0.0)
        + jnp.where(lane == 25, own, 0.0)
    )
    pairing = jnp.where((lane >= 12) & (lane < 24), own * twice, jnp.where(lane == 24, own, 0.0))
    at = lax.broadcasted_iota(jnp.int32, (1, 128), 1)
    row = jnp.where(at == 0, total(pairing), jnp.where(at == 1, total(products), 0.0))
    for n in range(NROWS):
        out_ref[n] = row


def third_kernel(recv_ref, k_ref, label_ref, inv_ref, z_ref, w_ref, scal_ref, own_ref, image_ref, znew_ref, map_ref):
    q = jnp.sum(recv_ref[:, 0:4, :], axis=0)
    spread_maps(around(q), map_ref)
    scal_ref[...] = q[0:1]
    rz, zw = q[0:1, SLAB : SLAB + 1], q[0:1, SLAB + 1 : SLAB + 2]
    alpha = rz / zw

    def first_step(s):
        def body(x, carry):
            inv, label = inv_ref[x], label_ref[x]
            for c in range(3):
                y = w_ref[c, x - 2] * inv + spread(label, map_ref, s, c)
                znew_ref[c, x - 2] = z_ref[c, x] - alpha * y
            return carry

        return body

    first_step(0)(2, 0)
    lax.fori_loop(3, 19, first_step(1), 0, unroll=16)
    first_step(2)(19, 0)

    def second_step(x, carry):
        here = k_ref[x + 2]
        faces, diagonal = coefficients(k_ref[x + 1], here, k_ref[x + 3])
        fields = [znew_ref[c, x] for c in range(3)]
        image = operate(
            faces, diagonal, here, [znew_ref[c, x - 1] for c in range(3)], fields, [znew_ref[c, x + 1] for c in range(3)]
        )
        for c in range(3):
            own_ref[c, x - 1] = fields[c][0:16]
            image_ref[c, x - 1] = image[c][0:16]
        return carry

    lax.fori_loop(1, 17, second_step, 0, unroll=16)


def last_kernel(recv_ref, scal_ref, r_ref, z_ref, w_ref, znew_ref, image_ref, x_hbm, res_hbm, x_ref, res_ref, sems):
    sums = jnp.sum(recv_ref[...], axis=0)
    wy, yay = sums[:, 0:1], sums[:, 1:2]
    scal = scal_ref[...]
    rz, zw = scal[:, SLAB : SLAB + 1], scal[:, SLAB + 1 : SLAB + 2]
    alpha = rz / zw
    new = rz + alpha * (alpha * wy - 2.0 * zw)
    zaz = zw + alpha * (alpha * yay - 2.0 * wy)
    cross = zw - alpha * wy
    ratio = new / rz
    second = new / (zaz + ratio * (2.0 * cross + ratio * zw))
    first = alpha + second * ratio

    copies = []
    for part in range(PARTS):
        planes = range(part * 16 // PARTS, (part + 1) * 16 // PARTS)
        for x in planes:
            for c in range(3):
                x_ref[c, x] = first * z_ref[c, x + 3, 0:16] + second * znew_ref[c, x]
                res_ref[c, x] = r_ref[c, x] - first * w_ref[c, x + 1, 0:16] - second * image_ref[c, x]
        own = pl.ds(planes[0], len(planes))
        for i, (ref, out) in enumerate(((x_ref, x_hbm), (res_ref, res_hbm))):
            copies.append(pltpu.make_async_copy(ref.at[:, own], out.at[:, own], sems.at[2 * part + i]))
            copies[-1].start()
    for copy in copies:
        copy.wait()


def exchange(array, axes):
    return lax.all_to_all(array, axes, 0, 0, tiled=True)


def swapped(array, axis, first):
    count = lax.axis_size(axis)
    pairs = [(i, i + 1) for i in range(first, count - 1, 2)]
    return lax.ppermute(array, axis, pairs + [(b, a) for a, b in pairs])


def local(right, occ, reg, coarse):
    field, plane = (16, 16, 128), (24, 128)
    send, r, label_own, coarse, rc, k_own, one, two = call(
        first_kernel,
        (
            shape(NROWS, 4, 128),
            shape(3, *field),
            shape(*field),
            shape(12, 6144),
            shape(12, 128),
            shape(*field),
            shape(3, 16, 4, 128),
            shape(3, 16, 4, 128),
        ),
        tuple(pltpu.with_memory_space_constraint(a, pltpu.HBM) for a in (right, reg, coarse, occ)),
        (
            pltpu.VMEM(field, jnp.int32),
            pltpu.VMEM(field, jnp.int32),
            pltpu.VMEM((12, 16, 128), F32),
            pltpu.SemaphoreType.DMA((4,)),
            *FOLD_SCRATCH,
        ),
        space=HBM,
        target=(HBM,) + (VMEM,) * 7,
    )
    one = swapped(one, "y", 0)
    two = swapped(two, "y", 1)
    got = exchange(send, ROWS)
    first, second = call(
        pack_kernel, (shape(PACK, 128), shape(PACK, 128)), (k_own, label_own, r, one, two), cost=1000000
    )
    first = swapped(first, WIDE, 0)
    second = swapped(second, WIDE, 1)
    send = call(around_kernel, shape(NCOLS, 4, 128), (got,))
    got = exchange(send, COLS)
    k, label, inv, f = call(
        extend_kernel,
        (shape(22, *plane), shape(22, *plane), shape(22, *plane), shape(3, 22, *plane)),
        (r, k_own, label_own, one, two, first, second),
        cost=3000000,
    )
    start = call(start_kernel, shape(14, 128), (k, label, f, r), (pltpu.VMEM((14, 16, 128), F32),), cost=3000000)
    pair, rows = call(
        pair_kernel,
        (shape(3, 128), shape(3, 12, 128)),
        (k, label, jnp.asarray(selection())),
        (pltpu.VMEM((88, 8, 128), F32), pltpu.VMEM((88, 128), F32)),
        cost=3000000,
    )
    send, own, near = call(
        second_kernel,
        (shape(NROWS, 4, 128), shape(1, 128), shape(3, 128)),
        (got, rc, start, rows, coarse),
        FOLD_SCRATCH,
        target=(HBM, VMEM, VMEM),
    )
    got = exchange(send, ROWS)
    z, w, own = call(
        moment_kernel,
        (shape(3, 22, *plane), shape(3, 18, *plane), shape(1, 128)),
        (near, k, label, inv, f, own),
        (pltpu.VMEM((3, 18, *plane), F32), pltpu.VMEM((12, 16, 128), F32), pltpu.VMEM((3, 12, *plane), F32)),
        cost=3000000,
        alias={4: 0},
    )
    send = call(pass_kernel, shape(NCOLS, 8, 128), (got, own, pair))
    got = exchange(send, COLS)
    send = call(group_kernel, shape(NROWS, 1, 128), (got,))
    scal, znew, image = call(
        third_kernel,
        (shape(1, 128), shape(3, *field), shape(3, *field)),
        (got, k, label, inv, z, w),
        (pltpu.VMEM((3, 18, *plane), F32), pltpu.VMEM((3, 12, *plane), F32)),
        cost=3000000,
    )
    got = exchange(send, ROWS)
    return call(
        last_kernel,
        (shape(3, *field), shape(3, *field)),
        (got, scal, right, z, w, znew, image),
        (pltpu.VMEM((3, *field), F32), pltpu.VMEM((3, *field), F32), pltpu.SemaphoreType.DMA((2 * PARTS,))),
        target=HBM,
    )


def solution(mesh):
    finer = Mesh(mesh.devices.reshape(4, 8, 2, 8), ("x", "z", "c", "y"))
    field = P(None, WIDE, "y", None)
    labels = P(WIDE, "y", None)
    return jax.shard_map(
        local,
        mesh=finer,
        in_specs=(field, labels, labels, P((*WIDE, "y"), None)),
        out_specs=(field, field),
        check_vma=False,
    )
```

```python
import jax
import jax.numpy as jnp
import numpy as np
from jax import lax
from jax.experimental import pallas as pl
from jax.experimental.pallas import tpu as pltpu
from jax.sharding import Mesh
from jax.sharding import PartitionSpec as P

WIDE = ("x", "z", "c")
ROWS = ("x", "z")
COLS = ("c", "y")
NROWS = 32
NCOLS = 16
F32 = jnp.float32
NREG = 4
SLAB = 96
VMEM = pl.BlockSpec(memory_space=pltpu.VMEM)
HBM = pl.BlockSpec(memory_space=pltpu.HBM)
PARTS = 4
CHUNK = 8


def shape(*dims):
    return jax.ShapeDtypeStruct(dims, F32)


def call(kernel, outs, ins, scratch=(), space=VMEM, target=VMEM, cost=0, limit=24, alias=None):
    return pl.pallas_call(
        kernel,
        out_shape=outs,
        in_specs=[space] * len(ins),
        out_specs=target if isinstance(target, tuple) else jax.tree.map(lambda _: target, outs),
        scratch_shapes=list(scratch),
        input_output_aliases=alias or {},
        cost_estimate=pl.CostEstimate(flops=cost, bytes_accessed=cost, transcendentals=0) if cost else None,
        compiler_params=pltpu.CompilerParams(vmem_limit_bytes=int(limit * 1024 * 1024)),
    )(*ins)


def total(v):
    return jnp.sum(jnp.sum(v, axis=0, keepdims=True), axis=1, keepdims=True)


def add_regions(accs, label, field):
    out = list(accs)
    for g in range(NREG):
        mask = label == g + 1
        for c in range(3):
            out[3 * g + c] = out[3 * g + c] + jnp.where(mask, field[c], 0.0)
    return out


def totals(acc_ref):
    return jnp.sum(jnp.sum(acc_ref[...], axis=1), axis=1, keepdims=True)


def in_lanes(column, at):
    row = lax.broadcasted_iota(jnp.int32, (12, 128), 0)
    lane = lax.broadcasted_iota(jnp.int32, (12, 128), 1)
    return jnp.sum(jnp.where(lane == row + at, column, 0.0), axis=0, keepdims=True)


def in_rows(lanes, at):
    row = lax.broadcasted_iota(jnp.int32, (12, 128), 0)
    lane = lax.broadcasted_iota(jnp.int32, (12, 128), 1)
    return jnp.sum(jnp.where(lane == row + at, lanes, 0.0), axis=1, keepdims=True)


def fold(rc, coarse_ref, u_ref, pad_ref, send_ref, sems, out_ref, sums=()):
    u_ref[...] = jnp.sum(coarse_ref[...] * rc, axis=0, keepdims=True)
    pad_ref[...] = jnp.zeros_like(pad_ref)
    for w in range(2 * NROWS):
        pad_ref[w + 1 : w + 2, 0:SLAB] = u_ref[0:1, SLAB * w : SLAB * (w + 1)]
    if sums:
        lane = lax.broadcasted_iota(jnp.int32, (1, 128), 1)
        row = jnp.zeros((1, 128), F32)
        for i, s in enumerate(sums):
            row = jnp.where(lane == SLAB + i, s, row)
        tail = jnp.broadcast_to(row, (4, 128))
    copies = []
    for n in range(NROWS):
        window = pad_ref[2 * n : 2 * n + 4, :]
        if sums:
            window = window + tail
        send_ref[n] = window
        if n % CHUNK == CHUNK - 1:
            part = pl.ds(n + 1 - CHUNK, CHUNK)
            copies.append(pltpu.make_async_copy(send_ref.at[part], out_ref.at[part], sems.at[n // CHUNK]))
            copies[-1].start()
    return copies


FOLD_SCRATCH = (
    pltpu.VMEM((1, 6144), F32),
    pltpu.VMEM((72, 128), F32),
    pltpu.VMEM((NROWS, 4, 128), F32),
    pltpu.SemaphoreType.DMA((NROWS // 8,)),
)


def even_column():
    return lax.rem(lax.axis_index("y"), 2) == 0


def first_kernel(
    r_hbm, reg_hbm, coarse_hbm, occ_hbm,
    out_hbm, r_ref, label_ref, coarse_ref, rc_ref, k_ref, a_ref, b_ref,
    reg_ref, occ_ref, acc_ref, sems, u_ref, pad_ref, send_ref, send_sems,
):
    pairs = ((r_hbm, r_ref), (reg_hbm, reg_ref), (coarse_hbm, coarse_ref), (occ_hbm, occ_ref))
    copies = [pltpu.make_async_copy(a, b, sems.at[i]) for i, (a, b) in enumerate(pairs)]
    for copy in copies:
        copy.start()
    for copy in copies[:2]:
        copy.wait()

    def step(x, accs):
        label = reg_ref[x].astype(F32) + 1.0
        label_ref[x] = label
        return tuple(add_regions(accs, label, [r_ref[c, x] for c in range(3)]))

    zero = jnp.zeros((16, 128), F32)
    accs = lax.fori_loop(0, 16, step, (zero,) * 12, unroll=16)
    for i in range(12):
        acc_ref[i] = accs[i]
    rc = totals(acc_ref)
    rc_ref[...] = jnp.broadcast_to(rc, (12, 128))
    copies[2].wait()
    sends = fold(rc, coarse_ref, u_ref, pad_ref, send_ref, send_sems, out_hbm)
    copies[3].wait()
    k_ref[...] = 0.1 + 0.9 * occ_ref[...].astype(F32)
    even = even_column()
    for ref, last in ((a_ref, even), (b_ref, jnp.logical_not(even))):
        ref[0] = jnp.where(last, k_ref[:, 12:16, :], k_ref[:, 0:4, :])
        for i, field in enumerate([label_ref] + [r_ref.at[c] for c in range(3)]):
            at = 2 * (i % 2)
            ref[1 + i // 2, :, at : at + 2] = jnp.where(last, field[:, 14:16, :], field[:, 0:2, :])
    for copy in sends:
        copy.wait()


def tail_rows(a_ref, b_ref, i, planes):
    even = even_column()
    if i == 0:
        one, two = a_ref[0, planes], b_ref[0, planes]
        return jnp.concatenate([jnp.where(even, one, two), jnp.where(even, two, one)], axis=1)
    block, at = 1 + (i - 1) // 2, 2 * ((i - 1) % 2)
    one, two = a_ref[block, planes, at : at + 2], b_ref[block, planes, at : at + 2]
    none = jnp.zeros((one.shape[0], 4, 128), F32)
    return jnp.concatenate([jnp.where(even, one, two), none, jnp.where(even, two, one)], axis=1)


PACK = 72 + 4 * 40


def pack_kernel(k_ref, label_ref, r_ref, a_ref, b_ref, first_ref, second_ref):
    fields = [label_ref] + [r_ref.at[c] for c in range(3)]
    core = lax.axis_index("c")
    for ref, up in ((first_ref, core == 0), (second_ref, core == 1)):
        deep, near, next_ = jnp.where(up, 13, 0), jnp.where(up, 15, 0), jnp.where(up, 14, 1)
        tails = tail_rows(a_ref, b_ref, 0, pl.ds(deep, 3))
        for i in range(3):
            ref[24 * i : 24 * i + 16] = k_ref[deep + i]
            ref[24 * i + 16 : 24 * i + 24] = tails[i]
        for i, field in enumerate(fields):
            at = 72 + 40 * i
            ref[at : at + 16] = field[near]
            ref[at + 16 : at + 24] = tail_rows(a_ref, b_ref, 1 + i, pl.ds(near, 1))[0]
            ref[at + 24 : at + 40] = field[next_]


def extend_kernel(
    r_ref, k_own_ref, label_own_ref, a_ref, b_ref, first_ref, second_ref, k_ref, label_ref, inv_ref, f_ref
):
    whole = pl.ds(0, 16)
    core = lax.axis_index("c")

    def sides(rows):
        one, two = first_ref[1 - core, rows], second_ref[rows]
        return jnp.where(core == 0, two, one), jnp.where(core == 0, one, two)

    k_ref[3:19, 0:16] = k_own_ref[...]
    label_ref[3:19, 0:16] = label_own_ref[...]
    k_ref[3:19, 16:24] = tail_rows(a_ref, b_ref, 0, whole)
    label_ref[3:19, 16:24] = tail_rows(a_ref, b_ref, 1, whole)
    none = jnp.zeros((8, 128), F32)
    for i in range(3):
        below, above = sides(slice(24 * i, 24 * i + 24))
        k_ref[i] = below
        k_ref[19 + i] = above
    targets = [label_ref] + [f_ref.at[c] for c in range(3)]
    for i, ref in enumerate(targets):
        at = 72 + 40 * i
        ref[2], ref[19] = sides(slice(at, at + 24))
        ref[1, 0:16], ref[20, 0:16] = sides(slice(at + 24, at + 40))
        ref[1, 16:24] = ref[20, 16:24] = none
    for c in range(3):
        f_ref[c, 3:19, 0:16] = r_ref[c]
        f_ref[c, 3:19, 16:24] = tail_rows(a_ref, b_ref, 2 + c, whole)

    def step(x, carry):
        here = k_ref[x]
        _, diagonal = coefficients(k_ref[x - 1], here, k_ref[x + 1])
        inside = here > 0.0
        inv = jnp.where(inside, 1.0 / jnp.where(inside, diagonal, 1.0), 0.0)
        inv_ref[x] = inv
        for c in range(3):
            f_ref[c, x] = f_ref[c, x] * inv
        return carry

    lax.fori_loop(1, 21, step, 0, unroll=20)


def around_kernel(recv_ref, out_ref):
    part = jnp.sum(recv_ref[...], axis=0)
    for n in range(NCOLS):
        out_ref[n] = part


def pass_kernel(recv_ref, own_ref, pair_ref, out_ref):
    part = jnp.sum(recv_ref[...], axis=0)
    rows = jnp.concatenate([part, own_ref[...], pair_ref[...]], axis=0)
    for n in range(NCOLS):
        out_ref[n] = rows


def around(q):
    near = jnp.where(lax.axis_index("c") == 0, q[0:3], q[1:4])
    return pltpu.roll(near, lax.rem(140 - 12 * lax.axis_index("y"), 128), axis=1)


def iotas():
    lane = lax.broadcasted_iota(jnp.int32, (24, 128), 1)
    return lane == 0, lane == 127


def coefficients(before, here, after):
    first, last = iotas()
    y_up = pltpu.roll(here, 23, axis=0)
    y_down = pltpu.roll(here, 1, axis=0)
    z_up = jnp.where(last, 0.0, pltpu.roll(here, 127, axis=1))
    z_down = jnp.where(first, 0.0, pltpu.roll(here, 1, axis=1))
    half = 0.5 * here
    faces = [half + 0.5 * other for other in (after, before, y_up, y_down, z_up, z_down)]
    diagonal = faces[0] + faces[1] + faces[2] + faces[3] + faces[4] + faces[5] + half
    faces[4] = jnp.where(last, 0.0, faces[4])
    faces[5] = jnp.where(first, 0.0, faces[5])
    return faces, diagonal


def operate(faces, diagonal, here, befores, fields, afters):
    quarter = 0.25 * here
    main = diagonal - quarter
    shared = quarter * (fields[0] + fields[1] + fields[2])
    out = []
    for c in range(3):
        u = fields[c]
        out.append(
            main * u
            + shared
            - faces[0] * afters[c]
            - faces[1] * befores[c]
            - faces[2] * pltpu.roll(u, 23, axis=0)
            - faces[3] * pltpu.roll(u, 1, axis=0)
            - faces[4] * pltpu.roll(u, 127, axis=1)
            - faces[5] * pltpu.roll(u, 1, axis=1)
        )
    return out


def spread_maps(q, map_ref):
    row = lax.broadcasted_iota(jnp.int32, (24, 128), 0)
    for s in range(3):
        for i in range(12):
            below, own, above = (q[s : s + 1, 12 * d + i : 12 * d + i + 1] for d in range(3))
            map_ref[s, i] = jnp.where(row < 16, own, jnp.where(row < 20, above, below))


def spread(label, map_ref, s, c):
    out = jnp.zeros((24, 128), F32)
    for g in range(NREG):
        out = jnp.where(label == g + 1, map_ref[s, 3 * g + c], out)
    return out


def image_of(k_ref, x, field_ref, at):
    here = k_ref[x]
    faces, diagonal = coefficients(k_ref[x - 1], here, k_ref[x + 1])
    planes = [[field_ref[c, i] for c in range(3)] for i in (at - 1, at, at + 1)]
    return planes[1], operate(faces, diagonal, here, *planes)


def start_kernel(k_ref, label_ref, f_ref, r_ref, out_ref, acc_ref):
    def step(x, carry):
        fields, image = image_of(k_ref, x, f_ref, x)
        own = [v[0:16] for v in image]
        rf, faf = carry[12], carry[13]
        for c in range(3):
            f = fields[c][0:16]
            rf = rf + r_ref[c, x - 3] * f
            faf = faf + f * own[c]
        return (*add_regions(carry[:12], label_ref[x, 0:16], own), rf, faf)

    zero = jnp.zeros((16, 128), F32)
    carry = lax.fori_loop(3, 19, step, (zero,) * 14, unroll=16)
    for i in range(14):
        acc_ref[i] = carry[i]
    out_ref[...] = jnp.broadcast_to(totals(acc_ref), (14, 128))


def second_kernel(
    recv_ref, rc_ref, start_ref, rows_ref, coarse_ref,
    out_hbm, own_ref, near_ref, u_ref, pad_ref, send_ref, send_sems,
):
    near = around(jnp.sum(recv_ref[...], axis=0))
    near_ref[...] = near
    product = rows_ref[0] * near[0:1] + rows_ref[1] * near[1:2] + rows_ref[2] * near[2:3]
    e = start_ref[0:12, 0:1]
    aggregates = e + jnp.sum(product, axis=1, keepdims=True)
    q = in_rows(near[1:2], 12)
    rz = start_ref[12:13, 0:1] + jnp.sum(rc_ref[:, 0:1] * q, axis=0, keepdims=True)
    zw = start_ref[13:14, 0:1] + jnp.sum(q * (e + aggregates), axis=0, keepdims=True)
    sends = fold(aggregates, coarse_ref, u_ref, pad_ref, send_ref, send_sems, out_hbm, (rz, zw))
    own_ref[...] = in_lanes(aggregates, 12)
    for copy in sends:
        copy.wait()


def selection():
    out = np.zeros((88, 3 * 128), np.float32)
    for n in range(5):
        for d in range(4):
            for h in range(4):
                g = (h + d) % 4
                for c in range(3):
                    lane = 128 * (n // 2) + 48 * (n % 2) + 12 * d + 3 * h + c
                    out[16 * n + 4 * g + h, lane] -= 1.0
                    if n == 0:
                        out[4 * h + g, lane] -= 1.0
                        if d == 0:
                            out[80 + g, lane] += 1.0
                            out[84 + g, lane] += 1.0
    for g in range(4):
        out[80 + g, 96 + 3 * g] = 1.0
    return out


def tiles(v):
    return v[0:8] + v[8:16]


def pair_kernel(k_ref, label_ref, select_ref, out_ref, rows_ref, acc_ref, sum_ref):
    row = lax.broadcasted_iota(jnp.int32, (24, 128), 0)
    lane = lax.broadcasted_iota(jnp.int32, (24, 128), 1)

    def plane(x, accs, inner):
        here, label = k_ref[x], label_ref[x]
        faces, diagonal = coefficients(k_ref[x - 1], here, k_ref[x + 1])
        y_label = jnp.where(row == 15, 0.0, pltpu.roll(label, 23, axis=0))[0:16]
        z_label = jnp.where(lane == 127, 0.0, pltpu.roll(label, 127, axis=1))[0:16]
        own = label[0:16]
        quarter, coupling = 0.25 * here[0:16], (diagonal - 0.5 * here)[0:16]
        masks = [own == g + 1 for g in range(NREG)]
        out = list(accs)
        for h in range(NREG):
            v = jnp.where(y_label == h + 1, faces[2][0:16], 0.0) + jnp.where(z_label == h + 1, faces[4][0:16], 0.0)
            if inner:
                v = v + jnp.where(label_ref[x + 1, 0:16] == h + 1, faces[0][0:16], 0.0)
            for g in range(NREG):
                out[4 * g + h] = out[4 * g + h] + tiles(jnp.where(masks[g], v, 0.0))
        for g in range(NREG):
            out[16 + g] = out[16 + g] + tiles(jnp.where(masks[g], quarter, 0.0))
            out[20 + g] = out[20 + g] + tiles(jnp.where(masks[g], coupling, 0.0))
        return tuple(out)

    zero = jnp.zeros((8, 128), F32)
    accs = lax.fori_loop(3, 18, lambda x, a: plane(x, a, True), (zero,) * 24, unroll=15)
    accs = plane(18, accs, False)
    for i in range(16):
        acc_ref[i] = accs[i]
    for i in range(8):
        acc_ref[80 + i] = accs[16 + i]
    own = pl.ds(3, 16)
    sides = (
        (k_ref[3, 0:16], label_ref[3, 0:16], k_ref[2, 0:16], label_ref[2, 0:16]),
        (k_ref[18, 0:16], label_ref[18, 0:16], k_ref[19, 0:16], label_ref[19, 0:16]),
        (k_ref[own, 0, :], label_ref[own, 0, :], k_ref[own, 23, :], label_ref[own, 23, :]),
        (k_ref[own, 15, :], label_ref[own, 15, :], k_ref[own, 16, :], label_ref[own, 16, :]),
    )
    for n, (k, label, other, other_label) in enumerate(sides):
        face = 0.5 * k + 0.5 * other
        for g in range(NREG):
            part = jnp.where(label == g + 1, face, 0.0)
            for h in range(NREG):
                acc_ref[16 * n + 16 + 4 * g + h] = tiles(jnp.where(other_label == h + 1, part, 0.0))
    sums = jnp.sum(jnp.sum(acc_ref[...], axis=1), axis=1, keepdims=True)
    for i in range(3):
        out_ref[i : i + 1] = jnp.sum(select_ref[:, 128 * i : 128 * i + 128] * sums, axis=0, keepdims=True)
    sum_ref[...] = jnp.broadcast_to(sums, (88, 128))
    row = lax.broadcasted_iota(jnp.int32, (12, 128), 0)
    lane = lax.broadcasted_iota(jnp.int32, (12, 128), 1)
    first = 3 * ((row >= 3).astype(jnp.int32) + (row >= 6).astype(jnp.int32) + (row >= 9).astype(jnp.int32))
    component = row - first

    def column(indices):
        return jnp.concatenate([jnp.broadcast_to(sum_ref[i : i + 1], (3, 128)) for i in indices], axis=0)

    def block(n, at):
        out = jnp.zeros((12, 128), F32)
        for h in range(NREG):
            value = column([16 * n + 4 * g + h for g in range(NREG)])
            if n == 0:
                value = value + column([4 * h + g for g in range(NREG)])
            out = out - jnp.where(lane == at + 3 * h + component, value, 0.0)
        return out

    quarter, coupling = column(range(80, 84)), column(range(84, 88))
    rows_ref[0] = block(1, 12)
    rows_ref[1] = (
        block(0, 12)
        + block(3, 0)
        + block(4, 24)
        + jnp.where(lane == 12 + row, quarter + coupling, 0.0)
        + jnp.where((lane >= 12 + first) & (lane < 15 + first), quarter, 0.0)
    )
    rows_ref[2] = block(2, 12)


def moment_kernel(
    near_ref, k_ref, label_ref, inv_ref, f_ref, own_ref, z_ref, w_ref, out_ref, g_ref, acc_ref, map_ref
):
    spread_maps(near_ref[...], map_ref)

    def first_step(s):
        def body(x, carry):
            label = label_ref[x]
            for c in range(3):
                z_ref[c, x] = f_ref[c, x] + spread(label, map_ref, s, c)
            return carry

        return body

    lax.fori_loop(1, 3, first_step(0), 0)
    lax.fori_loop(3, 19, first_step(1), 0, unroll=16)
    lax.fori_loop(19, 21, first_step(2), 0)

    def second_step(x, carry):
        _, w = image_of(k_ref, x, z_ref, x)
        inv = inv_ref[x]
        for c in range(3):
            w_ref[c, x - 2] = w[c]
            g_ref[c, x - 2] = w[c] * inv
        return carry

    lax.fori_loop(2, 20, second_step, 0, unroll=18)

    def step(x, carry):
        fields, image = image_of(k_ref, x + 2, g_ref, x)
        own = [v[0:16] for v in image]
        wg, gg = carry[12], carry[13]
        for c in range(3):
            g = fields[c][0:16]
            wg = wg + w_ref[c, x, 0:16] * g
            gg = gg + own[c] * g
        return (*add_regions(carry[:12], label_ref[x + 2, 0:16], own), wg, gg)

    zero = jnp.zeros((16, 128), F32)
    carry = lax.fori_loop(1, 17, step, (zero,) * 14, unroll=16)
    for i in range(12):
        acc_ref[i] = carry[i]
    lane = lax.broadcasted_iota(jnp.int32, (1, 128), 1)
    row = in_lanes(totals(acc_ref), 0) + own_ref[...]
    out_ref[...] = jnp.where(lane == 24, total(carry[12]), jnp.where(lane == 25, total(carry[13]), row))


def group_kernel(recv_ref, out_ref):
    q = jnp.sum(recv_ref[:, 0:4, :], axis=0)
    own = recv_ref[:, 4, :]
    lane = lax.broadcasted_iota(jnp.int32, (16, 128), 1)
    shifted_rows = []
    for s in range(4):
        shifted_rows.append(
            jnp.concatenate([pltpu.roll(q[s : s + 1], (128 - 12 * y) % 128, axis=1) for y in range(8)], axis=0)
        )
    mine, below, above = (
        jnp.concatenate([shifted_rows[s], shifted_rows[s + 1]], axis=0) for s in (1, 0, 2)
    )

    def right(v, by):
        return pltpu.roll(v, by % 128, axis=1)

    def first(v):
        return jnp.where(lane < 12, v, 0.0)

    def four(v):
        v = first(v)
        v = v + right(v, 12)
        return v + right(v, 24)

    alone = first(mine)
    twice = alone + right(alone, 12)
    turned = alone
    for d in range(1, 4):
        turned = turned + right(first(right(twice, -3 * d)), 12 * d)
    turned = turned + right(turned, 48)
    three = mine + right(mine, -1) + right(mine, -2)
    products = (
        recv_ref[:, 5, :] * (turned * (four(mine) + right(four(below), 48)) + right(first(three * three), 96))
        + recv_ref[:, 6, :] * turned * (four(above) + right(four(right(mine, 12)), 48))
        + recv_ref[:, 7, :] * turned * four(right(mine, -12))
        + 2.0 * jnp.where(lane < 12, own * alone, 0.0)
        + jnp.where(lane == 25, own, 0.0)
    )
    pairing = jnp.where((lane >= 12) & (lane < 24), own * twice, jnp.where(lane == 24, own, 0.0))
    at = lax.broadcasted_iota(jnp.int32, (1, 128), 1)
    row = jnp.where(at == 0, total(pairing), jnp.where(at == 1, total(products), 0.0))
    for n in range(NROWS):
        out_ref[n] = row


def third_kernel(recv_ref, k_ref, label_ref, inv_ref, z_ref, w_ref, scal_ref, own_ref, image_ref, znew_ref, map_ref):
    q = jnp.sum(recv_ref[:, 0:4, :], axis=0)
    spread_maps(around(q), map_ref)
    scal_ref[...] = q[0:1]
    rz, zw = q[0:1, SLAB : SLAB + 1], q[0:1, SLAB + 1 : SLAB + 2]
    alpha = rz / zw

    def first_step(s):
        def body(x, carry):
            inv, label = inv_ref[x], label_ref[x]
            for c in range(3):
                y = w_ref[c, x - 2] * inv + spread(label, map_ref, s, c)
                znew_ref[c, x - 2] = z_ref[c, x] - alpha * y
            return carry

        return body

    first_step(0)(2, 0)
    lax.fori_loop(3, 19, first_step(1), 0, unroll=16)
    first_step(2)(19, 0)

    def second_step(x, carry):
        here = k_ref[x + 2]
        faces, diagonal = coefficients(k_ref[x + 1], here, k_ref[x + 3])
        fields = [znew_ref[c, x] for c in range(3)]
        image = operate(
            faces, diagonal, here, [znew_ref[c, x - 1] for c in range(3)], fields, [znew_ref[c, x + 1] for c in range(3)]
        )
        for c in range(3):
            own_ref[c, x - 1] = fields[c][0:16]
            image_ref[c, x - 1] = image[c][0:16]
        return carry

    lax.fori_loop(1, 17, second_step, 0, unroll=16)


def last_kernel(recv_ref, scal_ref, r_ref, z_ref, w_ref, znew_ref, image_ref, x_hbm, res_hbm, x_ref, res_ref, sems):
    sums = jnp.sum(recv_ref[...], axis=0)
    wy, yay = sums[:, 0:1], sums[:, 1:2]
    scal = scal_ref[...]
    rz, zw = scal[:, SLAB : SLAB + 1], scal[:, SLAB + 1 : SLAB + 2]
    alpha = rz / zw
    new = rz + alpha * (alpha * wy - 2.0 * zw)
    zaz = zw + alpha * (alpha * yay - 2.0 * wy)
    cross = zw - alpha * wy
    ratio = new / rz
    second = new / (zaz + ratio * (2.0 * cross + ratio * zw))
    first = alpha + second * ratio

    copies = []
    for part in range(PARTS):
        planes = range(part * 16 // PARTS, (part + 1) * 16 // PARTS)
        for x in planes:
            for c in range(3):
                x_ref[c, x] = first * z_ref[c, x + 3, 0:16] + second * znew_ref[c, x]
                res_ref[c, x] = r_ref[c, x] - first * w_ref[c, x + 1, 0:16] - second * image_ref[c, x]
        own = pl.ds(planes[0], len(planes))
        for i, (ref, out) in enumerate(((x_ref, x_hbm), (res_ref, res_hbm))):
            copies.append(pltpu.make_async_copy(ref.at[:, own], out.at[:, own], sems.at[2 * part + i]))
            copies[-1].start()
    for copy in copies:
        copy.wait()


def exchange(array, axes):
    return lax.all_to_all(array, axes, 0, 0, tiled=True)


def swapped(array, axis, first):
    count = lax.axis_size(axis)
    pairs = [(i, i + 1) for i in range(first, count - 1, 2)]
    return lax.ppermute(array, axis, pairs + [(b, a) for a, b in pairs])


def local(right, occ, reg, coarse):
    field, plane = (16, 16, 128), (24, 128)
    send, r, label_own, coarse, rc, k_own, one, two = call(
        first_kernel,
        (
            shape(NROWS, 4, 128),
            shape(3, *field),
            shape(*field),
            shape(12, 6144),
            shape(12, 128),
            shape(*field),
            shape(3, 16, 4, 128),
            shape(3, 16, 4, 128),
        ),
        tuple(pltpu.with_memory_space_constraint(a, pltpu.HBM) for a in (right, reg, coarse, occ)),
        (
            pltpu.VMEM(field, jnp.int32),
            pltpu.VMEM(field, jnp.int32),
            pltpu.VMEM((12, 16, 128), F32),
            pltpu.SemaphoreType.DMA((4,)),
            *FOLD_SCRATCH,
        ),
        space=HBM,
        target=(HBM,) + (VMEM,) * 7,
    )
    one = swapped(one, "y", 0)
    two = swapped(two, "y", 1)
    got = exchange(send, ROWS)
    first, second = call(
        pack_kernel, (shape(PACK, 128), shape(PACK, 128)), (k_own, label_own, r, one, two), cost=1000000
    )
    first = lax.all_gather(first, "c")
    second = swapped(second, WIDE, 1)
    send = call(around_kernel, shape(NCOLS, 4, 128), (got,))
    got = exchange(send, COLS)
    k, label, inv, f = call(
        extend_kernel,
        (shape(22, *plane), shape(22, *plane), shape(22, *plane), shape(3, 22, *plane)),
        (r, k_own, label_own, one, two, first, second),
        cost=3000000,
    )
    start = call(start_kernel, shape(14, 128), (k, label, f, r), (pltpu.VMEM((14, 16, 128), F32),), cost=3000000)
    pair, rows = call(
        pair_kernel,
        (shape(3, 128), shape(3, 12, 128)),
        (k, label, jnp.asarray(selection())),
        (pltpu.VMEM((88, 8, 128), F32), pltpu.VMEM((88, 128), F32)),
        cost=3000000,
    )
    send, own, near = call(
        second_kernel,
        (shape(NROWS, 4, 128), shape(1, 128), shape(3, 128)),
        (got, rc, start, rows, coarse),
        FOLD_SCRATCH,
        target=(HBM, VMEM, VMEM),
    )
    got = exchange(send, ROWS)
    z, w, own = call(
        moment_kernel,
        (shape(3, 22, *plane), shape(3, 18, *plane), shape(1, 128)),
        (near, k, label, inv, f, own),
        (pltpu.VMEM((3, 18, *plane), F32), pltpu.VMEM((12, 16, 128), F32), pltpu.VMEM((3, 12, *plane), F32)),
        cost=3000000,
        alias={4: 0},
    )
    send = call(pass_kernel, shape(NCOLS, 8, 128), (got, own, pair))
    got = exchange(send, COLS)
    send = call(group_kernel, shape(NROWS, 1, 128), (got,))
    scal, znew, image = call(
        third_kernel,
        (shape(1, 128), shape(3, *field), shape(3, *field)),
        (got, k, label, inv, z, w),
        (pltpu.VMEM((3, 18, *plane), F32), pltpu.VMEM((3, 12, *plane), F32)),
        cost=3000000,
    )
    got = exchange(send, ROWS)
    return call(
        last_kernel,
        (shape(3, *field), shape(3, *field)),
        (got, scal, right, z, w, znew, image),
        (pltpu.VMEM((3, *field), F32), pltpu.VMEM((3, *field), F32), pltpu.SemaphoreType.DMA((2 * PARTS,))),
        target=HBM,
    )


def solution(mesh):
    finer = Mesh(mesh.devices.reshape(4, 8, 2, 8), ("x", "z", "c", "y"))
    field = P(None, WIDE, "y", None)
    labels = P(WIDE, "y", None)
    return jax.shard_map(
        local,
        mesh=finer,
        in_specs=(field, labels, labels, P((*WIDE, "y"), None)),
        out_specs=(field, field),
        check_vma=False,
    )
```

```python
import jax
import jax.numpy as jnp
import numpy as np
from jax import lax
from jax.experimental import pallas as pl
from jax.experimental.pallas import tpu as pltpu
from jax.sharding import Mesh
from jax.sharding import PartitionSpec as P

WIDE = ("x", "z", "c")
ROWS = ("z", "x")
COLS = ("c", "y")
NROWS = 32
NCOLS = 16
F32 = jnp.float32
NREG = 4
SLAB = 96
VMEM = pl.BlockSpec(memory_space=pltpu.VMEM)
HBM = pl.BlockSpec(memory_space=pltpu.HBM)
PARTS = 4
CHUNK = 8


def shape(*dims):
    return jax.ShapeDtypeStruct(dims, F32)


def call(kernel, outs, ins, scratch=(), space=VMEM, target=VMEM, cost=0, limit=24, alias=None):
    return pl.pallas_call(
        kernel,
        out_shape=outs,
        in_specs=[space] * len(ins),
        out_specs=target if isinstance(target, tuple) else jax.tree.map(lambda _: target, outs),
        scratch_shapes=list(scratch),
        input_output_aliases=alias or {},
        cost_estimate=pl.CostEstimate(flops=cost, bytes_accessed=cost, transcendentals=0) if cost else None,
        compiler_params=pltpu.CompilerParams(vmem_limit_bytes=int(limit * 1024 * 1024)),
    )(*ins)


def total(v):
    return jnp.sum(jnp.sum(v, axis=0, keepdims=True), axis=1, keepdims=True)


def add_regions(accs, label, field):
    out = list(accs)
    for g in range(NREG):
        mask = label == g + 1
        for c in range(3):
            out[3 * g + c] = out[3 * g + c] + jnp.where(mask, field[c], 0.0)
    return out


def totals(acc_ref):
    return jnp.sum(jnp.sum(acc_ref[...], axis=1), axis=1, keepdims=True)


def in_lanes(column, at):
    row = lax.broadcasted_iota(jnp.int32, (12, 128), 0)
    lane = lax.broadcasted_iota(jnp.int32, (12, 128), 1)
    return jnp.sum(jnp.where(lane == row + at, column, 0.0), axis=0, keepdims=True)


def in_rows(lanes, at):
    row = lax.broadcasted_iota(jnp.int32, (12, 128), 0)
    lane = lax.broadcasted_iota(jnp.int32, (12, 128), 1)
    return jnp.sum(jnp.where(lane == row + at, lanes, 0.0), axis=1, keepdims=True)


def fold(rc, coarse_ref, u_ref, pad_ref, send_ref, sems, out_ref, sums=()):
    u_ref[...] = jnp.sum(coarse_ref[...] * rc, axis=0, keepdims=True)
    pad_ref[...] = jnp.zeros_like(pad_ref)
    for w in range(2 * NROWS):
        pad_ref[w + 1 : w + 2, 0:SLAB] = u_ref[0:1, SLAB * w : SLAB * (w + 1)]
    if sums:
        lane = lax.broadcasted_iota(jnp.int32, (1, 128), 1)
        row = jnp.zeros((1, 128), F32)
        for i, s in enumerate(sums):
            row = jnp.where(lane == SLAB + i, s, row)
        tail = jnp.broadcast_to(row, (4, 128))
    copies = []
    for n in range(NROWS):
        at = 2 * (n % 4 * 8 + n // 4)
        window = pad_ref[at : at + 4, :]
        if sums:
            window = window + tail
        send_ref[n] = window
        if n % CHUNK == CHUNK - 1:
            part = pl.ds(n + 1 - CHUNK, CHUNK)
            copies.append(pltpu.make_async_copy(send_ref.at[part], out_ref.at[part], sems.at[n // CHUNK]))
            copies[-1].start()
    return copies


FOLD_SCRATCH = (
    pltpu.VMEM((1, 6144), F32),
    pltpu.VMEM((72, 128), F32),
    pltpu.VMEM((NROWS, 4, 128), F32),
    pltpu.SemaphoreType.DMA((NROWS // 8,)),
)


def even_column():
    return lax.rem(lax.axis_index("y"), 2) == 0


def first_kernel(
    r_hbm, reg_hbm, coarse_hbm, occ_hbm,
    out_hbm, r_ref, label_ref, coarse_ref, rc_ref, k_ref, a_ref, b_ref,
    reg_ref, occ_ref, acc_ref, sems, u_ref, pad_ref, send_ref, send_sems,
):
    pairs = ((r_hbm, r_ref), (reg_hbm, reg_ref), (coarse_hbm, coarse_ref), (occ_hbm, occ_ref))
    copies = [pltpu.make_async_copy(a, b, sems.at[i]) for i, (a, b) in enumerate(pairs)]
    for copy in copies:
        copy.start()
    for copy in copies[:2]:
        copy.wait()

    def step(x, accs):
        label = reg_ref[x].astype(F32) + 1.0
        label_ref[x] = label
        return tuple(add_regions(accs, label, [r_ref[c, x] for c in range(3)]))

    zero = jnp.zeros((16, 128), F32)
    accs = lax.fori_loop(0, 16, step, (zero,) * 12, unroll=16)
    for i in range(12):
        acc_ref[i] = accs[i]
    rc = totals(acc_ref)
    rc_ref[...] = jnp.broadcast_to(rc, (12, 128))
    copies[2].wait()
    sends = fold(rc, coarse_ref, u_ref, pad_ref, send_ref, send_sems, out_hbm)
    copies[3].wait()
    k_ref[...] = 0.1 + 0.9 * occ_ref[...].astype(F32)
    even = even_column()
    for ref, last in ((a_ref, even), (b_ref, jnp.logical_not(even))):
        ref[0] = jnp.where(last, k_ref[:, 12:16, :], k_ref[:, 0:4, :])
        for i, field in enumerate([label_ref] + [r_ref.at[c] for c in range(3)]):
            at = 2 * (i % 2)
            ref[1 + i // 2, :, at : at + 2] = jnp.where(last, field[:, 14:16, :], field[:, 0:2, :])
    for copy in sends:
        copy.wait()


def tail_rows(a_ref, b_ref, i, planes):
    even = even_column()
    if i == 0:
        one, two = a_ref[0, planes], b_ref[0, planes]
        return jnp.concatenate([jnp.where(even, one, two), jnp.where(even, two, one)], axis=1)
    block, at = 1 + (i - 1) // 2, 2 * ((i - 1) % 2)
    one, two = a_ref[block, planes, at : at + 2], b_ref[block, planes, at : at + 2]
    none = jnp.zeros((one.shape[0], 4, 128), F32)
    return jnp.concatenate([jnp.where(even, one, two), none, jnp.where(even, two, one)], axis=1)


PACK = 72 + 4 * 40


def pack_kernel(k_ref, label_ref, r_ref, a_ref, b_ref, first_ref, second_ref):
    fields = [label_ref] + [r_ref.at[c] for c in range(3)]
    core = lax.axis_index("c")
    for ref, up in ((first_ref, core == 0), (second_ref, core == 1)):
        deep, near, next_ = jnp.where(up, 13, 0), jnp.where(up, 15, 0), jnp.where(up, 14, 1)
        tails = tail_rows(a_ref, b_ref, 0, pl.ds(deep, 3))
        for i in range(3):
            ref[24 * i : 24 * i + 16] = k_ref[deep + i]
            ref[24 * i + 16 : 24 * i + 24] = tails[i]
        for i, field in enumerate(fields):
            at = 72 + 40 * i
            ref[at : at + 16] = field[near]
            ref[at + 16 : at + 24] = tail_rows(a_ref, b_ref, 1 + i, pl.ds(near, 1))[0]
            ref[at + 24 : at + 40] = field[next_]


def extend_kernel(
    r_ref, k_own_ref, label_own_ref, a_ref, b_ref, first_ref, second_ref, k_ref, label_ref, inv_ref, f_ref
):
    whole = pl.ds(0, 16)
    core = lax.axis_index("c")

    def sides(rows):
        one, two = first_ref[rows], second_ref[rows]
        return jnp.where(core == 0, two, one), jnp.where(core == 0, one, two)

    k_ref[3:19, 0:16] = k_own_ref[...]
    label_ref[3:19, 0:16] = label_own_ref[...]
    k_ref[3:19, 16:24] = tail_rows(a_ref, b_ref, 0, whole)
    label_ref[3:19, 16:24] = tail_rows(a_ref, b_ref, 1, whole)
    none = jnp.zeros((8, 128), F32)
    for i in range(3):
        below, above = sides(slice(24 * i, 24 * i + 24))
        k_ref[i] = below
        k_ref[19 + i] = above
    targets = [label_ref] + [f_ref.at[c] for c in range(3)]
    for i, ref in enumerate(targets):
        at = 72 + 40 * i
        ref[2], ref[19] = sides(slice(at, at + 24))
        ref[1, 0:16], ref[20, 0:16] = sides(slice(at + 24, at + 40))
        ref[1, 16:24] = ref[20, 16:24] = none
    for c in range(3):
        f_ref[c, 3:19, 0:16] = r_ref[c]
        f_ref[c, 3:19, 16:24] = tail_rows(a_ref, b_ref, 2 + c, whole)

    def step(x, carry):
        here = k_ref[x]
        _, diagonal = coefficients(k_ref[x - 1], here, k_ref[x + 1])
        inside = here > 0.0
        inv = jnp.where(inside, 1.0 / jnp.where(inside, diagonal, 1.0), 0.0)
        inv_ref[x] = inv
        for c in range(3):
            f_ref[c, x] = f_ref[c, x] * inv
        return carry

    lax.fori_loop(1, 21, step, 0, unroll=20)


def around_kernel(recv_ref, out_ref):
    part = jnp.sum(recv_ref[...], axis=0)
    for n in range(NCOLS):
        out_ref[n] = part


def pass_kernel(recv_ref, own_ref, pair_ref, out_ref):
    part = jnp.sum(recv_ref[...], axis=0)
    rows = jnp.concatenate([part, own_ref[...], pair_ref[...]], axis=0)
    for n in range(NCOLS):
        out_ref[n] = rows


def around(q):
    near = jnp.where(lax.axis_index("c") == 0, q[0:3], q[1:4])
    return pltpu.roll(near, lax.rem(140 - 12 * lax.axis_index("y"), 128), axis=1)


def iotas():
    lane = lax.broadcasted_iota(jnp.int32, (24, 128), 1)
    return lane == 0, lane == 127


def coefficients(before, here, after):
    first, last = iotas()
    y_up = pltpu.roll(here, 23, axis=0)
    y_down = pltpu.roll(here, 1, axis=0)
    z_up = jnp.where(last, 0.0, pltpu.roll(here, 127, axis=1))
    z_down = jnp.where(first, 0.0, pltpu.roll(here, 1, axis=1))
    half = 0.5 * here
    faces = [half + 0.5 * other for other in (after, before, y_up, y_down, z_up, z_down)]
    diagonal = faces[0] + faces[1] + faces[2] + faces[3] + faces[4] + faces[5] + half
    faces[4] = jnp.where(last, 0.0, faces[4])
    faces[5] = jnp.where(first, 0.0, faces[5])
    return faces, diagonal


def operate(faces, diagonal, here, befores, fields, afters):
    quarter = 0.25 * here
    main = diagonal - quarter
    shared = quarter * (fields[0] + fields[1] + fields[2])
    out = []
    for c in range(3):
        u = fields[c]
        out.append(
            main * u
            + shared
            - faces[0] * afters[c]
            - faces[1] * befores[c]
            - faces[2] * pltpu.roll(u, 23, axis=0)
            - faces[3] * pltpu.roll(u, 1, axis=0)
            - faces[4] * pltpu.roll(u, 127, axis=1)
            - faces[5] * pltpu.roll(u, 1, axis=1)
        )
    return out


def spread_maps(q, map_ref):
    row = lax.broadcasted_iota(jnp.int32, (24, 128), 0)
    for s in range(3):
        for i in range(12):
            below, own, above = (q[s : s + 1, 12 * d + i : 12 * d + i + 1] for d in range(3))
            map_ref[s, i] = jnp.where(row < 16, own, jnp.where(row < 20, above, below))


def spread(label, map_ref, s, c):
    out = jnp.zeros((24, 128), F32)
    for g in range(NREG):
        out = jnp.where(label == g + 1, map_ref[s, 3 * g + c], out)
    return out


def image_of(k_ref, x, field_ref, at):
    here = k_ref[x]
    faces, diagonal = coefficients(k_ref[x - 1], here, k_ref[x + 1])
    planes = [[field_ref[c, i] for c in range(3)] for i in (at - 1, at, at + 1)]
    return planes[1], operate(faces, diagonal, here, *planes)


def start_kernel(k_ref, label_ref, f_ref, r_ref, out_ref, acc_ref):
    def step(x, carry):
        fields, image = image_of(k_ref, x, f_ref, x)
        own = [v[0:16] for v in image]
        rf, faf = carry[12], carry[13]
        for c in range(3):
            f = fields[c][0:16]
            rf = rf + r_ref[c, x - 3] * f
            faf = faf + f * own[c]
        return (*add_regions(carry[:12], label_ref[x, 0:16], own), rf, faf)

    zero = jnp.zeros((16, 128), F32)
    carry = lax.fori_loop(3, 19, step, (zero,) * 14, unroll=16)
    for i in range(14):
        acc_ref[i] = carry[i]
    out_ref[...] = jnp.broadcast_to(totals(acc_ref), (14, 128))


def second_kernel(
    recv_ref, rc_ref, start_ref, rows_ref, coarse_ref,
    out_hbm, own_ref, near_ref, u_ref, pad_ref, send_ref, send_sems,
):
    near = around(jnp.sum(recv_ref[...], axis=0))
    near_ref[...] = near
    product = rows_ref[0] * near[0:1] + rows_ref[1] * near[1:2] + rows_ref[2] * near[2:3]
    e = start_ref[0:12, 0:1]
    aggregates = e + jnp.sum(product, axis=1, keepdims=True)
    q = in_rows(near[1:2], 12)
    rz = start_ref[12:13, 0:1] + jnp.sum(rc_ref[:, 0:1] * q, axis=0, keepdims=True)
    zw = start_ref[13:14, 0:1] + jnp.sum(q * (e + aggregates), axis=0, keepdims=True)
    sends = fold(aggregates, coarse_ref, u_ref, pad_ref, send_ref, send_sems, out_hbm, (rz, zw))
    own_ref[...] = in_lanes(aggregates, 12)
    for copy in sends:
        copy.wait()


def selection():
    out = np.zeros((88, 3 * 128), np.float32)
    for n in range(5):
        for d in range(4):
            for h in range(4):
                g = (h + d) % 4
                for c in range(3):
                    lane = 128 * (n // 2) + 48 * (n % 2) + 12 * d + 3 * h + c
                    out[16 * n + 4 * g + h, lane] -= 1.0
                    if n == 0:
                        out[4 * h + g, lane] -= 1.0
                        if d == 0:
                            out[80 + g, lane] += 1.0
                            out[84 + g, lane] += 1.0
    for g in range(4):
        out[80 + g, 96 + 3 * g] = 1.0
    return out


def tiles(v):
    return v[0:8] + v[8:16]


def pair_kernel(k_ref, label_ref, select_ref, out_ref, rows_ref, acc_ref, sum_ref):
    row = lax.broadcasted_iota(jnp.int32, (24, 128), 0)
    lane = lax.broadcasted_iota(jnp.int32, (24, 128), 1)

    def plane(x, accs, inner):
        here, label = k_ref[x], label_ref[x]
        faces, diagonal = coefficients(k_ref[x - 1], here, k_ref[x + 1])
        y_label = jnp.where(row == 15, 0.0, pltpu.roll(label, 23, axis=0))[0:16]
        z_label = jnp.where(lane == 127, 0.0, pltpu.roll(label, 127, axis=1))[0:16]
        own = label[0:16]
        quarter, coupling = 0.25 * here[0:16], (diagonal - 0.5 * here)[0:16]
        masks = [own == g + 1 for g in range(NREG)]
        out = list(accs)
        for h in range(NREG):
            v = jnp.where(y_label == h + 1, faces[2][0:16], 0.0) + jnp.where(z_label == h + 1, faces[4][0:16], 0.0)
            if inner:
                v = v + jnp.where(label_ref[x + 1, 0:16] == h + 1, faces[0][0:16], 0.0)
            for g in range(NREG):
                out[4 * g + h] = out[4 * g + h] + tiles(jnp.where(masks[g], v, 0.0))
        for g in range(NREG):
            out[16 + g] = out[16 + g] + tiles(jnp.where(masks[g], quarter, 0.0))
            out[20 + g] = out[20 + g] + tiles(jnp.where(masks[g], coupling, 0.0))
        return tuple(out)

    zero = jnp.zeros((8, 128), F32)
    accs = lax.fori_loop(3, 18, lambda x, a: plane(x, a, True), (zero,) * 24, unroll=15)
    accs = plane(18, accs, False)
    for i in range(16):
        acc_ref[i] = accs[i]
    for i in range(8):
        acc_ref[80 + i] = accs[16 + i]
    own = pl.ds(3, 16)
    sides = (
        (k_ref[3, 0:16], label_ref[3, 0:16], k_ref[2, 0:16], label_ref[2, 0:16]),
        (k_ref[18, 0:16], label_ref[18, 0:16], k_ref[19, 0:16], label_ref[19, 0:16]),
        (k_ref[own, 0, :], label_ref[own, 0, :], k_ref[own, 23, :], label_ref[own, 23, :]),
        (k_ref[own, 15, :], label_ref[own, 15, :], k_ref[own, 16, :], label_ref[own, 16, :]),
    )
    for n, (k, label, other, other_label) in enumerate(sides):
        face = 0.5 * k + 0.5 * other
        for g in range(NREG):
            part = jnp.where(label == g + 1, face, 0.0)
            for h in range(NREG):
                acc_ref[16 * n + 16 + 4 * g + h] = tiles(jnp.where(other_label == h + 1, part, 0.0))
    sums = jnp.sum(jnp.sum(acc_ref[...], axis=1), axis=1, keepdims=True)
    for i in range(3):
        out_ref[i : i + 1] = jnp.sum(select_ref[:, 128 * i : 128 * i + 128] * sums, axis=0, keepdims=True)
    sum_ref[...] = jnp.broadcast_to(sums, (88, 128))
    row = lax.broadcasted_iota(jnp.int32, (12, 128), 0)
    lane = lax.broadcasted_iota(jnp.int32, (12, 128), 1)
    first = 3 * ((row >= 3).astype(jnp.int32) + (row >= 6).astype(jnp.int32) + (row >= 9).astype(jnp.int32))
    component = row - first

    def column(indices):
        return jnp.concatenate([jnp.broadcast_to(sum_ref[i : i + 1], (3, 128)) for i in indices], axis=0)

    def block(n, at):
        out = jnp.zeros((12, 128), F32)
        for h in range(NREG):
            value = column([16 * n + 4 * g + h for g in range(NREG)])
            if n == 0:
                value = value + column([4 * h + g for g in range(NREG)])
            out = out - jnp.where(lane == at + 3 * h + component, value, 0.0)
        return out

    quarter, coupling = column(range(80, 84)), column(range(84, 88))
    rows_ref[0] = block(1, 12)
    rows_ref[1] = (
        block(0, 12)
        + block(3, 0)
        + block(4, 24)
        + jnp.where(lane == 12 + row, quarter + coupling, 0.0)
        + jnp.where((lane >= 12 + first) & (lane < 15 + first), quarter, 0.0)
    )
    rows_ref[2] = block(2, 12)


def moment_kernel(
    near_ref, k_ref, label_ref, inv_ref, f_ref, own_ref, z_ref, w_ref, out_ref, g_ref, acc_ref, map_ref
):
    spread_maps(near_ref[...], map_ref)

    def first_step(s):
        def body(x, carry):
            label = label_ref[x]
            for c in range(3):
                z_ref[c, x] = f_ref[c, x] + spread(label, map_ref, s, c)
            return carry

        return body

    lax.fori_loop(1, 3, first_step(0), 0)
    lax.fori_loop(3, 19, first_step(1), 0, unroll=16)
    lax.fori_loop(19, 21, first_step(2), 0)

    def second_step(x, carry):
        _, w = image_of(k_ref, x, z_ref, x)
        inv = inv_ref[x]
        for c in range(3):
            w_ref[c, x - 2] = w[c]
            g_ref[c, x - 2] = w[c] * inv
        return carry

    lax.fori_loop(2, 20, second_step, 0, unroll=18)

    def step(x, carry):
        fields, image = image_of(k_ref, x + 2, g_ref, x)
        own = [v[0:16] for v in image]
        wg, gg = carry[12], carry[13]
        for c in range(3):
            g = fields[c][0:16]
            wg = wg + w_ref[c, x, 0:16] * g
            gg = gg + own[c] * g
        return (*add_regions(carry[:12], label_ref[x + 2, 0:16], own), wg, gg)

    zero = jnp.zeros((16, 128), F32)
    carry = lax.fori_loop(1, 17, step, (zero,) * 14, unroll=16)
    for i in range(12):
        acc_ref[i] = carry[i]
    lane = lax.broadcasted_iota(jnp.int32, (1, 128), 1)
    row = in_lanes(totals(acc_ref), 0) + own_ref[...]
    out_ref[...] = jnp.where(lane == 24, total(carry[12]), jnp.where(lane == 25, total(carry[13]), row))


def group_kernel(recv_ref, out_ref):
    q = jnp.sum(recv_ref[:, 0:4, :], axis=0)
    own = recv_ref[:, 4, :]
    lane = lax.broadcasted_iota(jnp.int32, (16, 128), 1)
    shifted_rows = []
    for s in range(4):
        shifted_rows.append(
            jnp.concatenate([pltpu.roll(q[s : s + 1], (128 - 12 * y) % 128, axis=1) for y in range(8)], axis=0)
        )
    mine, below, above = (
        jnp.concatenate([shifted_rows[s], shifted_rows[s + 1]], axis=0) for s in (1, 0, 2)
    )

    def right(v, by):
        return pltpu.roll(v, by % 128, axis=1)

    def first(v):
        return jnp.where(lane < 12, v, 0.0)

    def four(v):
        v = first(v)
        v = v + right(v, 12)
        return v + right(v, 24)

    alone = first(mine)
    twice = alone + right(alone, 12)
    turned = alone
    for d in range(1, 4):
        turned = turned + right(first(right(twice, -3 * d)), 12 * d)
    turned = turned + right(turned, 48)
    three = mine + right(mine, -1) + right(mine, -2)
    products = (
        recv_ref[:, 5, :] * (turned * (four(mine) + right(four(below), 48)) + right(first(three * three), 96))
        + recv_ref[:, 6, :] * turned * (four(above) + right(four(right(mine, 12)), 48))
        + recv_ref[:, 7, :] * turned * four(right(mine, -12))
        + 2.0 * jnp.where(lane < 12, own * alone, 0.0)
        + jnp.where(lane == 25, own, 0.0)
    )
    pairing = jnp.where((lane >= 12) & (lane < 24), own * twice, jnp.where(lane == 24, own, 0.0))
    at = lax.broadcasted_iota(jnp.int32, (1, 128), 1)
    row = jnp.where(at == 0, total(pairing), jnp.where(at == 1, total(products), 0.0))
    for n in range(NROWS):
        out_ref[n] = row


def third_kernel(recv_ref, k_ref, label_ref, inv_ref, z_ref, w_ref, scal_ref, own_ref, image_ref, znew_ref, map_ref):
    q = jnp.sum(recv_ref[:, 0:4, :], axis=0)
    spread_maps(around(q), map_ref)
    scal_ref[...] = q[0:1]
    rz, zw = q[0:1, SLAB : SLAB + 1], q[0:1, SLAB + 1 : SLAB + 2]
    alpha = rz / zw

    def first_step(s):
        def body(x, carry):
            inv, label = inv_ref[x], label_ref[x]
            for c in range(3):
                y = w_ref[c, x - 2] * inv + spread(label, map_ref, s, c)
                znew_ref[c, x - 2] = z_ref[c, x] - alpha * y
            return carry

        return body

    first_step(0)(2, 0)
    lax.fori_loop(3, 19, first_step(1), 0, unroll=16)
    first_step(2)(19, 0)

    def second_step(x, carry):
        here = k_ref[x + 2]
        faces, diagonal = coefficients(k_ref[x + 1], here, k_ref[x + 3])
        fields = [znew_ref[c, x] for c in range(3)]
        image = operate(
            faces, diagonal, here, [znew_ref[c, x - 1] for c in range(3)], fields, [znew_ref[c, x + 1] for c in range(3)]
        )
        for c in range(3):
            own_ref[c, x - 1] = fields[c][0:16]
            image_ref[c, x - 1] = image[c][0:16]
        return carry

    lax.fori_loop(1, 17, second_step, 0, unroll=16)


def last_kernel(recv_ref, scal_ref, r_ref, z_ref, w_ref, znew_ref, image_ref, x_hbm, res_hbm, x_ref, res_ref, sems):
    sums = jnp.sum(recv_ref[...], axis=0)
    wy, yay = sums[:, 0:1], sums[:, 1:2]
    scal = scal_ref[...]
    rz, zw = scal[:, SLAB : SLAB + 1], scal[:, SLAB + 1 : SLAB + 2]
    alpha = rz / zw
    new = rz + alpha * (alpha * wy - 2.0 * zw)
    zaz = zw + alpha * (alpha * yay - 2.0 * wy)
    cross = zw - alpha * wy
    ratio = new / rz
    second = new / (zaz + ratio * (2.0 * cross + ratio * zw))
    first = alpha + second * ratio

    copies = []
    for part in range(PARTS):
        planes = range(part * 16 // PARTS, (part + 1) * 16 // PARTS)
        for x in planes:
            for c in range(3):
                x_ref[c, x] = first * z_ref[c, x + 3, 0:16] + second * znew_ref[c, x]
                res_ref[c, x] = r_ref[c, x] - first * w_ref[c, x + 1, 0:16] - second * image_ref[c, x]
        own = pl.ds(planes[0], len(planes))
        for i, (ref, out) in enumerate(((x_ref, x_hbm), (res_ref, res_hbm))):
            copies.append(pltpu.make_async_copy(ref.at[:, own], out.at[:, own], sems.at[2 * part + i]))
            copies[-1].start()
    for copy in copies:
        copy.wait()


def exchange(array, axes):
    return lax.all_to_all(array, axes, 0, 0, tiled=True)


def swapped(array, axis, first):
    count = lax.axis_size(axis)
    pairs = [(i, i + 1) for i in range(first, count - 1, 2)]
    return lax.ppermute(array, axis, pairs + [(b, a) for a, b in pairs])


def local(right, occ, reg, coarse):
    field, plane = (16, 16, 128), (24, 128)
    send, r, label_own, coarse, rc, k_own, one, two = call(
        first_kernel,
        (
            shape(NROWS, 4, 128),
            shape(3, *field),
            shape(*field),
            shape(12, 6144),
            shape(12, 128),
            shape(*field),
            shape(3, 16, 4, 128),
            shape(3, 16, 4, 128),
        ),
        tuple(pltpu.with_memory_space_constraint(a, pltpu.HBM) for a in (right, reg, coarse, occ)),
        (
            pltpu.VMEM(field, jnp.int32),
            pltpu.VMEM(field, jnp.int32),
            pltpu.VMEM((12, 16, 128), F32),
            pltpu.SemaphoreType.DMA((4,)),
            *FOLD_SCRATCH,
        ),
        space=HBM,
        target=(HBM,) + (VMEM,) * 7,
    )
    one = swapped(one, "y", 0)
    two = swapped(two, "y", 1)
    got = exchange(send, ROWS)
    first, second = call(
        pack_kernel, (shape(PACK, 128), shape(PACK, 128)), (k_own, label_own, r, one, two), cost=1000000
    )
    first = swapped(first, WIDE, 0)
    second = swapped(second, WIDE, 1)
    send = call(around_kernel, shape(NCOLS, 4, 128), (got,))
    got = exchange(send, COLS)
    k, label, inv, f = call(
        extend_kernel,
        (shape(22, *plane), shape(22, *plane), shape(22, *plane), shape(3, 22, *plane)),
        (r, k_own, label_own, one, two, first, second),
        cost=3000000,
    )
    start = call(start_kernel, shape(14, 128), (k, label, f, r), (pltpu.VMEM((14, 16, 128), F32),), cost=3000000)
    pair, rows = call(
        pair_kernel,
        (shape(3, 128), shape(3, 12, 128)),
        (k, label, jnp.asarray(selection())),
        (pltpu.VMEM((88, 8, 128), F32), pltpu.VMEM((88, 128), F32)),
        cost=3000000,
    )
    send, own, near = call(
        second_kernel,
        (shape(NROWS, 4, 128), shape(1, 128), shape(3, 128)),
        (got, rc, start, rows, coarse),
        FOLD_SCRATCH,
        target=(HBM, VMEM, VMEM),
    )
    got = exchange(send, ROWS)
    z, w, own = call(
        moment_kernel,
        (shape(3, 22, *plane), shape(3, 18, *plane), shape(1, 128)),
        (near, k, label, inv, f, own),
        (pltpu.VMEM((3, 18, *plane), F32), pltpu.VMEM((12, 16, 128), F32), pltpu.VMEM((3, 12, *plane), F32)),
        cost=3000000,
        alias={4: 0},
    )
    send = call(pass_kernel, shape(NCOLS, 8, 128), (got, own, pair))
    got = exchange(send, COLS)
    send = call(group_kernel, shape(NROWS, 1, 128), (got,))
    scal, znew, image = call(
        third_kernel,
        (shape(1, 128), shape(3, *field), shape(3, *field)),
        (got, k, label, inv, z, w),
        (pltpu.VMEM((3, 18, *plane), F32), pltpu.VMEM((3, 12, *plane), F32)),
        cost=3000000,
    )
    got = exchange(send, ROWS)
    return call(
        last_kernel,
        (shape(3, *field), shape(3, *field)),
        (got, scal, right, z, w, znew, image),
        (pltpu.VMEM((3, *field), F32), pltpu.VMEM((3, *field), F32), pltpu.SemaphoreType.DMA((2 * PARTS,))),
        target=HBM,
    )


def solution(mesh):
    finer = Mesh(mesh.devices.reshape(4, 8, 2, 8), ("x", "z", "c", "y"))
    field = P(None, WIDE, "y", None)
    labels = P(WIDE, "y", None)
    return jax.shard_map(
        local,
        mesh=finer,
        in_specs=(field, labels, labels, P((*WIDE, "y"), None)),
        out_specs=(field, field),
        check_vma=False,
    )
```
